256 devices in a mesh: dom: 64 (over y, z, core), feat: 4 (over x).
Axes of the slice: x: 4, y: 4, z: 8, core: 2. Of those that a mesh axis runs over, the one named last changes fastest.
Arguments:
- features: bfloat16 [16384, 512], P('dom', 'feat'), may hold values from -6 to 6
- hub_feats: bfloat16 [2048, 256], P('dom'), may hold values from -6 to 6
- nbr_owner: int32 [8, 32768, 1], P(None, 'dom'), may hold values from 0 to 63; in each aligned block of 512 rows (0 to 511, 512 to 1023, ..., all dimensions but the last counted through in order) at most 16 rows name the same one
- nbr_row: int32 [8, 32768], P(None, 'dom'), may hold values from 0 to 511
- hub_ids: int32 [32768, 4], P('dom'), may hold values from 0 to 2047
- w_self: bfloat16 [256, 256], replicated, may hold values from -0.375 to 0.375
- w_nbr: bfloat16 [256, 256], replicated, may hold values from -0.375 to 0.375
- grad_out: bfloat16 [16384, 512], P('dom', 'feat'), may hold values from -6 to 6
Outputs:
- outputs: bfloat16 [16384, 512], P('dom', 'feat')
- grad_features: bfloat16 [16384, 512], P('dom', 'feat')
- grad_hubs: float32 [2048, 256], P('dom', 'feat')
- grad_self: float32 [256, 256], P('feat')
- grad_nbr: float32 [256, 256], P('feat')
The draws below stay inside these ranges and needn't reach their ends.
Inputs may be any that keep to these rules, and one draw needn't show every extreme that they name: `nbr_owner`: for each sample index k, among the 512 targets of one partition at most 16 have their k-th neighbour on one owner; that many is reached.
All inputs are finite; a program needn't handle non-finite values.
Results may differ from the reference program's by a relative error of at most 0.0054.
Values may be sent and summed in bfloat16 or wider, within the bound.
No kernel may reach another device: no remote copies, remote signals or barrier semaphores. Data moves between devices by JAX's collectives and lax.ppermute only.
A program may use at most 64 MiB of HBM per device.

```python
import math
import jax
import jax.numpy as jnp
import numpy as np

H = 256
K = 8
KH = 4
V_DEV = 512
VERTS = 32768
HUBS = 2048
CAPK = 16
N_DOM = 64


def plant(array, own_key, low, largest):
    longest = array.shape.index(max(array.shape))
    spots = []
    for shift in (0, 1):
        where = [jax.random.randint(jax.random.fold_in(own_key, axis), (), 0, length) for axis, length in enumerate(array.shape)]
        where[longest] = (where[longest] + shift) % array.shape[longest]
        spots.append(tuple(where))
    return array.at[spots[0]].set(low).at[spots[1]].set(largest)


def level_of(own_key, shape, pieces, low, high):
    gain, own = 1.0, jax.random.fold_in(own_key, 6)
    for axis_at, blocks in pieces:
        steps = jnp.exp(jax.random.uniform(jax.random.fold_in(own, axis_at), (blocks,), jnp.float32, low / len(pieces), high / len(pieces)))
        gain = gain * jnp.repeat(steps, shape[axis_at] // blocks).reshape([-1 if axis == axis_at else 1 for axis in range(len(shape))])
    return gain


def rank_table(amount, lean):
    weights = [(1 << 20) // math.isqrt(grade ** lean) + 1 for grade in range(1, amount + 1)]
    spread = 1 + sum(weights) // (1 << 30)
    return np.cumsum(np.array([max(1, weight // spread) for weight in weights]))


def ranked_ids(rng, dims, number_of, skew):
    listing = rank_table(number_of, skew)
    pick = jax.random.randint(jax.random.fold_in(rng, 1), dims, 0, int(listing[number_of - 1]))
    grade = jnp.searchsorted(jnp.asarray(listing, jnp.int32), pick, side="right")
    return jax.random.permutation(jax.random.fold_in(rng, 2), number_of)[grade].astype(jnp.int32)


def assign_block(key, own, number, rows, count, top, bound, skew):
    ranking = jax.random.permutation(key, count)
    heavy_load, usual = shares(count, rows * top, bound, skew, True), shares(count, rows * top, bound, skew, False)
    places = jnp.arange(count)

    def named(lengths, rotation):
        used = int((lengths > 0).sum())
        fixed = max(1, used // 4)
        shifted = fixed + (places - fixed + rotation * (used - fixed)) % max(1, count - fixed)
        return jnp.zeros((count,), jnp.int32).at[ranking[jnp.where(places < fixed, places, shifted)]].set(jnp.asarray(lengths, jnp.int32))

    lengths = jnp.where(number % 4 == 0, named(heavy_load, number // 4), named(usual, number - number // 4 - 1))
    mixed = jax.random.permutation(jax.random.fold_in(own, 3), count)
    source_of, taker = mixed[0:count // 2 * 2:2], mixed[1:count // 2 * 2:2]
    margin = jnp.minimum(lengths[source_of] - 1, bound - lengths[taker]) // 2
    margin = jnp.where((source_of == ranking[0]) | (taker == ranking[0]) | (lengths[taker] == 0), 0, jnp.maximum(margin, 0))
    shifted = jax.random.randint(jax.random.fold_in(own, 4), (count // 2,), 0, 1 << 20) % (margin + 1)
    lengths = lengths.at[source_of].add(-shifted).at[taker].add(shifted)
    items = jnp.searchsorted(jnp.cumsum(lengths), jnp.arange(rows * top), side="right").astype(jnp.int32)
    grid = items.reshape(top, rows).T
    grid = grid[jax.random.permutation(jax.random.fold_in(own, 1), rows)]
    rotation = jax.random.randint(jax.random.fold_in(own, 2), (rows, 1), 0, top)
    return jnp.take_along_axis(grid, (jnp.arange(top)[None, :] + rotation) % top, axis=1)


def shares(count, total, bound, skew, full):
    portions = [(1 << 20) // math.isqrt(standing ** skew) + 1 for standing in range(1, count + 1)]
    largest = bound if full else min(bound, max(-(-total // count), total * portions[0] // sum(portions)))
    least = 1 if total - largest >= count - 1 else 0
    given, spare = [largest] + [least] * (count - 1), total - largest - least * (count - 1)
    while spare > 0:
        free = [i for i in range(1, count) if given[i] < largest] or [i for i in range(1, count) if given[i] < bound]
        whole, left = sum([portions[i] for i in free]), spare
        for i in free:
            addition = min(bound - given[i], max(1, left * portions[i] // whole), spare)
            given[i] = given[i] + addition
            spare = spare - addition
    return np.array(given)


def noise(rng, extent, deviation, limit, shards=(), held_as=jnp.bfloat16):
    array = deviation * jax.random.normal(rng, extent, jnp.float32)
    if shards:
        array = array * level_of(rng, extent, shards, -0.22, 0.18)
    return jnp.clip(array, -limit, limit).astype(held_as)


def setup_inputs(seed: int = 0) -> dict:
    streams_of = jax.random.split(jax.random.key(seed), 9)
    features = noise(streams_of[0], (VERTS // 2, 2 * H), 1.0, 6.0, ((0, 64), (1, 4)))
    hub_feats = noise(streams_of[1], (HUBS, H), 1.0, 6.0, ((0, 64),))
    nbr_owner_keys = jax.random.split(jax.random.fold_in(streams_of[2], 1), K * VERTS // V_DEV)
    nbr_owner_turns = jax.random.permutation(jax.random.fold_in(streams_of[2], 3), K * VERTS // V_DEV)
    nbr_owner = jax.vmap(lambda own, number: assign_block(jax.random.fold_in(streams_of[2], 2), own, number, V_DEV, N_DOM, 1, CAPK, 2))(nbr_owner_keys, nbr_owner_turns).reshape((K, VERTS, 1))
    nbr_row = plant(jax.random.randint(streams_of[3], (K, VERTS), 0, V_DEV), jax.random.fold_in(streams_of[3], 1), 0, V_DEV - 1).astype(jnp.int32)
    hub_ids = plant(ranked_ids(streams_of[4], (VERTS, KH), HUBS, 2), jax.random.fold_in(streams_of[4], 3), 0, HUBS - 1).astype(jnp.int32)
    w_self = noise(streams_of[5], (H, H), H ** -0.5, 0.375)
    w_nbr = noise(streams_of[6], (H, H), H ** -0.5, 0.375)
    grad_out = noise(streams_of[7], (VERTS // 2, 2 * H), 1.0, 6.0, ((0, 64), (1, 4)))
    return dict(features=features, hub_feats=hub_feats, nbr_owner=nbr_owner, nbr_row=nbr_row, hub_ids=hub_ids, w_self=w_self, w_nbr=w_nbr, grad_out=grad_out)


def reference(features, hub_feats, nbr_owner, nbr_row, hub_ids, w_self, w_nbr, grad_out):
    divisor = float(K + KH)
    feature_rows = features.reshape(VERTS, H)
    grad_rows = grad_out.reshape(VERTS, H)
    flat_index = (nbr_owner[:, :, 0] * V_DEV + nbr_row).astype(jnp.int32)
    running = jnp.zeros((VERTS, H), jnp.float32)
    for level_index in range(K):
        running = running + feature_rows[flat_index[level_index]].astype(jnp.float32)
    for column in range(KH):
        running = running + hub_feats[hub_ids[:, column]].astype(jnp.float32)
    mean_rows = (running / divisor).astype(jnp.bfloat16)
    pre_act = jnp.dot(feature_rows, w_self, preferred_element_type=jnp.float32) + jnp.dot(mean_rows, w_nbr, preferred_element_type=jnp.float32)
    outputs = jax.nn.silu(pre_act).astype(jnp.bfloat16)
    gate_sig = jax.nn.sigmoid(pre_act)
    grad_pre = (grad_rows.astype(jnp.float32) * gate_sig * (1.0 + pre_act * (1.0 - gate_sig))).astype(jnp.bfloat16)
    grad_self = jnp.dot(feature_rows.T, grad_pre, preferred_element_type=jnp.float32)
    grad_nbr = jnp.dot(mean_rows.T, grad_pre, preferred_element_type=jnp.float32)
    self_term = jnp.dot(grad_pre, w_self.T, preferred_element_type=jnp.float32)
    grad_mean = (jnp.dot(grad_pre, w_nbr.T, preferred_element_type=jnp.float32) / divisor).astype(jnp.bfloat16)
    mean_wide = grad_mean.astype(jnp.float32)
    neighbour_grad = jnp.zeros((VERTS, H), jnp.float32)
    for level_index in range(K):
        neighbour_grad = neighbour_grad.at[flat_index[level_index]].add(mean_wide)
    grad_hubs = jnp.zeros((HUBS, H), jnp.float32)
    for column in range(KH):
        grad_hubs = grad_hubs.at[hub_ids[:, column]].add(mean_wide)
    grad_features = (self_term + neighbour_grad).astype(jnp.bfloat16)
    return outputs.reshape(VERTS // 2, 2 * H), grad_features.reshape(VERTS // 2, 2 * H), grad_hubs, grad_self, grad_nbr
```

```python
import functools

import jax
import jax.numpy as jnp
from jax import lax
from jax.experimental import pallas as pl
from jax.experimental.pallas import tpu as pltpu
from jax.sharding import Mesh, PartitionSpec as P

NY, NZ, NC, NX = 4, 8, 2, 4
V = 512
HALF = 256
COLS = 128
PLANE = NY * NC * V
HUB_ROWS = 16
BLOCK = HALF + HUB_ROWS
BF = jnp.bfloat16
F32 = jnp.float32


def shift(x, axis, size, step):
    return lax.ppermute(x, axis, [(i, (i + step) % size) for i in range(size)])


def swap(x, axis, size, mask):
    return lax.ppermute(x, axis, [(i, i ^ mask) for i in range(size)])


def count_kernel(place, ids_ref, out_ref, *, first):
    delta = pl.program_id(0) + first
    owner = place[0] * (NZ * NC) + ((place[1] + delta) % NZ) * NC + place[2]
    parity = place[3] // 2
    rows = lax.broadcasted_iota(jnp.int32, (16, 16, 128), 0) * 16 + lax.broadcasted_iota(
        jnp.int32, (16, 16, 128), 1
    )
    rows = rows.astype(F32).astype(BF)

    def multiplicity(keys):
        total = jnp.zeros(keys.shape, F32)
        for k in range(keys.shape[0]):
            total = total + (keys == keys[k : k + 1]).astype(F32)
        return total

    def spread(row):
        return jnp.broadcast_to(row, (16, 128)).astype(BF)

    def tile(index, carry):
        part = index // 4
        lane = pl.multiple_of((index % 4) * 128, 128)
        ids = ids_ref[part, :, pl.ds(lane, 128)]
        flat = ids[0:8]
        row = flat % V
        mine = (flat // V == owner) & (row % 2 == parity)
        keys = jnp.where(mine, row // 2, -1).astype(F32)
        times = multiplicity(keys)
        block = jnp.zeros((16, 16, 128), BF)
        for k in range(8):
            block = jnp.where(spread(keys[k : k + 1])[None] == rows, spread(times[k : k + 1])[None], block)
        dest = pl.ds(pl.multiple_of(index * 128, 128), 128)
        out_ref[0, 0:HALF, dest] = block.reshape(HALF, 128)
        hub = ids[8:16]
        hub_row = hub % (2 * HUB_ROWS)
        here = hub // (2 * HUB_ROWS) == owner
        for which in range(2):
            side = parity if which == 0 else 1 - parity
            hub_keys = jnp.where(here & (hub_row % 2 == side), hub_row // 2, -1).astype(F32)
            hub_times = multiplicity(hub_keys[0:4])
            hub_block = jnp.zeros((16, 128), BF)
            for j in range(4):
                hub_block = jnp.where(
                    spread(hub_keys[j : j + 1]) == rows[0], spread(hub_times[j : j + 1]), hub_block
                )
            start = HALF + which * HUB_ROWS
            out_ref[0, start : start + HUB_ROWS, dest] = hub_block
        return carry

    lax.fori_loop(0, PLANE // 128, tile, 0)


def counts_of(ids, place, first, number):
    rows = HALF + 2 * HUB_ROWS
    return pl.pallas_call(
        functools.partial(count_kernel, first=first),
        out_shape=jax.ShapeDtypeStruct((number, rows, PLANE), BF),
        grid_spec=pltpu.PrefetchScalarGridSpec(
            num_scalar_prefetch=1,
            grid=(number,),
            in_specs=[pl.BlockSpec((NY * NC, 16, V), lambda d, s: (0, 0, 0))],
            out_specs=pl.BlockSpec((1, rows, PLANE), lambda d, s: (d, 0, 0)),
        ),
        compiler_params=pltpu.CompilerParams(vmem_limit_bytes=24 << 20),
        cost_estimate=pl.CostEstimate(
            flops=number * rows * PLANE * 16, bytes_accessed=number * rows * PLANE * 2, transcendentals=0
        ),
        name="counts",
    )(place, ids)


def dense_kernel(
    place, f0, f1, f2, f3, g0, g1, g2, g3, s0, s1, s2, s3, ws_ref, wn_ref,
    out_ref, grad_ref, self_ref, weight_ref,
    f_scr, g_scr, s_scr, o_scr, w_scr,
):
    x = place[3]
    parity, half = x // 2, x % 2
    for mask, (fr, gr, sr) in enumerate(((f0, g0, s0), (f1, g1, s1), (f2, g2, s2), (f3, g3, s3))):
        f_scr[x ^ mask] = fr[...]
        g_scr[x ^ mask] = gr[...]
        s_scr[x ^ mask] = sr[...]
    feats = jnp.concatenate(
        [jnp.concatenate([f_scr[0], f_scr[1]], 1), jnp.concatenate([f_scr[2], f_scr[3]], 1)], 0
    )
    cot = jnp.concatenate(
        [jnp.concatenate([g_scr[0], g_scr[1]], 1), jnp.concatenate([g_scr[2], g_scr[3]], 1)], 0
    ).astype(F32)
    mean_t = jnp.concatenate(
        [
            s_scr[0].astype(F32) + s_scr[2].astype(F32),
            s_scr[1].astype(F32) + s_scr[3].astype(F32),
        ],
        0,
    )
    mean_t = (mean_t / 12.0).astype(BF)
    ordered = lax.broadcasted_iota(jnp.int32, (V, V), 0)
    natural = lax.broadcasted_iota(jnp.int32, (V, V), 1)
    order = ((ordered % HALF) * 2 + ordered // HALF == natural).astype(F32).astype(BF)
    last = (((1,), (1,)), ((), ()))
    firsts = (((0,), (0,)), ((), ()))
    dot = functools.partial(lax.dot_general, preferred_element_type=F32)
    mean = dot(order, mean_t, last).astype(BF)
    w_self, w_nbr = ws_ref[...], wn_ref[...]
    plain = (((1,), (0,)), ((), ()))
    pre = dot(feats, w_self, plain) + dot(mean, w_nbr, plain)
    sig = jax.nn.sigmoid(pre)
    value = (pre * sig).astype(BF)
    grad_pre = (cot * sig * (1.0 + pre * (1.0 - sig))).astype(BF)
    for q in range(2):
        for h in range(2):
            o_scr[q * 2 + h] = value[q * HALF : (q + 1) * HALF, h * COLS : (h + 1) * COLS]
    out_ref[...] = o_scr[x]
    rows = pl.ds(pl.multiple_of(half * COLS, COLS), COLS)
    grad_mean = (dot(grad_pre, wn_ref[rows, :], last) / 12.0).astype(BF)
    grad_ref[...] = dot(order, grad_mean, firsts).astype(BF)
    own_self = dot(grad_pre, ws_ref[rows, :], last)
    self_ref[...] = jnp.where(parity == 0, own_self[0:HALF], own_self[HALF:V])
    w_scr[0] = dot(feats, grad_pre, firsts)
    w_scr[1] = dot(mean, grad_pre, firsts)
    quarter = pl.ds(pl.multiple_of(x * 64, 64), 64)
    for which in range(2):
        part = w_scr[which, quarter, :]
        for h in range(2):
            start = which * 128 + h * 64
            weight_ref[start : start + 64, :] = part[:, h * COLS : (h + 1) * COLS].astype(BF)


def dense(place, feats, cots, sums, w_self, w_nbr):
    vm = pl.BlockSpec(memory_space=pltpu.VMEM)
    return pl.pallas_call(
        dense_kernel,
        out_shape=(
            jax.ShapeDtypeStruct((HALF, COLS), BF),
            jax.ShapeDtypeStruct((V, COLS), BF),
            jax.ShapeDtypeStruct((HALF, COLS), F32),
            jax.ShapeDtypeStruct((256, COLS), BF),
        ),
        in_specs=[pl.BlockSpec(memory_space=pltpu.SMEM)] + [vm] * 14,
        out_specs=(vm, vm, vm, vm),
        scratch_shapes=[
            pltpu.VMEM((4, HALF, COLS), BF),
            pltpu.VMEM((4, HALF, COLS), BF),
            pltpu.VMEM((4, COLS, V), BF),
            pltpu.VMEM((4, HALF, COLS), BF),
            pltpu.VMEM((2, 256, 256), F32),
        ],
        compiler_params=pltpu.CompilerParams(vmem_limit_bytes=24 << 20),
        name="dense",
    )(place, *feats, *cots, *sums, w_self, w_nbr)


def final_kernel(
    place, self_ref, nbr0, nbr1, nbr2, hub0, hub1, hub2, w0, w1, w2, w3, w4, w5, w6, w7,
    feat_ref, hub_ref, gself_ref, gnbr_ref, w_scr,
):
    z = place[1]
    total = nbr0[...] + nbr1[...].astype(F32) + nbr2[...].astype(F32)
    feat_ref[...] = (self_ref[...] + total).astype(BF)
    hub_ref[...] = hub0[...].astype(F32) + hub1[...].astype(F32) + hub2[...].astype(F32)
    for step, ref in enumerate((w0, w1, w2, w3, w4, w5, w6, w7)):
        w_scr[(z + step) % NZ] = ref[...]
    weight = w_scr[0].astype(F32)
    for step in range(1, NZ):
        weight = weight + w_scr[step].astype(F32)
    gself_ref[...] = jnp.concatenate([weight[0:64], weight[64:128]], 1)
    gnbr_ref[...] = jnp.concatenate([weight[128:192], weight[192:256]], 1)


def final(place, self_term, nbrs, hubs, weights):
    vm = pl.BlockSpec(memory_space=pltpu.VMEM)
    return pl.pallas_call(
        final_kernel,
        out_shape=(
            jax.ShapeDtypeStruct((HALF, COLS), BF),
            jax.ShapeDtypeStruct((HUB_ROWS, COLS), F32),
            jax.ShapeDtypeStruct((64, 256), F32),
            jax.ShapeDtypeStruct((64, 256), F32),
        ),
        in_specs=[pl.BlockSpec(memory_space=pltpu.SMEM)] + [vm] * 15,
        out_specs=(vm, vm, vm, vm),
        scratch_shapes=[pltpu.VMEM((NZ, 256, COLS), BF)],
        name="last_sums",
    )(place, self_term, *nbrs, *hubs, *weights)


def body(features, hub_feats, nbr_owner, nbr_row, hub_ids, w_self, w_nbr, grad_out):
    y, z, c, x = (lax.axis_index(a) for a in ("y", "z", "c", "x"))
    parity, half = x // 2, x % 2
    place = jnp.stack([y, z, c, x]).astype(jnp.int32)

    flat = nbr_owner.reshape(8, V) * V + nbr_row
    ids = jnp.concatenate([flat, hub_ids.T, jnp.full((4, V), -1, jnp.int32)], 0)
    ids_y = jnp.stack([ids] + [swap(ids, "y", NY, m) for m in range(1, NY)])
    ids_plane = jnp.concatenate([ids_y, swap(ids_y, "c", NC, 1)], 0)

    hub_own = lax.dynamic_slice(
        lax.dynamic_index_in_dim(hub_feats.reshape(HUB_ROWS, 2, 256), parity, 1, keepdims=False),
        (0, half * COLS),
        (HUB_ROWS, COLS),
    )
    mine = jnp.concatenate([features, hub_own], 0)
    ahead, behind = [mine], [mine]
    for step in range(4):
        ahead.append(shift(ahead[-1], "z", NZ, -1))
        if step < 3:
            behind.append(shift(behind[-1], "z", NZ, 1))
    tables = ahead + behind[:0:-1]

    counts = counts_of(ids_plane, place, 0, NZ)
    firsts = (((0,), (0,)), ((), ()))
    table = jnp.stack(tables)
    part = lax.dot_general(
        table, counts[:, :BLOCK], (((0, 1), (0, 1)), ((), ())), preferred_element_type=F32
    )
    both = part[:, : PLANE // 2] + swap(part[:, PLANE // 2 :].astype(BF), "c", NC, 1).astype(F32)
    mine_sum = both[:, :V]
    for m in range(1, NY):
        mine_sum = mine_sum + swap(both[:, m * V : (m + 1) * V].astype(BF), "y", NY, m).astype(F32)
    mine_sum = mine_sum.astype(BF)

    feats = [features] + [swap(features, "x", NX, m) for m in range(1, NX)]
    cots = [grad_out] + [swap(grad_out, "x", NX, m) for m in range(1, NX)]
    sums = [mine_sum] + [swap(mine_sum, "x", NX, m) for m in range(1, NX)]
    outputs, grad_mean, self_term, weight = dense(place, feats, cots, sums, w_self, w_nbr)

    message = jnp.concatenate([grad_mean, weight], 0)
    got = [message] + [swap(message, "y", NY, m) for m in range(1, NY)]
    weight = (got[0][V:].astype(F32) + got[1][V:].astype(F32)) + (
        got[2][V:].astype(F32) + got[3][V:].astype(F32)
    )
    grads = jnp.concatenate([g[:V] for g in got], 0)
    message = jnp.concatenate([grads, weight.astype(BF)], 0)
    other = swap(message, "c", NC, 1)
    weight = (message[NY * V :].astype(F32) + other[NY * V :].astype(F32)).astype(BF)
    grads = jnp.concatenate([grads, other[: NY * V]], 0)

    lane = lax.broadcasted_iota(jnp.int32, (HUB_ROWS, COLS), 1)

    def term(delta):
        rows = jnp.dot(counts[delta], grads, preferred_element_type=F32)
        own = rows[HALF:BLOCK]
        rest = jnp.roll(rows[BLOCK:], 64, 1)
        hub = jnp.where((lane < 64) == (parity == 0), own, rest)
        return rows[:HALF], hub

    def cross(hub, step):
        pairs = []
        for a in range(NZ):
            for b in range(NX):
                target = {0: 0, 1: 2, 2: 1, 3: 3}[b]
                pairs.append((a * NX + b, ((a + step) % NZ) * NX + target))
        return lax.ppermute(hub, ("z", "x"), pairs)

    def travel(deltas, step):
        passing, seen = weight, []
        total, hub = term(deltas[0])
        for index in range(len(deltas)):
            pieces = [total.astype(BF), passing]
            final_hop = index == len(deltas) - 1
            if not final_hop:
                pieces.insert(1, hub.astype(BF))
            arrived = shift(jnp.concatenate(pieces, 0), "z", NZ, step)
            passing = arrived[-256:]
            seen.append(passing)
            if final_hop:
                return arrived[:HALF], cross(hub.astype(BF), step), seen
            more, more_hub = term(deltas[index + 1])
            total = arrived[:HALF].astype(F32) + more
            hub = arrived[HALF:BLOCK].astype(F32) + more_hub

    nbr_up, hub_up, seen_up = travel([4, 3, 2, 1], 1)
    nbr_down, hub_down, seen_down = travel([5, 6, 7], -1)
    nbr_here, hub_here = term(0)
    hub_here = cross(hub_here.astype(BF), 0)
    weights = [weight] + seen_down + seen_up[::-1]
    grad_features, hub_rows, grad_self, grad_nbr = final(
        place, self_term, (nbr_here, nbr_up, nbr_down), (hub_here, hub_up, hub_down), weights
    )
    return outputs, grad_features, hub_rows.reshape(2 * HUB_ROWS, 64), grad_self, grad_nbr


def solution(mesh):
    fine = Mesh(mesh.devices.reshape(NY, NZ, NC, NX), ("y", "z", "c", "x"))
    dom = ("y", "z", "c")
    in_specs = (
        P(dom, "x"),
        P(dom, None),
        P(None, dom, None),
        P(None, dom),
        P(dom, None),
        P(),
        P(),
        P(dom, "x"),
    )
    out_specs = (P(dom, "x"), P(dom, "x"), P(dom, "x"), P("x", None), P("x", None))
    return jax.shard_map(body, mesh=fine, in_specs=in_specs, out_specs=out_specs, check_vma=False)
```

```python
import functools

import jax
import jax.numpy as jnp
from jax import lax
from jax.experimental import pallas as pl
from jax.experimental.pallas import tpu as pltpu
from jax.sharding import Mesh, PartitionSpec as P

NY, NZ, NC, NX = 4, 8, 2, 4
V = 512
HALF = 256
COLS = 128
HUB_ROWS = 16
BLOCK = HALF + HUB_ROWS
ROWS = (NZ + 1) * HALF
PARTS = NC * NY
WROWS = 256
DISTINCT = 4
BF = jnp.bfloat16
F32 = jnp.float32
VM = pl.BlockSpec(memory_space=pltpu.VMEM)
SM = pl.BlockSpec(memory_space=pltpu.SMEM)
PLAIN = (((1,), (0,)), ((), ()))
LAST = (((1,), (1,)), ((), ()))
FIRST = (((0,), (0,)), ((), ()))


def dot(a, b, dims=PLAIN, **kw):
    return lax.dot_general(a, b, dims, preferred_element_type=F32, **kw)


def shift(x, axis, size, step):
    return lax.ppermute(x, axis, [(i, (i + step) % size) for i in range(size)])


def swap(x, axis, size, mask):
    return lax.ppermute(x, axis, [(i, i ^ mask) for i in range(size)])


def call(kernel, outs, inputs, name, scratch=(), flops=0, mib=16):
    return pl.pallas_call(
        kernel,
        out_shape=outs,
        in_specs=[SM] + [VM] * (len(inputs) - 1),
        out_specs=jax.tree.map(lambda _: VM, outs),
        scratch_shapes=list(scratch),
        compiler_params=pltpu.CompilerParams(vmem_limit_bytes=mib << 20),
        cost_estimate=pl.CostEstimate(flops=flops, bytes_accessed=1 << 18, transcendentals=0),
        name=name,
    )(*inputs)


def shaped(shape, dtype):
    return jax.ShapeDtypeStruct(shape, dtype)


def prepare_kernel(place, feat_ref, cot_ref, hub_ref, owner_ref, row_ref, hub_id_ref, ids_ref, mine_ref, both_ref):
    parity, half = place[3] // 2, place[3] % 2
    ids_ref[0:8] = owner_ref[...] * V + row_ref[...]
    ids_ref[8:12] = hub_id_ref[...]
    ids_ref[12:16] = jnp.full((4, V), -1, jnp.int32)
    mine_ref[0:HALF] = feat_ref[...]
    pick = lax.broadcasted_iota(jnp.int32, (HUB_ROWS, 2 * HUB_ROWS), 1) == (
        2 * lax.broadcasted_iota(jnp.int32, (HUB_ROWS, 2 * HUB_ROWS), 0) + parity
    )
    columns = hub_ref[:, pl.ds(pl.multiple_of(half * COLS, COLS), COLS)]
    mine_ref[HALF:BLOCK] = dot(pick.astype(F32).astype(BF), columns).astype(BF)
    both_ref[0:HALF] = feat_ref[...]
    both_ref[HALF:V] = cot_ref[...]


def counts_kernel(place, ids0, ids1, ids2, ids3, out_ref):
    y, z, c, x = place[0], place[1], place[2], place[3]
    parity = x // 2
    rows = lax.broadcasted_iota(jnp.int32, (16, 16, 128), 0) * 16 + lax.broadcasted_iota(
        jnp.int32, (16, 16, 128), 1
    )
    rows = rows.astype(F32).astype(BF)
    level = lax.broadcasted_iota(jnp.int32, (8, V), 0)
    column = y * (NZ * NC) + c
    mask = (NY - 1) * (NZ * NC) + (NC - 1)

    def allmax(a):
        for s in (4, 2, 1):
            a = jnp.maximum(a, pltpu.roll(a, s, 0))
        return a

    def allsum(a):
        for s in (4, 2, 1):
            a = a + pltpu.roll(a, s, 0)
        return a

    def extract(keys):
        top = allmax(keys)
        hit = keys == top
        return jnp.where(hit, -1.0, keys), top, allsum(jnp.where(hit, 1.0, 0.0))

    def pair(a):
        return jnp.concatenate([a, a], 0).astype(BF)

    for dy, ids_ref in enumerate((ids0, ids1, ids2, ids3)):

        def part(dc, carry, dy=dy, ids_ref=ids_ref):
            index = dc * NY + dy
            ids = ids_ref[dc]
            flat, hub = ids[0:8], ids[8:16]
            here = ((flat >> 9) & mask) == column
            here = here & ((flat & 1) == parity)
            keys = jnp.where(here, (((flat >> 10) - z) & 7) * HALF + ((flat >> 1) & 255), -1).astype(F32)
            here = (((hub >> 5) & mask) == column) & (level < 4)
            hub_row = (((hub >> 6) - z) & 7) * 32 + ((hub & 1) ^ parity) * 16 + ((hub >> 1) & 15)
            hub_keys = jnp.where(here, hub_row, -1).astype(F32)
            found, hub_found = [], []
            for _ in range(DISTINCT):
                keys, top, times = extract(keys)
                found.append((top, pair(times)))
            for _ in range(4):
                hub_keys, top, times = extract(hub_keys)
                hub_found.append((pair(top), pair(times)))
            for tile in range(V // 128):
                lanes = slice(tile * 128, (tile + 1) * 128)
                for delta in range(NZ):
                    block = jnp.zeros((16, 16, 128), BF)
                    for top, times in found:
                        match = pair(top[:, lanes] - float(HALF * delta))[None] == rows
                        block = jnp.where(match, times[:, lanes][None], block)
                    out_ref[index, delta * HALF : (delta + 1) * HALF, lanes] = block.reshape(HALF, 128)
                block = jnp.zeros((16, 16, 128), BF)
                for top, times in hub_found:
                    block = jnp.where(top[:, lanes][None] == rows, times[:, lanes][None], block)
                out_ref[index, NZ * HALF : ROWS, lanes] = block.reshape(HALF, 128)

            @pl.when(jnp.max(keys) >= 0)
            def _():
                def more(_, keys):
                    keys, top, times = extract(keys)
                    for tile in range(V // 128):
                        lanes = slice(tile * 128, (tile + 1) * 128)
                        for delta in range(NZ):
                            span = slice(delta * HALF, (delta + 1) * HALF)
                            block = out_ref[index, span, lanes].reshape(16, 16, 128)
                            match = pair(top[:, lanes] - float(HALF * delta))[None] == rows
                            block = jnp.where(match, pair(times[:, lanes])[None], block)
                            out_ref[index, span, lanes] = block.reshape(HALF, 128)
                    return keys

                lax.fori_loop(0, 8 - DISTINCT, more, keys)

            return carry

        lax.fori_loop(0, NC, part, 0)


def far_sums_kernel(place, counts, t0, t1, t7, t23, t65, t4, sums_ref, turned_ref, table):
    blocks = {0: t0[...], 1: t1[...], 7: t7[...], 4: t4[...]}
    blocks[2], blocks[3] = t23[0:BLOCK], t23[BLOCK : 2 * BLOCK]
    blocks[6], blocks[5] = t65[0:BLOCK], t65[BLOCK : 2 * BLOCK]
    for delta in range(NZ):
        table[delta * HALF : (delta + 1) * HALF] = blocks[delta][0:HALF]
        start = NZ * HALF + delta * 2 * HUB_ROWS
        table[start : start + HUB_ROWS] = blocks[delta][HALF:BLOCK]
        table[start + HUB_ROWS : start + 2 * HUB_ROWS] = jnp.zeros((HUB_ROWS, COLS), BF)
    turned_ref[...] = table[...].T

    def step(dy, carry):
        sums_ref[dy] = dot(turned_ref[...], counts[NY + dy]).astype(BF)
        return carry

    lax.fori_loop(0, NY, step, 0)


def near_sums_kernel(place, counts, turned, sums_ref):
    def step(dy, carry):
        sums_ref[dy] = dot(turned[...], counts[dy])
        return carry

    lax.fori_loop(0, NY, step, 0)


def dense_kernel(
    place, fg0, fg1, fg23, s0, s1, s2, s3, ws_ref, wn_ref,
    out_ref, message_ref, self_ref,
    f_scr, g_scr, s_scr, o_scr, w_scr,
):
    x = place[3]
    parity, half = x // 2, x % 2
    sources = ((fg0, 0), (fg1, 0), (fg23, 0), (fg23, V))
    for mask, ((ref, start), sr) in enumerate(zip(sources, (s0, s1, s2, s3))):
        f_scr[x ^ mask] = ref[start : start + HALF]
        g_scr[x ^ mask] = ref[start + HALF : start + V]
        s_scr[x ^ mask] = sr[...]
    feats = jnp.concatenate(
        [jnp.concatenate([f_scr[0], f_scr[1]], 1), jnp.concatenate([f_scr[2], f_scr[3]], 1)], 0
    )
    cot = jnp.concatenate(
        [jnp.concatenate([g_scr[0], g_scr[1]], 1), jnp.concatenate([g_scr[2], g_scr[3]], 1)], 0
    ).astype(F32)
    mean_t = jnp.concatenate(
        [
            s_scr[0].astype(F32) + s_scr[2].astype(F32),
            s_scr[1].astype(F32) + s_scr[3].astype(F32),
        ],
        0,
    )
    mean_t = (mean_t / 12.0).astype(BF)
    ordered = lax.broadcasted_iota(jnp.int32, (V, V), 0)
    natural = lax.broadcasted_iota(jnp.int32, (V, V), 1)
    order = ((ordered % HALF) * 2 + ordered // HALF == natural).astype(F32).astype(BF)
    mean = dot(order, mean_t, LAST).astype(BF)
    pre = dot(feats, ws_ref[...]) + dot(mean, wn_ref[...])
    sig = jax.nn.sigmoid(pre)
    value = (pre * sig).astype(BF)
    grad_pre = (cot * sig * (1.0 + pre * (1.0 - sig))).astype(BF)
    for q in range(2):
        for h in range(2):
            o_scr[q * 2 + h] = value[q * HALF : (q + 1) * HALF, h * COLS : (h + 1) * COLS]
    out_ref[...] = o_scr[x]
    rows = pl.ds(pl.multiple_of(half * COLS, COLS), COLS)
    grad_mean = (dot(grad_pre, wn_ref[rows, :], LAST) / 12.0).astype(BF)
    message_ref[0:V] = dot(order, grad_mean, FIRST).astype(BF)
    own_self = dot(grad_pre, ws_ref[rows, :], LAST)
    self_ref[...] = jnp.where(parity == 0, own_self[0:HALF], own_self[HALF:V])
    w_scr[0] = dot(feats, grad_pre, FIRST)
    w_scr[1] = dot(mean, grad_pre, FIRST)
    quarter = pl.ds(pl.multiple_of(x * 64, 64), 64)
    for which in range(2):
        part = w_scr[which, quarter, :]
        for h in range(2):
            start = V + which * 128 + h * 64
            message_ref[start : start + 64, :] = part[:, h * COLS : (h + 1) * COLS].astype(BF)


def gather_kernel(place, m0, m1, m2, m3, out_ref):
    for dy, ref in enumerate((m0, m1, m2, m3)):
        out_ref[dy * V : (dy + 1) * V] = ref[0:V]
    tail = slice(V, V + WROWS)
    weight = (m0[tail].astype(F32) + m1[tail].astype(F32)) + (m2[tail].astype(F32) + m3[tail].astype(F32))
    high = weight.astype(BF)
    out_ref[NY * V : NY * V + WROWS] = high
    out_ref[NY * V + WROWS :] = (weight - high.astype(F32)).astype(BF)


def near_grads_kernel(place, counts, m0, m1, m2, m3, out_ref):
    for block in range(NZ + 1):
        span = slice(block * HALF, (block + 1) * HALF)
        total = jnp.zeros((HALF, COLS), F32)
        for dy, ref in enumerate((m0, m1, m2, m3)):
            total = total + dot(counts[dy, span], ref[0:V])
        out_ref[block] = total


def far_block(counts, other, near, block):
    span = slice(block * HALF, (block + 1) * HALF)
    total = near[block]
    for dy in range(NY):
        total = total + dot(counts[NY + dy, span], other[dy * V : (dy + 1) * V])
    return total


def first_grads_kernel(place, counts, own, other, near, up_ref, down_ref, hub_ref):
    parity = place[3] // 2
    hubs = far_block(counts, other, near, NZ)
    lane = lax.broadcasted_iota(jnp.int32, (HUB_ROWS, COLS), 1)
    low = (lane < 64) == (parity == 0)
    for delta in range(NZ):
        start = delta * 2 * HUB_ROWS
        mine = hubs[start : start + HUB_ROWS]
        rest = pltpu.roll(hubs[start + HUB_ROWS : start + 2 * HUB_ROWS], 64, 1)
        hub_ref[delta] = jnp.where(low, mine, rest)
    high, small = slice(NY * V, NY * V + WROWS), slice(NY * V + WROWS, NY * V + 2 * WROWS)
    weight = (own[high].astype(F32) + own[small].astype(F32)) + (
        other[high].astype(F32) + other[small].astype(F32)
    )
    weight = weight.astype(BF)
    for delta, ref in ((4, up_ref), (5, down_ref)):
        ref[0:HALF] = far_block(counts, other, near, delta).astype(BF)
        ref[HALF:BLOCK] = hub_ref[delta].astype(BF)
        ref[BLOCK:] = weight


REST = (0, 1, 2, 3, 6, 7)


def rest_grads_kernel(place, counts, other, near, out_ref):
    for index, delta in enumerate(REST):
        out_ref[index] = far_block(counts, other, near, delta)


def hop_kernel(place, up, down, rest, hubs, next_up, next_down, *, deltas):
    for delta, got, ref in zip(deltas, (up, down), (next_up, next_down)):
        ref[0:HALF] = (got[0:HALF].astype(F32) + rest[REST.index(delta)]).astype(BF)
        ref[HALF:BLOCK] = (got[HALF:BLOCK].astype(F32) + hubs[delta]).astype(BF)
        ref[BLOCK:] = got[BLOCK:]


def last_hop_kernel(place, up, down, rest, hubs, next_up, hub_up, hub_here):
    next_up[0:HALF] = (up[0:HALF].astype(F32) + rest[REST.index(1)]).astype(BF)
    next_up[HALF:] = up[BLOCK:]
    hub_up[...] = up[HALF:BLOCK].astype(F32) + hubs[1]
    hub_here[...] = down[HALF:BLOCK].astype(F32) + hubs[0]


def final_kernel(
    place, self_ref, rest, first, up1, up2, up3, up4, down1, down2, down3, hub_up, hub_here,
    feat_ref, hub_ref, gself_ref, gnbr_ref, w_scr,
):
    z = place[1]
    total = rest[0] + up4[0:HALF].astype(F32) + down3[0:HALF].astype(F32)
    feat_ref[...] = (self_ref[...] + total).astype(BF)
    hubs = hub_up[...] + hub_here[...]
    shape = (2 * HUB_ROWS, HUB_ROWS)
    target = lax.broadcasted_iota(jnp.int32, shape, 0)
    source = lax.broadcasted_iota(jnp.int32, shape, 1)
    spread = [
        dot((target == 2 * source + q).astype(F32), hubs[:, q * 64 : (q + 1) * 64], precision=lax.Precision.HIGHEST)
        for q in range(2)
    ]
    hub_ref[...] = spread[0] + spread[1]
    arrived = {0: first, 7: up1, 6: up2, 5: up3, 1: down1, 2: down2, 3: down3}
    for step in range(NZ):
        if step == 4:
            w_scr[(z + step) % NZ] = up4[HALF:]
        else:
            w_scr[(z + step) % NZ] = arrived[step][BLOCK:]
    weight = w_scr[0].astype(F32)
    for step in range(1, NZ):
        weight = weight + w_scr[step].astype(F32)
    gself_ref[...] = jnp.concatenate([weight[0:64], weight[64:128]], 1)
    gnbr_ref[...] = jnp.concatenate([weight[128:192], weight[192:256]], 1)


def body(features, hub_feats, nbr_owner, nbr_row, hub_ids, w_self, w_nbr, grad_out):
    place = jnp.stack([lax.axis_index(a) for a in ("y", "z", "c", "x")]).astype(jnp.int32)
    ids, mine, fg = call(
        prepare_kernel,
        (shaped((16, V), jnp.int32), shaped((BLOCK, COLS), BF), shaped((V, COLS), BF)),
        (place, features, grad_out, hub_feats, nbr_owner.reshape(8, V), nbr_row, hub_ids.T),
        "prepare",
    )

    t1, t7 = shift(mine, "z", NZ, -1), shift(mine, "z", NZ, 1)
    pair = jnp.stack([ids, swap(ids, "c", NC, 1)])
    fg1 = swap(fg, "x", NX, 1)
    pairs = [pair] + [swap(pair, "y", NY, m) for m in range(1, NY)]
    t23 = shift(jnp.concatenate([mine, t1], 0), "z", NZ, -2)
    t65 = shift(jnp.concatenate([mine, t7], 0), "z", NZ, 2)
    t4 = shift(t1, "z", NZ, -3)
    fg23 = swap(jnp.concatenate([fg, fg1], 0), "x", NX, 2)
    counts = call(
        counts_kernel,
        pltpu.VMEM((PARTS, ROWS, V), BF),
        (place, *pairs),
        "counts",
        flops=1 << 34,
        mib=8,
    )

    far, turned = call(
        far_sums_kernel,
        (shaped((NY, COLS, V), BF), shaped((COLS, ROWS), BF)),
        (place, counts, mine, t1, t7, t23, t65, t4),
        "far_sums",
        scratch=[pltpu.VMEM((ROWS, COLS), BF)],
        flops=1 << 31,
    )
    got = swap(far, "c", NC, 1)
    near = call(
        near_sums_kernel, shaped((NY, COLS, V), F32), (place, counts, turned), "near_sums", flops=1 << 31
    )
    both = near + got.astype(F32)
    total = both[0]
    for m in range(1, NY):
        total = total + swap(both[m].astype(BF), "y", NY, m).astype(F32)
    total = total.astype(BF)
    sums = [total] + [swap(total, "x", NX, m) for m in range(1, NX)]

    outputs, message, self_term = call(
        dense_kernel,
        (shaped((HALF, COLS), BF), shaped((V + WROWS, COLS), BF), shaped((HALF, COLS), F32)),
        (place, fg, fg1, fg23, *sums, w_self, w_nbr),
        "dense",
        scratch=[
            pltpu.VMEM((4, HALF, COLS), BF),
            pltpu.VMEM((4, HALF, COLS), BF),
            pltpu.VMEM((4, COLS, V), BF),
            pltpu.VMEM((4, HALF, COLS), BF),
            pltpu.VMEM((2, 256, 256), F32),
        ],
        flops=1 << 30,
    )

    messages = [message] + [swap(message, "y", NY, m) for m in range(1, NY)]
    own = call(
        gather_kernel, shaped((NY * V + 2 * WROWS, COLS), BF), (place, *messages), "gather_grads"
    )
    other = swap(own, "c", NC, 1)
    near_grads = call(
        near_grads_kernel,
        shaped((NZ + 1, HALF, COLS), F32),
        (place, counts, *messages),
        "near_grads",
        flops=1 << 31,
    )
    up0, down0, hubs = call(
        first_grads_kernel,
        (
            shaped((BLOCK + WROWS, COLS), BF),
            shaped((BLOCK + WROWS, COLS), BF),
            shaped((NZ, HUB_ROWS, COLS), F32),
        ),
        (place, counts, own, other, near_grads),
        "first_grads",
        flops=1 << 29,
    )
    up1, down1 = shift(up0, "z", NZ, 1), shift(down0, "z", NZ, -1)
    rest = call(
        rest_grads_kernel,
        shaped((len(REST), HALF, COLS), F32),
        (place, counts, other, near_grads),
        "rest_grads",
        flops=1 << 30,
    )
    hop_shapes = (shaped((BLOCK + WROWS, COLS), BF),) * 2
    ups, downs = [up1], [down1]
    for deltas in ((3, 6), (2, 7)):
        up, down = call(
            functools.partial(hop_kernel, deltas=deltas),
            hop_shapes,
            (place, ups[-1], downs[-1], rest, hubs),
            "hop",
        )
        ups.append(shift(up, "z", NZ, 1))
        downs.append(shift(down, "z", NZ, -1))
    up, hub_up, hub_here = call(
        last_hop_kernel,
        (
            shaped((HALF + WROWS, COLS), BF),
            shaped((HUB_ROWS, COLS), F32),
            shaped((HUB_ROWS, COLS), F32),
        ),
        (place, ups[-1], downs[-1], rest, hubs),
        "last_hop",
    )
    ups.append(shift(up, "z", NZ, 1))
    turn = (0, 2, 1, 3)
    cross = [(z * NX + x, (z + 1) % NZ * NX + turn[x]) for z in range(NZ) for x in range(NX)]
    hub_up = lax.ppermute(hub_up, ("z", "x"), cross)
    hub_here = lax.ppermute(hub_here, "x", [(x, turn[x]) for x in range(NX)])
    grad_features, hub_rows, grad_self, grad_nbr = call(
        final_kernel,
        (
            shaped((HALF, COLS), BF),
            shaped((2 * HUB_ROWS, 64), F32),
            shaped((64, 256), F32),
            shaped((64, 256), F32),
        ),
        (place, self_term, rest, up0, *ups, *downs, hub_up, hub_here),
        "last_sums",
        scratch=[pltpu.VMEM((NZ, WROWS, COLS), BF)],
    )
    return outputs, grad_features, hub_rows, grad_self, grad_nbr


def solution(mesh):
    fine = Mesh(mesh.devices.reshape(NY, NZ, NC, NX), ("y", "z", "c", "x"))
    dom = ("y", "z", "c")
    in_specs = (
        P(dom, "x"),
        P(dom, None),
        P(None, dom, None),
        P(None, dom),
        P(dom, None),
        P(),
        P(),
        P(dom, "x"),
    )
    out_specs = (P(dom, "x"), P(dom, "x"), P(dom, "x"), P("x", None), P("x", None))
    return jax.shard_map(body, mesh=fine, in_specs=in_specs, out_specs=out_specs, check_vma=False)
```

```python
import functools

import jax
import jax.numpy as jnp
from jax import lax
from jax.experimental import pallas as pl
from jax.experimental.pallas import tpu as pltpu
from jax.sharding import Mesh, PartitionSpec as P

NY, NZ, NC, NX = 4, 8, 2, 4
V = 512
HALF = 256
COLS = 128
HUB_ROWS = 16
BLOCK = HALF + HUB_ROWS
ROWS = (NZ + 1) * HALF
PARTS = NC * NY
WROWS = 256
DISTINCT = 4
BF = jnp.bfloat16
F32 = jnp.float32
VM = pl.BlockSpec(memory_space=pltpu.VMEM)
SM = pl.BlockSpec(memory_space=pltpu.SMEM)
PLAIN = (((1,), (0,)), ((), ()))
LAST = (((1,), (1,)), ((), ()))
FIRST = (((0,), (0,)), ((), ()))


def dot(a, b, dims=PLAIN, **kw):
    return lax.dot_general(a, b, dims, preferred_element_type=F32, **kw)


def shift(x, axis, size, step):
    return lax.ppermute(x, axis, [(i, (i + step) % size) for i in range(size)])


def swap(x, axis, size, mask):
    return lax.ppermute(x, axis, [(i, i ^ mask) for i in range(size)])


def call(kernel, outs, inputs, name, scratch=(), flops=0, mib=16, far=0):
    return pl.pallas_call(
        kernel,
        out_shape=outs,
        in_specs=[SM] + [VM] * (len(inputs) - 1 - far) + [pl.BlockSpec(memory_space=pl.ANY)] * far,
        out_specs=jax.tree.map(lambda _: VM, outs),
        scratch_shapes=list(scratch),
        compiler_params=pltpu.CompilerParams(vmem_limit_bytes=mib << 20),
        cost_estimate=pl.CostEstimate(flops=flops, bytes_accessed=1 << 18, transcendentals=0),
        name=name,
    )(*inputs)


def shaped(shape, dtype):
    return jax.ShapeDtypeStruct(shape, dtype)


def prepare_kernel(
    place, feat, cot, hub, owner, row, hub_id, ids_ref, mine_ref, both_ref,
    owner_scr, row_scr, hub_id_scr, hub_scr, sems,
):
    parity, half = place[3] // 2, place[3] % 2
    copies = [
        pltpu.make_async_copy(source, target, sems.at[index])
        for index, (source, target) in enumerate(
            (
                (owner, owner_scr),
                (row, row_scr),
                (hub_id, hub_id_scr),
                (hub, hub_scr),
                (feat, mine_ref.at[pl.ds(0, HALF)]),
                (feat, both_ref.at[pl.ds(0, HALF)]),
                (cot, both_ref.at[pl.ds(HALF, HALF)]),
            )
        )
    ]
    for copy in copies:
        copy.start()
    for copy in copies:
        copy.wait()
    ids_ref[0:8] = owner_scr[...].reshape(8, V) * V + row_scr[...]
    ids_ref[8:12] = hub_id_scr[...]
    ids_ref[12:16] = jnp.full((4, V), -1, jnp.int32)
    pick = lax.broadcasted_iota(jnp.int32, (HUB_ROWS, 2 * HUB_ROWS), 1) == (
        2 * lax.broadcasted_iota(jnp.int32, (HUB_ROWS, 2 * HUB_ROWS), 0) + parity
    )
    columns = hub_scr[:, pl.ds(pl.multiple_of(half * COLS, COLS), COLS)]
    mine_ref[HALF:BLOCK] = dot(pick.astype(F32).astype(BF), columns).astype(BF)


def counts_kernel(place, *refs, number):
    out_ref = refs[-1]
    y, z, c, x = place[0], place[1], place[2], place[3]
    parity = x // 2
    rows = lax.broadcasted_iota(jnp.int32, (16, 16, 128), 0) * 16 + lax.broadcasted_iota(
        jnp.int32, (16, 16, 128), 1
    )
    rows = rows.astype(F32).astype(BF)
    level = lax.broadcasted_iota(jnp.int32, (8, V), 0)
    column = y * (NZ * NC) + c
    mask = (NY - 1) * (NZ * NC) + (NC - 1)

    def allmax(a):
        for s in (4, 2, 1):
            a = jnp.maximum(a, pltpu.roll(a, s, 0))
        return a

    def allsum(a):
        for s in (4, 2, 1):
            a = a + pltpu.roll(a, s, 0)
        return a

    def extract(keys):
        top = allmax(keys)
        hit = keys == top
        return jnp.where(hit, -1.0, keys), top, allsum(jnp.where(hit, 1.0, 0.0))

    def pair(a):
        return jnp.concatenate([a, a], 0).astype(BF)

    for dy, ids_ref in enumerate(refs[:number]):

        def part(dc, carry, dy=dy, ids_ref=ids_ref):
            index = dc * number + dy
            ids = ids_ref[dc]
            flat, hub = ids[0:8], ids[8:16]
            here = ((flat >> 9) & mask) == column
            here = here & ((flat & 1) == parity)
            keys = jnp.where(here, (((flat >> 10) - z) & 7) * HALF + ((flat >> 1) & 255), -1).astype(F32)
            here = (((hub >> 5) & mask) == column) & (level < 4)
            hub_row = (((hub >> 6) - z) & 7) * 32 + ((hub & 1) ^ parity) * 16 + ((hub >> 1) & 15)
            hub_keys = jnp.where(here, hub_row, -1).astype(F32)
            found, hub_found = [], []
            for _ in range(DISTINCT):
                keys, top, times = extract(keys)
                found.append((top, pair(times)))
            for _ in range(4):
                hub_keys, top, times = extract(hub_keys)
                hub_found.append((pair(top), pair(times)))
            for tile in range(V // 128):
                lanes = slice(tile * 128, (tile + 1) * 128)
                for delta in range(NZ):
                    block = jnp.zeros((16, 16, 128), BF)
                    for top, times in found:
                        match = pair(top[:, lanes] - float(HALF * delta))[None] == rows
                        block = jnp.where(match, times[:, lanes][None], block)
                    out_ref[index, delta * HALF : (delta + 1) * HALF, lanes] = block.reshape(HALF, 128)
                block = jnp.zeros((16, 16, 128), BF)
                for top, times in hub_found:
                    block = jnp.where(top[:, lanes][None] == rows, times[:, lanes][None], block)
                out_ref[index, NZ * HALF : ROWS, lanes] = block.reshape(HALF, 128)

            @pl.when(jnp.max(keys) >= 0)
            def _():
                def more(_, keys):
                    keys, top, times = extract(keys)
                    for tile in range(V // 128):
                        lanes = slice(tile * 128, (tile + 1) * 128)
                        for delta in range(NZ):
                            span = slice(delta * HALF, (delta + 1) * HALF)
                            block = out_ref[index, span, lanes].reshape(16, 16, 128)
                            match = pair(top[:, lanes] - float(HALF * delta))[None] == rows
                            block = jnp.where(match, pair(times[:, lanes])[None], block)
                            out_ref[index, span, lanes] = block.reshape(HALF, 128)
                    return keys

                lax.fori_loop(0, 8 - DISTINCT, more, keys)

            return carry

        lax.fori_loop(0, NC, part, 0)


def near_counts_kernel(place, ids, t0, t1, t7, fg0, fg1, out_ref, ahead, behind, skip, both, token):
    ahead[0:BLOCK] = t0[...]
    ahead[BLOCK:] = t1[...]
    behind[0:BLOCK] = t0[...]
    behind[BLOCK:] = t7[...]
    skip[...] = t1[...]
    both[0:V] = fg0[...]
    both[V:] = fg1[...]
    token[...] = place[0] + jnp.zeros_like(token)
    counts_kernel(place, ids, out_ref, number=1)


def far_counts_kernel(place, token, ids1, ids2, ids3, out_ref):
    counts_kernel(place, ids1, ids2, ids3, out_ref, number=NY - 1)


def far_sums_kernel(place, counts0, counts, t0, t1, t7, t23, t65, t4, sums_ref, turned_ref, table):
    blocks = {0: t0[...], 1: t1[...], 7: t7[...], 4: t4[...]}
    blocks[2], blocks[3] = t23[0:BLOCK], t23[BLOCK : 2 * BLOCK]
    blocks[6], blocks[5] = t65[0:BLOCK], t65[BLOCK : 2 * BLOCK]
    for delta in range(NZ):
        table[delta * HALF : (delta + 1) * HALF] = blocks[delta][0:HALF]
        start = NZ * HALF + delta * 2 * HUB_ROWS
        table[start : start + HUB_ROWS] = blocks[delta][HALF:BLOCK]
        table[start + HUB_ROWS : start + 2 * HUB_ROWS] = jnp.zeros((HUB_ROWS, COLS), BF)
    turned_ref[...] = table[...].T
    sums_ref[0] = dot(turned_ref[...], counts0[1]).astype(BF)

    def step(dy, carry):
        sums_ref[dy] = dot(turned_ref[...], counts[NY - 2 + dy]).astype(BF)
        return carry

    lax.fori_loop(1, NY, step, 0)


def near_sums_kernel(place, counts0, counts, turned, sums_ref):
    sums_ref[0] = dot(turned[...], counts0[0])

    def step(dy, carry):
        sums_ref[dy] = dot(turned[...], counts[dy - 1])
        return carry

    lax.fori_loop(1, NY, step, 0)


def dense_kernel(
    place, fg0, fg1, fg23, s0, s1, s2, s3, ws_ref, wn_ref,
    out_ref, message_ref, self_ref,
    f_scr, g_scr, s_scr, o_scr, w_scr,
):
    x = place[3]
    parity, half = x // 2, x % 2
    sources = ((fg0, 0), (fg1, 0), (fg23, 0), (fg23, V))
    for mask, ((ref, start), sr) in enumerate(zip(sources, (s0, s1, s2, s3))):
        f_scr[x ^ mask] = ref[start : start + HALF]
        g_scr[x ^ mask] = ref[start + HALF : start + V]
        s_scr[x ^ mask] = sr[...]
    feats = jnp.concatenate(
        [jnp.concatenate([f_scr[0], f_scr[1]], 1), jnp.concatenate([f_scr[2], f_scr[3]], 1)], 0
    )
    cot = jnp.concatenate(
        [jnp.concatenate([g_scr[0], g_scr[1]], 1), jnp.concatenate([g_scr[2], g_scr[3]], 1)], 0
    ).astype(F32)
    mean_t = jnp.concatenate(
        [
            s_scr[0].astype(F32) + s_scr[2].astype(F32),
            s_scr[1].astype(F32) + s_scr[3].astype(F32),
        ],
        0,
    )
    mean_t = (mean_t / 12.0).astype(BF)
    ordered = lax.broadcasted_iota(jnp.int32, (V, V), 0)
    natural = lax.broadcasted_iota(jnp.int32, (V, V), 1)
    order = ((ordered % HALF) * 2 + ordered // HALF == natural).astype(F32).astype(BF)
    mean = dot(order, mean_t, LAST).astype(BF)
    pre = dot(feats, ws_ref[...]) + dot(mean, wn_ref[...])
    sig = jax.nn.sigmoid(pre)
    value = (pre * sig).astype(BF)
    grad_pre = (cot * sig * (1.0 + pre * (1.0 - sig))).astype(BF)
    for q in range(2):
        for h in range(2):
            o_scr[q * 2 + h] = value[q * HALF : (q + 1) * HALF, h * COLS : (h + 1) * COLS]
    out_ref[...] = o_scr[x]
    rows = pl.ds(pl.multiple_of(half * COLS, COLS), COLS)
    grad_mean = (dot(grad_pre, wn_ref[rows, :], LAST) / 12.0).astype(BF)
    message_ref[0:V] = dot(order, grad_mean, FIRST).astype(BF)
    own_self = dot(grad_pre, ws_ref[rows, :], LAST)
    self_ref[...] = jnp.where(parity == 0, own_self[0:HALF], own_self[HALF:V])
    w_scr[0] = dot(feats, grad_pre, FIRST)
    w_scr[1] = dot(mean, grad_pre, FIRST)
    quarter = pl.ds(pl.multiple_of(x * 64, 64), 64)
    for which in range(2):
        part = w_scr[which, quarter, :]
        for h in range(2):
            start = V + which * 128 + h * 64
            message_ref[start : start + 64, :] = part[:, h * COLS : (h + 1) * COLS].astype(BF)


def own_grads_kernel(place, counts0, m0, out_ref):
    for block in range(NZ + 1):
        out_ref[block] = dot(counts0[0, block * HALF : (block + 1) * HALF], m0[0:V])


def near_grads_kernel(place, counts, m1, m2, m3, start, out_ref):
    for block in range(NZ + 1):
        span = slice(block * HALF, (block + 1) * HALF)
        total = start[block]
        for dy, ref in enumerate((m1, m2, m3)):
            total = total + dot(counts[dy, span], ref[0:V])
        out_ref[block] = total


def far_block(counts0, counts, others, near, block):
    span = slice(block * HALF, (block + 1) * HALF)
    total = near[block] + dot(counts0[1, span], others[0][0:V])
    for dy in range(1, NY):
        total = total + dot(counts[NY - 2 + dy, span], others[dy][0:V])
    return total


def first_grads_kernel(
    place, counts0, counts, m0, m1, m2, m3, o0, o1, o2, o3, near, up_ref, down_ref, hub_ref, hub4_ref
):
    parity = place[3] // 2
    others = (o0, o1, o2, o3)
    hubs = far_block(counts0, counts, others, near, NZ)
    lane = lax.broadcasted_iota(jnp.int32, (HUB_ROWS, COLS), 1)
    low = (lane < 64) == (parity == 0)
    for delta in range(NZ):
        start = delta * 2 * HUB_ROWS
        mine = hubs[start : start + HUB_ROWS]
        rest = pltpu.roll(hubs[start + HUB_ROWS : start + 2 * HUB_ROWS], 64, 1)
        hub_ref[delta] = jnp.where(low, mine, rest)
    hub4_ref[...] = hub_ref[4]
    tail = slice(V, V + WROWS)
    sums = [
        (a[tail].astype(F32) + b[tail].astype(F32)) + (c[tail].astype(F32) + d[tail].astype(F32))
        for a, b, c, d in ((m0, m1, m2, m3), others)
    ]
    weight = (sums[0] + sums[1]).astype(BF)
    for delta, hub_delta, ref in ((4, 3, up_ref), (5, 5, down_ref)):
        ref[0:HALF] = far_block(counts0, counts, others, near, delta).astype(BF)
        ref[HALF:BLOCK] = hub_ref[hub_delta].astype(BF)
        ref[BLOCK:] = weight


REST = (0, 1, 2, 3, 6, 7)


def rest_grads_kernel(place, counts0, counts, o0, o1, o2, o3, near, out_ref):
    for index, delta in enumerate(REST):
        out_ref[index] = far_block(counts0, counts, (o0, o1, o2, o3), near, delta)


def hop_kernel(place, up, down, rest, hubs, next_up, next_down, *, deltas):
    for (delta, hub_delta), got, ref in zip(deltas, (up, down), (next_up, next_down)):
        ref[0:HALF] = (got[0:HALF].astype(F32) + rest[REST.index(delta)]).astype(BF)
        ref[HALF:BLOCK] = (got[HALF:BLOCK].astype(F32) + hubs[hub_delta]).astype(BF)
        ref[BLOCK:] = got[BLOCK:]


def last_hop_kernel(place, up, down, rest, hubs, hub4, next_up, hub_sum):
    next_up[0:HALF] = (up[0:HALF].astype(F32) + rest[REST.index(1)]).astype(BF)
    next_up[HALF:] = up[BLOCK:]
    arrived = up[HALF:BLOCK].astype(F32) + down[HALF:BLOCK].astype(F32)
    hub_sum[...] = arrived + hubs[0] + hub4[...]


def final_kernel(
    place, self_ref, rest, first, up1, up2, up3, up4, down1, down2, down3, hub_sum,
    feat_ref, hub_ref, gself_ref, gnbr_ref, w_scr,
):
    z = place[1]
    total = rest[0] + up4[0:HALF].astype(F32) + down3[0:HALF].astype(F32)
    feat_ref[...] = (self_ref[...] + total).astype(BF)
    hubs = hub_sum[...]
    shape = (2 * HUB_ROWS, HUB_ROWS)
    target = lax.broadcasted_iota(jnp.int32, shape, 0)
    source = lax.broadcasted_iota(jnp.int32, shape, 1)
    spread = [
        dot((target == 2 * source + q).astype(F32), hubs[:, q * 64 : (q + 1) * 64], precision=lax.Precision.HIGHEST)
        for q in range(2)
    ]
    hub_ref[...] = spread[0] + spread[1]
    arrived = {0: first, 7: up1, 6: up2, 5: up3, 1: down1, 2: down2, 3: down3}
    for step in range(NZ):
        if step == 4:
            w_scr[(z + step) % NZ] = up4[HALF:]
        else:
            w_scr[(z + step) % NZ] = arrived[step][BLOCK:]
    weight = w_scr[0].astype(F32)
    for step in range(1, NZ):
        weight = weight + w_scr[step].astype(F32)
    gself_ref[...] = jnp.concatenate([weight[0:64], weight[64:128]], 1)
    gnbr_ref[...] = jnp.concatenate([weight[128:192], weight[192:256]], 1)


def body(features, hub_feats, nbr_owner, nbr_row, hub_ids, w_self, w_nbr, grad_out):
    place = jnp.stack([lax.axis_index(a) for a in ("y", "z", "c", "x")]).astype(jnp.int32)
    ids, mine, fg = call(
        prepare_kernel,
        (pltpu.VMEM((16, V), jnp.int32), pltpu.VMEM((BLOCK, COLS), BF), pltpu.VMEM((V, COLS), BF)),
        (place, features, grad_out, hub_feats, nbr_owner.reshape(8, 1, V), nbr_row, hub_ids.T),
        "prepare",
        scratch=[
            pltpu.VMEM((8, 1, V), jnp.int32),
            pltpu.VMEM((8, V), jnp.int32),
            pltpu.VMEM((4, V), jnp.int32),
            pltpu.VMEM((2 * HUB_ROWS, 256), BF),
            pltpu.SemaphoreType.DMA((7,)),
        ],
        far=6,
        mib=56,
    )

    pair = jnp.stack([ids, swap(ids, "c", NC, 1)])
    t1, t7 = shift(mine, "z", NZ, -1), shift(mine, "z", NZ, 1)
    fg1 = swap(fg, "x", NX, 1)
    pairs = [swap(pair, "y", NY, m) for m in range(1, NY)]
    counts0, ahead, behind, skip, both, token = call(
        near_counts_kernel,
        (
            pltpu.VMEM((NC, ROWS, V), BF),
            shaped((2 * BLOCK, COLS), BF),
            shaped((2 * BLOCK, COLS), BF),
            shaped((BLOCK, COLS), BF),
            shaped((2 * V, COLS), BF),
            shaped((8, 128), jnp.int32),
        ),
        (place, pair, mine, t1, t7, fg, fg1),
        "near_counts",
        flops=1 << 32,
        mib=8,
    )
    t23, t65, t4 = shift(ahead, "z", NZ, -2), shift(behind, "z", NZ, 2), shift(skip, "z", NZ, -3)
    fg23 = swap(both, "x", NX, 2)
    counts = call(
        far_counts_kernel,
        pltpu.VMEM((NC * (NY - 1), ROWS, V), BF),
        (place, token, *pairs),
        "far_counts",
        flops=3 << 32,
        mib=8,
    )
    t23, t65, t4, fg23 = lax.optimization_barrier((t23, t65, t4, fg23))

    far, turned = call(
        far_sums_kernel,
        (shaped((NY, COLS, V), BF), shaped((COLS, ROWS), BF)),
        (place, counts0, counts, mine, t1, t7, t23, t65, t4),
        "far_sums",
        scratch=[pltpu.VMEM((ROWS, COLS), BF)],
        flops=1 << 31,
    )
    got = swap(far, "c", NC, 1)
    near = call(
        near_sums_kernel,
        shaped((NY, COLS, V), F32),
        (place, counts0, counts, turned),
        "near_sums",
        flops=1 << 31,
    )
    both = near + got.astype(F32)
    total = both[0]
    for m in range(1, NY):
        total = total + swap(both[m].astype(BF), "y", NY, m).astype(F32)
    total = total.astype(BF)
    sums = [total] + [swap(total, "x", NX, m) for m in range(1, NX)]

    outputs, message, self_term = call(
        dense_kernel,
        (shaped((HALF, COLS), BF), shaped((V + WROWS, COLS), BF), shaped((HALF, COLS), F32)),
        (place, fg, fg1, fg23, *sums, w_self, w_nbr),
        "dense",
        scratch=[
            pltpu.VMEM((4, HALF, COLS), BF),
            pltpu.VMEM((4, HALF, COLS), BF),
            pltpu.VMEM((4, COLS, V), BF),
            pltpu.VMEM((4, HALF, COLS), BF),
            pltpu.VMEM((2, 256, 256), F32),
        ],
        flops=1 << 30,
    )

    messages = [message] + [swap(message, "y", NY, m) for m in range(1, NY)]
    other = swap(message, "c", NC, 1)
    grads_shape = shaped((NZ + 1, HALF, COLS), F32)
    own_grads = call(own_grads_kernel, grads_shape, (place, counts0, message), "own_grads", flops=1 << 29)
    *arrived, own_grads = lax.optimization_barrier((*messages[1:], own_grads))
    messages = [message, *arrived]
    others = [other] + [swap(m, "c", NC, 1) for m in arrived]
    near_grads = call(
        near_grads_kernel,
        grads_shape,
        (place, counts, *messages[1:], own_grads),
        "near_grads",
        flops=3 << 29,
    )
    hop_shapes = (shaped((BLOCK + WROWS, COLS), BF),) * 2
    hub_shape = shaped((HUB_ROWS, COLS), F32)
    up0, down0, hubs, hub4 = call(
        first_grads_kernel,
        (*hop_shapes, shaped((NZ, HUB_ROWS, COLS), F32), hub_shape),
        (place, counts0, counts, *messages, *others, near_grads),
        "first_grads",
        flops=1 << 29,
    )
    up1, down1 = shift(up0, "z", NZ, 1), shift(down0, "z", NZ, -1)
    hub4 = shift(hub4, "z", NZ, 4)
    rest = call(
        rest_grads_kernel,
        shaped((len(REST), HALF, COLS), F32),
        (place, counts0, counts, *others, near_grads),
        "rest_grads",
        flops=1 << 30,
    )
    ups, downs = [up1], [down1]
    for deltas in (((3, 2), (6, 6)), ((2, 1), (7, 7))):
        up, down = call(
            functools.partial(hop_kernel, deltas=deltas),
            hop_shapes,
            (place, ups[-1], downs[-1], rest, hubs),
            "hop",
        )
        ups.append(shift(up, "z", NZ, 1))
        downs.append(shift(down, "z", NZ, -1))
        if len(ups) == 2:
            ups[1], downs[1], hub4 = lax.optimization_barrier((ups[1], downs[1], hub4))
    up, hub_sum = call(
        last_hop_kernel,
        (shaped((HALF + WROWS, COLS), BF), hub_shape),
        (place, ups[-1], downs[-1], rest, hubs, hub4),
        "last_hop",
    )
    ups.append(shift(up, "z", NZ, 1))
    hub_sum = lax.ppermute(hub_sum, "x", [(0, 0), (1, 2), (2, 1), (3, 3)])
    grad_features, hub_rows, grad_self, grad_nbr = call(
        final_kernel,
        (
            shaped((HALF, COLS), BF),
            shaped((2 * HUB_ROWS, 64), F32),
            shaped((64, 256), F32),
            shaped((64, 256), F32),
        ),
        (place, self_term, rest, up0, *ups, *downs, hub_sum),
        "last_sums",
        scratch=[pltpu.VMEM((NZ, WROWS, COLS), BF)],
    )
    return outputs, grad_features, hub_rows, grad_self, grad_nbr


def solution(mesh):
    fine = Mesh(mesh.devices.reshape(NY, NZ, NC, NX), ("y", "z", "c", "x"))
    dom = ("y", "z", "c")
    in_specs = (
        P(dom, "x"),
        P(dom, None),
        P(None, dom, None),
        P(None, dom),
        P(dom, None),
        P(),
        P(),
        P(dom, "x"),
    )
    out_specs = (P(dom, "x"), P(dom, "x"), P(dom, "x"), P("x", None), P("x", None))
    return jax.shard_map(body, mesh=fine, in_specs=in_specs, out_specs=out_specs, check_vma=False)
```

```python
import functools

import jax
import jax.numpy as jnp
from jax import lax
from jax.experimental import pallas as pl
from jax.experimental.pallas import tpu as pltpu
from jax.sharding import Mesh, PartitionSpec as P

NY, NZ, NC, NX = 4, 8, 2, 4
V = 512
HALF = 256
COLS = 128
HUB_ROWS = 16
BLOCK = HALF + HUB_ROWS
ROWS = (NZ + 1) * HALF
PARTS = NC * NY
WROWS = 256
DISTINCT = 4
BF = jnp.bfloat16
F32 = jnp.float32
VM = pl.BlockSpec(memory_space=pltpu.VMEM)
PLAIN = (((1,), (0,)), ((), ()))
LAST = (((1,), (1,)), ((), ()))
FIRST = (((0,), (0,)), ((), ()))


def dot(a, b, dims=PLAIN, **kw):
    return lax.dot_general(a, b, dims, preferred_element_type=F32, **kw)


def shift(x, axis, size, step):
    return lax.ppermute(x, axis, [(i, (i + step) % size) for i in range(size)])


def swap(x, axis, size, mask):
    return lax.ppermute(x, axis, [(i, i ^ mask) for i in range(size)])


def call(kernel, outs, inputs, name, scratch=(), flops=0, mib=16, far=0, far_outs=0):
    out_specs = jax.tree.map(lambda _: VM, outs)
    if far_outs:
        out_specs = (*out_specs[:-far_outs], *[pl.BlockSpec(memory_space=pl.ANY)] * far_outs)
    return pl.pallas_call(
        kernel,
        out_shape=outs,
        in_specs=[VM] * (len(inputs) - far) + [pl.BlockSpec(memory_space=pl.ANY)] * far,
        out_specs=out_specs,
        scratch_shapes=list(scratch),
        compiler_params=pltpu.CompilerParams(vmem_limit_bytes=mib << 20),
        cost_estimate=pl.CostEstimate(flops=flops, bytes_accessed=1 << 18, transcendentals=0),
        name=name,
    )(*inputs)


def shaped(shape, dtype):
    return jax.ShapeDtypeStruct(shape, dtype)


def prepare_kernel(
    feat, cot, hub, owner, row, hub_id, ids_ref, mine_ref, both,
    owner_scr, row_scr, hub_id_scr, hub_scr, sems,
):
    parity, half = lax.axis_index("x") // 2, lax.axis_index("x") % 2
    copies = [
        pltpu.make_async_copy(source, target, sems.at[index])
        for index, (source, target) in enumerate(
            (
                (owner, owner_scr),
                (row, row_scr),
                (hub_id, hub_id_scr),
                (hub, hub_scr),
                (feat, mine_ref.at[pl.ds(0, HALF)]),
                (feat, both.at[pl.ds(0, HALF)]),
                (cot, both.at[pl.ds(HALF, HALF)]),
                (feat, both.at[pl.ds(V, HALF)]),
                (cot, both.at[pl.ds(V + HALF, HALF)]),
            )
        )
    ]
    for copy in copies:
        copy.start()
    for copy in copies[:5]:
        copy.wait()
    ids_ref[0:8] = owner_scr[...].reshape(8, V) * V + row_scr[...]
    ids_ref[8:12] = hub_id_scr[...]
    ids_ref[12:16] = jnp.full((4, V), -1, jnp.int32)
    pick = lax.broadcasted_iota(jnp.int32, (HUB_ROWS, 2 * HUB_ROWS), 1) == (
        2 * lax.broadcasted_iota(jnp.int32, (HUB_ROWS, 2 * HUB_ROWS), 0) + parity
    )
    columns = hub_scr[:, pl.ds(pl.multiple_of(half * COLS, COLS), COLS)]
    mine_ref[HALF:BLOCK] = dot(pick.astype(F32).astype(BF), columns).astype(BF)
    for copy in copies[5:]:
        copy.wait()


def counts_kernel(ids0, ids1, ids2, ids3, out_ref):
    y, z, c, x = (lax.axis_index(a) for a in ("y", "z", "c", "x"))
    parity = x // 2
    rows = lax.broadcasted_iota(jnp.int32, (16, 16, 128), 0) * 16 + lax.broadcasted_iota(
        jnp.int32, (16, 16, 128), 1
    )
    rows = rows.astype(F32).astype(BF)
    level = lax.broadcasted_iota(jnp.int32, (8, V), 0)
    column = y * (NZ * NC) + c
    mask = (NY - 1) * (NZ * NC) + (NC - 1)

    def allmax(a):
        for s in (4, 2, 1):
            a = jnp.maximum(a, pltpu.roll(a, s, 0))
        return a

    def allsum(a):
        for s in (4, 2, 1):
            a = a + pltpu.roll(a, s, 0)
        return a

    def extract(keys):
        top = allmax(keys)
        hit = keys == top
        return jnp.where(hit, -1.0, keys), top, allsum(jnp.where(hit, 1.0, 0.0))

    def pair(a):
        return jnp.concatenate([a, a], 0).astype(BF)

    for dy, ids_ref in enumerate((ids0, ids1, ids2, ids3)):

        def part(dc, carry, dy=dy, ids_ref=ids_ref):
            index = dc * NY + dy
            ids = ids_ref[dc]
            flat, hub = ids[0:8], ids[8:16]
            here = ((flat >> 9) & mask) == column
            here = here & ((flat & 1) == parity)
            keys = jnp.where(here, (((flat >> 10) - z) & 7) * HALF + ((flat >> 1) & 255), -1).astype(F32)
            here = (((hub >> 5) & mask) == column) & (level < 4)
            hub_row = (((hub >> 6) - z) & 7) * 32 + ((hub & 1) ^ parity) * 16 + ((hub >> 1) & 15)
            hub_keys = jnp.where(here, hub_row, -1).astype(F32)
            found, hub_found = [], []
            for _ in range(DISTINCT):
                keys, top, times = extract(keys)
                found.append((top, pair(times)))
            for _ in range(4):
                hub_keys, top, times = extract(hub_keys)
                hub_found.append((pair(top), pair(times)))
            for tile in range(V // 128):
                lanes = slice(tile * 128, (tile + 1) * 128)
                for delta in range(NZ):
                    block = jnp.zeros((16, 16, 128), BF)
                    for top, times in found:
                        match = pair(top[:, lanes] - float(HALF * delta))[None] == rows
                        block = jnp.where(match, times[:, lanes][None], block)
                    out_ref[index, delta * HALF : (delta + 1) * HALF, lanes] = block.reshape(HALF, 128)
                block = jnp.zeros((16, 16, 128), BF)
                for top, times in hub_found:
                    block = jnp.where(top[:, lanes][None] == rows, times[:, lanes][None], block)
                out_ref[index, NZ * HALF : ROWS, lanes] = block.reshape(HALF, 128)

            @pl.when(jnp.max(keys) >= 0)
            def _():
                def more(_, keys):
                    keys, top, times = extract(keys)
                    for tile in range(V // 128):
                        lanes = slice(tile * 128, (tile + 1) * 128)
                        for delta in range(NZ):
                            span = slice(delta * HALF, (delta + 1) * HALF)
                            block = out_ref[index, span, lanes].reshape(16, 16, 128)
                            match = pair(top[:, lanes] - float(HALF * delta))[None] == rows
                            block = jnp.where(match, pair(times[:, lanes])[None], block)
                            out_ref[index, span, lanes] = block.reshape(HALF, 128)
                    return keys

                lax.fori_loop(0, 8 - DISTINCT, more, keys)

            return carry

        lax.fori_loop(0, NC, part, 0)


def far_sums_kernel(counts, t0, t1, t2, t7, t34, t65, sums_ref, turned_ref, table):
    blocks = {0: t0[...], 1: t1[...], 2: t2[...], 7: t7[...]}
    blocks[3], blocks[4] = t34[0:BLOCK], t34[BLOCK : 2 * BLOCK]
    blocks[6], blocks[5] = t65[0:BLOCK], t65[BLOCK : 2 * BLOCK]
    for delta in range(NZ):
        table[delta * HALF : (delta + 1) * HALF] = blocks[delta][0:HALF]
        start = NZ * HALF + delta * 2 * HUB_ROWS
        table[start : start + HUB_ROWS] = blocks[delta][HALF:BLOCK]
        table[start + HUB_ROWS : start + 2 * HUB_ROWS] = jnp.zeros((HUB_ROWS, COLS), BF)
    turned_ref[...] = table[...].T

    def step(dy, carry):
        sums_ref[dy] = dot(turned_ref[...], counts[NY + dy]).astype(BF)
        return carry

    lax.fori_loop(0, NY, step, 0)


def near_sums_kernel(counts, turned, sums_ref):
    def step(dy, carry):
        sums_ref[dy] = dot(turned[...], counts[dy])
        return carry

    lax.fori_loop(0, NY, step, 0)


def arrange_kernel(fg, ws_ref, feat_ref, cot_ref, pre_ref):
    for start, ref in ((0, feat_ref), (HALF, cot_ref)):
        quarters = [fg[q, start : start + HALF] for q in range(NX)]
        ref[...] = jnp.concatenate(
            [jnp.concatenate(quarters[0:2], 1), jnp.concatenate(quarters[2:4], 1)], 0
        )
    pre_ref[...] = dot(feat_ref[...], ws_ref[...])


def dense_kernel(
    feat_ref, cot_ref, pre_ref, s0, s1, s2, s3, ws_ref, wn_ref,
    out_ref, message_ref, self_ref,
    s_scr, o_scr, w_scr,
):
    x = lax.axis_index("x")
    parity, half = x // 2, x % 2
    for mask, ref in enumerate((s0, s1, s2, s3)):
        s_scr[x ^ mask] = ref[...]
    mean_t = jnp.concatenate(
        [
            s_scr[0].astype(F32) + s_scr[2].astype(F32),
            s_scr[1].astype(F32) + s_scr[3].astype(F32),
        ],
        0,
    )
    mean_t = (mean_t / 12.0).astype(BF)
    ordered = lax.broadcasted_iota(jnp.int32, (V, V), 0)
    natural = lax.broadcasted_iota(jnp.int32, (V, V), 1)
    order = ((ordered % HALF) * 2 + ordered // HALF == natural).astype(F32).astype(BF)
    mean = dot(order, mean_t, LAST).astype(BF)
    pre = pre_ref[...] + dot(mean, wn_ref[...])
    sig = jax.nn.sigmoid(pre)
    value = (pre * sig).astype(BF)
    grad_pre = (cot_ref[...].astype(F32) * sig * (1.0 + pre * (1.0 - sig))).astype(BF)
    for q in range(2):
        for h in range(2):
            o_scr[q * 2 + h] = value[q * HALF : (q + 1) * HALF, h * COLS : (h + 1) * COLS]
    out_ref[...] = o_scr[x]
    rows = pl.ds(pl.multiple_of(half * COLS, COLS), COLS)
    grad_mean = (dot(grad_pre, wn_ref[rows, :], LAST) / 12.0).astype(BF)
    message_ref[0:V] = dot(order, grad_mean, FIRST).astype(BF)
    own_self = dot(grad_pre, ws_ref[rows, :], LAST)
    self_ref[...] = jnp.where(parity == 0, own_self[0:HALF], own_self[HALF:V])
    w_scr[0] = dot(feat_ref[...], grad_pre, FIRST)
    w_scr[1] = dot(mean, grad_pre, FIRST)
    quarter = pl.ds(pl.multiple_of(x * 64, 64), 64)
    for which in range(2):
        part = w_scr[which, quarter, :]
        for h in range(2):
            start = V + which * 128 + h * 64
            message_ref[start : start + 64, :] = part[:, h * COLS : (h + 1) * COLS].astype(BF)


def block_sum(counts, base, messages, block, total=None):
    span = slice(block * HALF, (block + 1) * HALF)
    for dy, ref in enumerate(messages):
        term = dot(counts[base + dy, span], ref[0:V])
        total = term if total is None else total + term
    return total


FIRST_BLOCKS = (4, 5, NZ)
REST = (0, 1, 2, 3, 6, 7)


def near_grads_kernel(counts, m0, m1, m2, m3, out_ref):
    for index, block in enumerate(FIRST_BLOCKS):
        out_ref[index] = block_sum(counts, 0, (m0, m1, m2, m3), block)


def first_grads_kernel(
    counts, m0, m1, m2, m3, o0, o1, o2, o3, near, up_ref, down_ref, hub_ref
):
    parity = lax.axis_index("x") // 2
    others = (o0, o1, o2, o3)
    blocks = [block_sum(counts, NY, others, block, near[index]) for index, block in enumerate(FIRST_BLOCKS)]
    hubs = blocks[2]
    lane = lax.broadcasted_iota(jnp.int32, (HUB_ROWS, COLS), 1)
    low = (lane < 64) == (parity == 0)
    for delta in range(NZ):
        start = delta * 2 * HUB_ROWS
        mine = hubs[start : start + HUB_ROWS]
        rest = pltpu.roll(hubs[start + HUB_ROWS : start + 2 * HUB_ROWS], 64, 1)
        hub_ref[delta] = jnp.where(low, mine, rest)
    tail = slice(V, V + WROWS)
    sums = [
        (a[tail].astype(F32) + b[tail].astype(F32)) + (c[tail].astype(F32) + d[tail].astype(F32))
        for a, b, c, d in ((m0, m1, m2, m3), others)
    ]
    weight = (sums[0] + sums[1]).astype(BF)
    for index, ref in enumerate((up_ref, down_ref)):
        ref[0:HALF] = blocks[index].astype(BF)
        ref[HALF:BLOCK] = hub_ref[FIRST_BLOCKS[index]].astype(BF)
        ref[BLOCK:] = weight


def rest_grads_kernel(counts, m0, m1, m2, m3, o0, o1, o2, o3, out_ref):
    for index, block in enumerate(REST):
        out_ref[index] = block_sum(counts, 0, (m0, m1, m2, m3, o0, o1, o2, o3), block)


def hop_kernel(up, down, rest, hubs, next_up, next_down, *, deltas):
    for delta, got, ref in zip(deltas, (up, down), (next_up, next_down)):
        ref[0:HALF] = (got[0:HALF].astype(F32) + rest[REST.index(delta)]).astype(BF)
        ref[HALF:BLOCK] = (got[HALF:BLOCK].astype(F32) + hubs[delta]).astype(BF)
        ref[BLOCK:] = got[BLOCK:]


def last_hop_kernel(up, down, rest, hubs, next_up, hub_up, hub_here):
    next_up[0:HALF] = (up[0:HALF].astype(F32) + rest[REST.index(1)]).astype(BF)
    next_up[HALF:] = up[BLOCK:]
    hub_up[...] = up[HALF:BLOCK].astype(F32) + hubs[1]
    hub_here[...] = down[HALF:BLOCK].astype(F32) + hubs[0]


def final_kernel(
    self_ref, rest, first, up1, up2, up3, up4, down1, down2, down3, hub_up, hub_here,
    feat_ref, hub_ref, gself_ref, gnbr_ref, w_scr,
):
    z = lax.axis_index("z")
    total = rest[0] + up4[0:HALF].astype(F32) + down3[0:HALF].astype(F32)
    feat_ref[...] = (self_ref[...] + total).astype(BF)
    hubs = hub_up[...] + hub_here[...]
    shape = (2 * HUB_ROWS, HUB_ROWS)
    target = lax.broadcasted_iota(jnp.int32, shape, 0)
    source = lax.broadcasted_iota(jnp.int32, shape, 1)
    spread = [
        dot((target == 2 * source + q).astype(F32), hubs[:, q * 64 : (q + 1) * 64], precision=lax.Precision.HIGHEST)
        for q in range(2)
    ]
    hub_ref[...] = spread[0] + spread[1]
    arrived = {0: first, 7: up1, 6: up2, 5: up3, 1: down1, 2: down2, 3: down3}
    for step in range(NZ):
        if step == 4:
            w_scr[(z + step) % NZ] = up4[HALF:]
        else:
            w_scr[(z + step) % NZ] = arrived[step][BLOCK:]
    weight = w_scr[0].astype(F32)
    for step in range(1, NZ):
        weight = weight + w_scr[step].astype(F32)
    gself_ref[...] = jnp.concatenate([weight[0:64], weight[64:128]], 1)
    gnbr_ref[...] = jnp.concatenate([weight[128:192], weight[192:256]], 1)


def body(features, hub_feats, nbr_owner, nbr_row, hub_ids, w_self, w_nbr, grad_out):
    ids, mine, fg = call(
        prepare_kernel,
        (pltpu.VMEM((16, V), jnp.int32), pltpu.VMEM((BLOCK, COLS), BF), shaped((2 * V, COLS), BF)),
        (features, grad_out, hub_feats, nbr_owner.reshape(8, 1, V), nbr_row, hub_ids.T),
        "prepare",
        scratch=[
            pltpu.VMEM((8, 1, V), jnp.int32),
            pltpu.VMEM((8, V), jnp.int32),
            pltpu.VMEM((4, V), jnp.int32),
            pltpu.VMEM((2 * HUB_ROWS, 256), BF),
            pltpu.SemaphoreType.DMA((9,)),
        ],
        far=6,
        far_outs=1,
        mib=56,
    )

    everything = lax.all_gather(fg, "x", axis=0)

    pair = jnp.stack([ids, swap(ids, "c", NC, 1)])
    t1, t7, t2 = shift(mine, "z", NZ, -1), shift(mine, "z", NZ, 1), shift(mine, "z", NZ, -2)
    pairs = [pair] + [swap(pair, "y", NY, m) for m in range(1, NY)]
    t34 = shift(jnp.concatenate([t1, t2], 0), "z", NZ, -2)
    t65 = shift(jnp.concatenate([mine, t7], 0), "z", NZ, 2)
    counts = call(
        counts_kernel,
        pltpu.VMEM((PARTS, ROWS, V), BF),
        (*pairs,),
        "counts",
        flops=1 << 34,
        mib=8,
    )

    far, turned = call(
        far_sums_kernel,
        (shaped((NY, COLS, V), BF), shaped((COLS, ROWS), BF)),
        (counts, mine, t1, t2, t7, t34, t65),
        "far_sums",
        scratch=[pltpu.VMEM((ROWS, COLS), BF)],
        flops=1 << 31,
    )
    got = swap(far, "c", NC, 1)
    near = call(
        near_sums_kernel, shaped((NY, COLS, V), F32), (counts, turned), "near_sums", flops=1 << 31
    )
    both = near + got.astype(F32)
    total = both[0]
    for m in range(1, NY):
        total = total + swap(both[m].astype(BF), "y", NY, m).astype(F32)
    total = total.astype(BF)
    sums = [total] + [swap(total, "x", NX, m) for m in range(1, NX)]

    feats, cots, base = call(
        arrange_kernel,
        (shaped((V, 256), BF), shaped((V, 256), BF), shaped((V, 256), F32)),
        (everything, w_self),
        "arrange",
        flops=1 << 28,
    )
    outputs, message, self_term = call(
        dense_kernel,
        (shaped((HALF, COLS), BF), shaped((V + WROWS, COLS), BF), shaped((HALF, COLS), F32)),
        (feats, cots, base, *sums, w_self, w_nbr),
        "dense",
        scratch=[
            pltpu.VMEM((4, COLS, V), BF),
            pltpu.VMEM((4, HALF, COLS), BF),
            pltpu.VMEM((2, 256, 256), F32),
        ],
        flops=1 << 30,
    )

    messages = [message] + [swap(message, "y", NY, m) for m in range(1, NY)]
    others = [swap(m, "c", NC, 1) for m in messages]
    near_grads = call(
        near_grads_kernel,
        shaped((len(FIRST_BLOCKS), HALF, COLS), F32),
        (counts, *messages),
        "near_grads",
        flops=1 << 30,
    )
    hop_shapes = (shaped((BLOCK + WROWS, COLS), BF),) * 2
    up0, down0, hubs = call(
        first_grads_kernel,
        (*hop_shapes, shaped((NZ, HUB_ROWS, COLS), F32)),
        (counts, *messages, *others, near_grads),
        "first_grads",
        flops=1 << 30,
    )
    up1, down1 = shift(up0, "z", NZ, 1), shift(down0, "z", NZ, -1)
    rest = call(
        rest_grads_kernel,
        shaped((len(REST), HALF, COLS), F32),
        (counts, *messages, *others),
        "rest_grads",
        flops=1 << 31,
    )
    ups, downs = [up1], [down1]
    for deltas in ((3, 6), (2, 7)):
        up, down = call(
            functools.partial(hop_kernel, deltas=deltas),
            hop_shapes,
            (ups[-1], downs[-1], rest, hubs),
            "hop",
        )
        ups.append(shift(up, "z", NZ, 1))
        downs.append(shift(down, "z", NZ, -1))
    up, hub_up, hub_here = call(
        last_hop_kernel,
        (
            shaped((HALF + WROWS, COLS), BF),
            shaped((HUB_ROWS, COLS), F32),
            shaped((HUB_ROWS, COLS), F32),
        ),
        (ups[-1], downs[-1], rest, hubs),
        "last_hop",
    )
    ups.append(shift(up, "z", NZ, 1))
    turn = (0, 2, 1, 3)
    cross = [(z * NX + x, (z + 1) % NZ * NX + turn[x]) for z in range(NZ) for x in range(NX)]
    hub_up = lax.ppermute(hub_up, ("z", "x"), cross)
    hub_here = lax.ppermute(hub_here, "x", [(x, turn[x]) for x in range(NX)])
    grad_features, hub_rows, grad_self, grad_nbr = call(
        final_kernel,
        (
            shaped((HALF, COLS), BF),
            shaped((2 * HUB_ROWS, 64), F32),
            shaped((64, 256), F32),
            shaped((64, 256), F32),
        ),
        (self_term, rest, up0, *ups, *downs, hub_up, hub_here),
        "last_sums",
        scratch=[pltpu.VMEM((NZ, WROWS, COLS), BF)],
    )
    return outputs, grad_features, hub_rows, grad_self, grad_nbr


def solution(mesh):
    fine = Mesh(mesh.devices.reshape(NY, NZ, NC, NX), ("y", "z", "c", "x"))
    dom = ("y", "z", "c")
    in_specs = (
        P(dom, "x"),
        P(dom, None),
        P(None, dom, None),
        P(None, dom),
        P(dom, None),
        P(),
        P(),
        P(dom, "x"),
    )
    out_specs = (P(dom, "x"), P(dom, "x"), P(dom, "x"), P("x", None), P("x", None))
    return jax.shard_map(body, mesh=fine, in_specs=in_specs, out_specs=out_specs, check_vma=False)
```

```python
import functools

import jax
import jax.numpy as jnp
from jax import lax
from jax.experimental import pallas as pl
from jax.experimental.pallas import tpu as pltpu
from jax.sharding import Mesh, PartitionSpec as P

NY, NZ, NC, NX = 4, 8, 2, 4
V = 512
HALF = 256
COLS = 128
HUB_ROWS = 16
BLOCK = HALF + HUB_ROWS
ROWS = (NZ + 1) * HALF
PARTS = NC * NY
WROWS = 256
DISTINCT = 4
BF = jnp.bfloat16
F32 = jnp.float32
VM = pl.BlockSpec(memory_space=pltpu.VMEM)
PLAIN = (((1,), (0,)), ((), ()))
LAST = (((1,), (1,)), ((), ()))
FIRST = (((0,), (0,)), ((), ()))


def dot(a, b, dims=PLAIN, **kw):
    return lax.dot_general(a, b, dims, preferred_element_type=F32, **kw)


def shift(x, axis, size, step):
    return lax.ppermute(x, axis, [(i, (i + step) % size) for i in range(size)])


def swap(x, axis, size, mask):
    return lax.ppermute(x, axis, [(i, i ^ mask) for i in range(size)])


def call(kernel, outs, inputs, name, scratch=(), flops=0, mib=16, far=0):
    return pl.pallas_call(
        kernel,
        out_shape=outs,
        in_specs=[VM] * (len(inputs) - far) + [pl.BlockSpec(memory_space=pl.ANY)] * far,
        out_specs=jax.tree.map(lambda _: VM, outs),
        scratch_shapes=list(scratch),
        compiler_params=pltpu.CompilerParams(vmem_limit_bytes=mib << 20),
        cost_estimate=pl.CostEstimate(flops=flops, bytes_accessed=1 << 18, transcendentals=0),
        name=name,
    )(*inputs)


def shaped(shape, dtype):
    return jax.ShapeDtypeStruct(shape, dtype)


def prepare_kernel(
    feat, cot, hub, owner, row, hub_id, ids_ref, mine_ref, both,
    owner_scr, row_scr, hub_id_scr, hub_scr, sems,
):
    parity, half = lax.axis_index("x") // 2, lax.axis_index("x") % 2
    pairs = (
        (owner, owner_scr),
        (row, row_scr),
        (hub_id, hub_id_scr),
        (hub, hub_scr),
        (feat, mine_ref.at[pl.ds(0, HALF)]),
        (feat, both.at[pl.ds(0, HALF)]),
        (cot, both.at[pl.ds(HALF, HALF)]),
    )
    copies = [pltpu.make_async_copy(a, b, sems.at[i]) for i, (a, b) in enumerate(pairs)]
    for copy in copies:
        copy.start()
    for copy in copies:
        copy.wait()
    ids_ref[0:8] = owner_scr[...].reshape(8, V) * V + row_scr[...]
    ids_ref[8:12] = hub_id_scr[...]
    ids_ref[12:16] = jnp.full((4, V), -1, jnp.int32)
    pick = lax.broadcasted_iota(jnp.int32, (HUB_ROWS, 2 * HUB_ROWS), 1) == (
        2 * lax.broadcasted_iota(jnp.int32, (HUB_ROWS, 2 * HUB_ROWS), 0) + parity
    )
    columns = hub_scr[:, pl.ds(pl.multiple_of(half * COLS, COLS), COLS)]
    mine_ref[HALF:BLOCK] = dot(pick.astype(F32).astype(BF), columns).astype(BF)


def counts_kernel(ids0, ids1, ids2, ids3, out_ref):
    y, z, c, x = (lax.axis_index(a) for a in ("y", "z", "c", "x"))
    parity = x // 2
    rows = lax.broadcasted_iota(jnp.int32, (16, 16, 128), 0) * 16 + lax.broadcasted_iota(
        jnp.int32, (16, 16, 128), 1
    )
    rows = rows.astype(F32).astype(BF)
    level = lax.broadcasted_iota(jnp.int32, (8, V), 0)
    column = y * (NZ * NC) + c
    mask = (NY - 1) * (NZ * NC) + (NC - 1)

    def allmax(a):
        for s in (4, 2, 1):
            a = jnp.maximum(a, pltpu.roll(a, s, 0))
        return a

    def allsum(a):
        for s in (4, 2, 1):
            a = a + pltpu.roll(a, s, 0)
        return a

    def extract(keys):
        top = allmax(keys)
        hit = keys == top
        return jnp.where(hit, -1.0, keys), top, allsum(jnp.where(hit, 1.0, 0.0))

    def pair(a):
        return jnp.concatenate([a, a], 0).astype(BF)

    for dy, ids_ref in enumerate((ids0, ids1, ids2, ids3)):

        def part(dc, carry, dy=dy, ids_ref=ids_ref):
            index = dc * NY + dy
            ids = ids_ref[dc]
            flat, hub = ids[0:8], ids[8:16]
            here = ((flat >> 9) & mask) == column
            here = here & ((flat & 1) == parity)
            keys = jnp.where(here, (((flat >> 10) - z) & 7) * HALF + ((flat >> 1) & 255), -1).astype(F32)
            here = (((hub >> 5) & mask) == column) & (level < 4)
            hub_row = (((hub >> 6) - z) & 7) * 32 + ((hub & 1) ^ parity) * 16 + ((hub >> 1) & 15)
            hub_keys = jnp.where(here, hub_row, -1).astype(F32)
            found, hub_found = [], []
            for _ in range(DISTINCT):
                keys, top, times = extract(keys)
                found.append((top, pair(times)))
            for _ in range(4):
                hub_keys, top, times = extract(hub_keys)
                hub_found.append((pair(top), pair(times)))
            for tile in range(V // 128):
                lanes = slice(tile * 128, (tile + 1) * 128)
                for delta in range(NZ):
                    block = jnp.zeros((16, 16, 128), BF)
                    for top, times in found:
                        match = pair(top[:, lanes] - float(HALF * delta))[None] == rows
                        block = jnp.where(match, times[:, lanes][None], block)
                    out_ref[index, delta * HALF : (delta + 1) * HALF, lanes] = block.reshape(HALF, 128)
                block = jnp.zeros((16, 16, 128), BF)
                for top, times in hub_found:
                    block = jnp.where(top[:, lanes][None] == rows, times[:, lanes][None], block)
                out_ref[index, NZ * HALF : ROWS, lanes] = block.reshape(HALF, 128)

            @pl.when(jnp.max(keys) >= 0)
            def _():
                def more(_, keys):
                    keys, top, times = extract(keys)
                    for tile in range(V // 128):
                        lanes = slice(tile * 128, (tile + 1) * 128)
                        for delta in range(NZ):
                            span = slice(delta * HALF, (delta + 1) * HALF)
                            block = out_ref[index, span, lanes].reshape(16, 16, 128)
                            match = pair(top[:, lanes] - float(HALF * delta))[None] == rows
                            block = jnp.where(match, pair(times[:, lanes])[None], block)
                            out_ref[index, span, lanes] = block.reshape(HALF, 128)
                    return keys

                lax.fori_loop(0, 8 - DISTINCT, more, keys)

            return carry

        lax.fori_loop(0, NC, part, 0)


def far_sums_kernel(counts, t0, t1, t2, t7, t34, t65, sums_ref, turned_ref, table):
    blocks = {0: t0[...], 1: t1[...], 2: t2[...], 7: t7[...]}
    blocks[3], blocks[4] = t34[0:BLOCK], t34[BLOCK : 2 * BLOCK]
    blocks[6], blocks[5] = t65[0:BLOCK], t65[BLOCK : 2 * BLOCK]
    for delta in range(NZ):
        table[delta * HALF : (delta + 1) * HALF] = blocks[delta][0:HALF]
        start = NZ * HALF + delta * 2 * HUB_ROWS
        table[start : start + HUB_ROWS] = blocks[delta][HALF:BLOCK]
        table[start + HUB_ROWS : start + 2 * HUB_ROWS] = jnp.zeros((HUB_ROWS, COLS), BF)
    turned_ref[...] = table[...].T

    def step(dy, carry):
        sums_ref[dy] = dot(turned_ref[...], counts[NY + dy]).astype(BF)
        return carry

    lax.fori_loop(0, NY, step, 0)


def near_sums_kernel(counts, turned, sums_ref):
    def step(dy, carry):
        sums_ref[dy] = dot(turned[...], counts[dy])
        return carry

    lax.fori_loop(0, NY, step, 0)


def arrange_kernel(fg0, fg1, fg23, ws_ref, feat_ref, cot_ref, pre_ref, scr):
    x = lax.axis_index("x")
    for mask, (ref, start) in enumerate(((fg0, 0), (fg1, 0), (fg23, 0), (fg23, V))):
        scr[x ^ mask] = ref[start : start + V]
    for start, ref in ((0, feat_ref), (HALF, cot_ref)):
        quarters = [scr[q, start : start + HALF] for q in range(NX)]
        ref[...] = jnp.concatenate(
            [jnp.concatenate(quarters[0:2], 1), jnp.concatenate(quarters[2:4], 1)], 0
        )
    pre_ref[...] = dot(feat_ref[...], ws_ref[...])


def dense_kernel(
    feat_ref, cot_ref, pre_ref, s0, s1, s2, s3, ws_ref, wn_ref,
    out_ref, message_ref, self_ref,
    s_scr, o_scr, w_scr,
):
    x = lax.axis_index("x")
    parity, half = x // 2, x % 2
    for mask, ref in enumerate((s0, s1, s2, s3)):
        s_scr[x ^ mask] = ref[...]
    mean_t = jnp.concatenate(
        [
            s_scr[0].astype(F32) + s_scr[2].astype(F32),
            s_scr[1].astype(F32) + s_scr[3].astype(F32),
        ],
        0,
    )
    mean_t = (mean_t / 12.0).astype(BF)
    ordered = lax.broadcasted_iota(jnp.int32, (V, V), 0)
    natural = lax.broadcasted_iota(jnp.int32, (V, V), 1)
    order = ((ordered % HALF) * 2 + ordered // HALF == natural).astype(F32).astype(BF)
    mean = dot(order, mean_t, LAST).astype(BF)
    pre = pre_ref[...] + dot(mean, wn_ref[...])
    sig = jax.nn.sigmoid(pre)
    value = (pre * sig).astype(BF)
    grad_pre = (cot_ref[...].astype(F32) * sig * (1.0 + pre * (1.0 - sig))).astype(BF)
    for q in range(2):
        for h in range(2):
            o_scr[q * 2 + h] = value[q * HALF : (q + 1) * HALF, h * COLS : (h + 1) * COLS]
    out_ref[...] = o_scr[x]
    rows = pl.ds(pl.multiple_of(half * COLS, COLS), COLS)
    grad_mean = (dot(grad_pre, wn_ref[rows, :], LAST) / 12.0).astype(BF)
    message_ref[0:V] = dot(order, grad_mean, FIRST).astype(BF)
    own_self = dot(grad_pre, ws_ref[rows, :], LAST)
    self_ref[...] = jnp.where(parity == 0, own_self[0:HALF], own_self[HALF:V])
    w_scr[0] = dot(feat_ref[...], grad_pre, FIRST)
    w_scr[1] = dot(mean, grad_pre, FIRST)
    quarter = pl.ds(pl.multiple_of(x * 64, 64), 64)
    for which in range(2):
        part = w_scr[which, quarter, :]
        for h in range(2):
            start = V + which * 128 + h * 64
            message_ref[start : start + 64, :] = part[:, h * COLS : (h + 1) * COLS].astype(BF)


def block_sum(counts, base, messages, block, total=None):
    span = slice(block * HALF, (block + 1) * HALF)
    for dy, ref in enumerate(messages):
        term = dot(counts[base + dy, span], ref[0:V])
        total = term if total is None else total + term
    return total


FIRST_BLOCKS = (4, 5, NZ)
REST = (0, 1, 2, 3, 6, 7)


def near_grads_kernel(counts, m0, m1, m2, m3, out_ref):
    for index, block in enumerate(FIRST_BLOCKS):
        out_ref[index] = block_sum(counts, 0, (m0, m1, m2, m3), block)


def first_grads_kernel(
    counts, m0, m1, m2, m3, o0, o1, o2, o3, near, up_ref, down_ref, hub_ref
):
    parity = lax.axis_index("x") // 2
    others = (o0, o1, o2, o3)
    blocks = [block_sum(counts, NY, others, block, near[index]) for index, block in enumerate(FIRST_BLOCKS)]
    hubs = blocks[2]
    lane = lax.broadcasted_iota(jnp.int32, (HUB_ROWS, COLS), 1)
    low = (lane < 64) == (parity == 0)
    for delta in range(NZ):
        start = delta * 2 * HUB_ROWS
        mine = hubs[start : start + HUB_ROWS]
        rest = pltpu.roll(hubs[start + HUB_ROWS : start + 2 * HUB_ROWS], 64, 1)
        hub_ref[delta] = jnp.where(low, mine, rest)
    tail = slice(V, V + WROWS)
    sums = [
        (a[tail].astype(F32) + b[tail].astype(F32)) + (c[tail].astype(F32) + d[tail].astype(F32))
        for a, b, c, d in ((m0, m1, m2, m3), others)
    ]
    weight = (sums[0] + sums[1]).astype(BF)
    for index, ref in enumerate((up_ref, down_ref)):
        ref[0:HALF] = blocks[index].astype(BF)
        ref[HALF:BLOCK] = hub_ref[FIRST_BLOCKS[index]].astype(BF)
        ref[BLOCK:] = weight


def rest_grads_kernel(counts, m0, m1, m2, m3, o0, o1, o2, o3, out_ref):
    for index, block in enumerate(REST):
        out_ref[index] = block_sum(counts, 0, (m0, m1, m2, m3, o0, o1, o2, o3), block)


def hop_kernel(up, down, rest, hubs, next_up, next_down, *, deltas):
    for delta, got, ref in zip(deltas, (up, down), (next_up, next_down)):
        ref[0:HALF] = (got[0:HALF].astype(F32) + rest[REST.index(delta)]).astype(BF)
        ref[HALF:BLOCK] = (got[HALF:BLOCK].astype(F32) + hubs[delta]).astype(BF)
        ref[BLOCK:] = got[BLOCK:]


def last_hop_kernel(up, down, rest, hubs, next_up, hub_up, hub_here):
    next_up[0:HALF] = (up[0:HALF].astype(F32) + rest[REST.index(1)]).astype(BF)
    next_up[HALF:] = up[BLOCK:]
    hub_up[...] = up[HALF:BLOCK].astype(F32) + hubs[1]
    hub_here[...] = down[HALF:BLOCK].astype(F32) + hubs[0]


def final_kernel(
    self_ref, rest, first, up1, up2, up3, up4, down1, down2, down3, hub_up, hub_here,
    feat_ref, hub_ref, gself_ref, gnbr_ref, w_scr,
):
    z = lax.axis_index("z")
    total = rest[0] + up4[0:HALF].astype(F32) + down3[0:HALF].astype(F32)
    feat_ref[...] = (self_ref[...] + total).astype(BF)
    hubs = hub_up[...] + hub_here[...]
    shape = (2 * HUB_ROWS, HUB_ROWS)
    target = lax.broadcasted_iota(jnp.int32, shape, 0)
    source = lax.broadcasted_iota(jnp.int32, shape, 1)
    spread = [
        dot((target == 2 * source + q).astype(F32), hubs[:, q * 64 : (q + 1) * 64], precision=lax.Precision.HIGHEST)
        for q in range(2)
    ]
    hub_ref[...] = spread[0] + spread[1]
    arrived = {0: first, 7: up1, 6: up2, 5: up3, 1: down1, 2: down2, 3: down3}
    for step in range(NZ):
        if step == 4:
            w_scr[(z + step) % NZ] = up4[HALF:]
        else:
            w_scr[(z + step) % NZ] = arrived[step][BLOCK:]
    weight = w_scr[0].astype(F32)
    for step in range(1, NZ):
        weight = weight + w_scr[step].astype(F32)
    gself_ref[...] = jnp.concatenate([weight[0:64], weight[64:128]], 1)
    gnbr_ref[...] = jnp.concatenate([weight[128:192], weight[192:256]], 1)


def body(features, hub_feats, nbr_owner, nbr_row, hub_ids, w_self, w_nbr, grad_out):
    ids, mine, fg = call(
        prepare_kernel,
        (pltpu.VMEM((16, V), jnp.int32), pltpu.VMEM((BLOCK, COLS), BF), pltpu.VMEM((V, COLS), BF)),
        (features, grad_out, hub_feats, nbr_owner.reshape(8, 1, V), nbr_row, hub_ids.T),
        "prepare",
        scratch=[
            pltpu.VMEM((8, 1, V), jnp.int32),
            pltpu.VMEM((8, V), jnp.int32),
            pltpu.VMEM((4, V), jnp.int32),
            pltpu.VMEM((2 * HUB_ROWS, 256), BF),
            pltpu.SemaphoreType.DMA((7,)),
        ],
        far=6,
        mib=56,
    )

    fg1 = swap(fg, "x", NX, 1)
    fg23 = swap(jnp.concatenate([fg, fg1], 0), "x", NX, 2)

    pair = jnp.stack([ids, swap(ids, "c", NC, 1)])
    t1, t7, t2 = shift(mine, "z", NZ, -1), shift(mine, "z", NZ, 1), shift(mine, "z", NZ, -2)
    pairs = [pair] + [swap(pair, "y", NY, m) for m in range(1, NY)]
    t34 = shift(jnp.concatenate([t1, t2], 0), "z", NZ, -2)
    t65 = shift(jnp.concatenate([mine, t7], 0), "z", NZ, 2)
    counts = call(
        counts_kernel,
        pltpu.VMEM((PARTS, ROWS, V), BF),
        (*pairs,),
        "counts",
        flops=1 << 34,
        mib=8,
    )

    far, turned = call(
        far_sums_kernel,
        (shaped((NY, COLS, V), BF), shaped((COLS, ROWS), BF)),
        (counts, mine, t1, t2, t7, t34, t65),
        "far_sums",
        scratch=[pltpu.VMEM((ROWS, COLS), BF)],
        flops=1 << 31,
    )
    got = swap(far, "c", NC, 1)
    near = call(
        near_sums_kernel, shaped((NY, COLS, V), F32), (counts, turned), "near_sums", flops=1 << 31
    )
    both = near + got.astype(F32)
    total = both[0]
    for m in range(1, NY):
        total = total + swap(both[m].astype(BF), "y", NY, m).astype(F32)
    total = total.astype(BF)
    sums = [total] + [swap(total, "x", NX, m) for m in range(1, NX)]

    feats, cots, base = call(
        arrange_kernel,
        (shaped((V, 256), BF), shaped((V, 256), BF), shaped((V, 256), F32)),
        (fg, fg1, fg23, w_self),
        "arrange",
        scratch=[pltpu.VMEM((NX, V, COLS), BF)],
        flops=1 << 28,
    )
    outputs, message, self_term = call(
        dense_kernel,
        (shaped((HALF, COLS), BF), shaped((V + WROWS, COLS), BF), shaped((HALF, COLS), F32)),
        (feats, cots, base, *sums, w_self, w_nbr),
        "dense",
        scratch=[
            pltpu.VMEM((4, COLS, V), BF),
            pltpu.VMEM((4, HALF, COLS), BF),
            pltpu.VMEM((2, 256, 256), F32),
        ],
        flops=1 << 30,
    )

    messages = [message] + [swap(message, "y", NY, m) for m in range(1, NY)]
    others = [swap(m, "c", NC, 1) for m in messages]
    near_grads = call(
        near_grads_kernel,
        shaped((len(FIRST_BLOCKS), HALF, COLS), F32),
        (counts, *messages),
        "near_grads",
        flops=1 << 30,
    )
    hop_shapes = (shaped((BLOCK + WROWS, COLS), BF),) * 2
    up0, down0, hubs = call(
        first_grads_kernel,
        (*hop_shapes, shaped((NZ, HUB_ROWS, COLS), F32)),
        (counts, *messages, *others, near_grads),
        "first_grads",
        flops=1 << 30,
    )
    up1, down1 = shift(up0, "z", NZ, 1), shift(down0, "z", NZ, -1)
    rest = call(
        rest_grads_kernel,
        shaped((len(REST), HALF, COLS), F32),
        (counts, *messages, *others),
        "rest_grads",
        flops=1 << 31,
    )
    ups, downs = [up1], [down1]
    for deltas in ((3, 6), (2, 7)):
        up, down = call(
            functools.partial(hop_kernel, deltas=deltas),
            hop_shapes,
            (ups[-1], downs[-1], rest, hubs),
            "hop",
        )
        ups.append(shift(up, "z", NZ, 1))
        downs.append(shift(down, "z", NZ, -1))
    up, hub_up, hub_here = call(
        last_hop_kernel,
        (
            shaped((HALF + WROWS, COLS), BF),
            shaped((HUB_ROWS, COLS), F32),
            shaped((HUB_ROWS, COLS), F32),
        ),
        (ups[-1], downs[-1], rest, hubs),
        "last_hop",
    )
    ups.append(shift(up, "z", NZ, 1))
    turn = (0, 2, 1, 3)
    cross = [(z * NX + x, (z + 1) % NZ * NX + turn[x]) for z in range(NZ) for x in range(NX)]
    hub_up = lax.ppermute(hub_up, ("z", "x"), cross)
    hub_here = lax.ppermute(hub_here, "x", [(x, turn[x]) for x in range(NX)])
    grad_features, hub_rows, grad_self, grad_nbr = call(
        final_kernel,
        (
            shaped((HALF, COLS), BF),
            shaped((2 * HUB_ROWS, 64), F32),
            shaped((64, 256), F32),
            shaped((64, 256), F32),
        ),
        (self_term, rest, up0, *ups, *downs, hub_up, hub_here),
        "last_sums",
        scratch=[pltpu.VMEM((NZ, WROWS, COLS), BF)],
    )
    return outputs, grad_features, hub_rows, grad_self, grad_nbr


def solution(mesh):
    fine = Mesh(mesh.devices.reshape(NY, NZ, NC, NX), ("y", "z", "c", "x"))
    dom = ("y", "z", "c")
    in_specs = (
        P(dom, "x"),
        P(dom, None),
        P(None, dom, None),
        P(None, dom),
        P(dom, None),
        P(),
        P(),
        P(dom, "x"),
    )
    out_specs = (P(dom, "x"), P(dom, "x"), P(dom, "x"), P("x", None), P("x", None))
    return jax.shard_map(body, mesh=fine, in_specs=in_specs, out_specs=out_specs, check_vma=False)
```

```python
import functools

import jax
import jax.numpy as jnp
from jax import lax
from jax.experimental import pallas as pl
from jax.experimental.pallas import tpu as pltpu
from jax.sharding import Mesh, PartitionSpec as P

NY, NZ, NC, NX = 4, 8, 2, 4
V = 512
HALF = 256
COLS = 128
HUB_ROWS = 16
BLOCK = HALF + HUB_ROWS
ROWS = (NZ + 1) * HALF
PARTS = NC * NY
WROWS = 256
DISTINCT = 4
BF = jnp.bfloat16
F32 = jnp.float32
VM = pl.BlockSpec(memory_space=pltpu.VMEM)
PLAIN = (((1,), (0,)), ((), ()))
LAST = (((1,), (1,)), ((), ()))
FIRST = (((0,), (0,)), ((), ()))


def dot(a, b, dims=PLAIN, **kw):
    return lax.dot_general(a, b, dims, preferred_element_type=F32, **kw)


def shift(x, axis, size, step):
    return lax.ppermute(x, axis, [(i, (i + step) % size) for i in range(size)])


def swap(x, axis, size, mask):
    return lax.ppermute(x, axis, [(i, i ^ mask) for i in range(size)])


MASKS = (0, 2, 1, 3)


def three(x, axis, size, each=False):
    own = x[0] if each else x
    return [own] + [swap(x[mask] if each else x, axis, size, mask) for mask in MASKS[1:]]


def call(kernel, outs, inputs, name, scratch=(), flops=0, mib=16, far=0):
    return pl.pallas_call(
        kernel,
        out_shape=outs,
        in_specs=[VM] * (len(inputs) - far) + [pl.BlockSpec(memory_space=pl.ANY)] * far,
        out_specs=jax.tree.map(lambda _: VM, outs),
        scratch_shapes=list(scratch),
        compiler_params=pltpu.CompilerParams(vmem_limit_bytes=mib << 20),
        cost_estimate=pl.CostEstimate(flops=flops, bytes_accessed=1 << 18, transcendentals=0),
        name=name,
    )(*inputs)


def shaped(shape, dtype):
    return jax.ShapeDtypeStruct(shape, dtype)


def prepare_kernel(
    feat, cot, hub, owner, row, hub_id, ids_ref, mine_ref, both,
    owner_scr, row_scr, hub_id_scr, hub_scr, sems,
):
    parity, half = lax.axis_index("x") // 2, lax.axis_index("x") % 2
    pairs = (
        (owner, owner_scr),
        (row, row_scr),
        (hub_id, hub_id_scr),
        (hub, hub_scr),
        (feat, mine_ref.at[pl.ds(0, HALF)]),
        (feat, both.at[pl.ds(0, HALF)]),
        (cot, both.at[pl.ds(HALF, HALF)]),
    )
    copies = [pltpu.make_async_copy(a, b, sems.at[i]) for i, (a, b) in enumerate(pairs)]
    for copy in copies:
        copy.start()
    for copy in copies:
        copy.wait()
    ids_ref[0:8] = owner_scr[...].reshape(8, V) * V + row_scr[...]
    ids_ref[8:12] = hub_id_scr[...]
    ids_ref[12:16] = jnp.full((4, V), -1, jnp.int32)
    pick = lax.broadcasted_iota(jnp.int32, (HUB_ROWS, 2 * HUB_ROWS), 1) == (
        2 * lax.broadcasted_iota(jnp.int32, (HUB_ROWS, 2 * HUB_ROWS), 0) + parity
    )
    columns = hub_scr[:, pl.ds(pl.multiple_of(half * COLS, COLS), COLS)]
    mine_ref[HALF:BLOCK] = dot(pick.astype(F32).astype(BF), columns).astype(BF)


def counts_kernel(ids0, ids1, ids2, ids3, out_ref):
    y, z, c, x = (lax.axis_index(a) for a in ("y", "z", "c", "x"))
    parity = x // 2
    rows = lax.broadcasted_iota(jnp.int32, (16, 16, 128), 0) * 16 + lax.broadcasted_iota(
        jnp.int32, (16, 16, 128), 1
    )
    rows = rows.astype(F32).astype(BF)
    level = lax.broadcasted_iota(jnp.int32, (8, V), 0)
    column = y * (NZ * NC) + c
    mask = (NY - 1) * (NZ * NC) + (NC - 1)

    def allmax(a):
        for s in (4, 2, 1):
            a = jnp.maximum(a, pltpu.roll(a, s, 0))
        return a

    def allsum(a):
        for s in (4, 2, 1):
            a = a + pltpu.roll(a, s, 0)
        return a

    def extract(keys):
        top = allmax(keys)
        hit = keys == top
        return jnp.where(hit, -1.0, keys), top, allsum(jnp.where(hit, 1.0, 0.0))

    def pair(a):
        return jnp.concatenate([a, a], 0).astype(BF)

    for dy, ids_ref in zip(MASKS, (ids0, ids1, ids2, ids3)):

        def part(dc, carry, dy=dy, ids_ref=ids_ref):
            index = dc * NY + dy
            ids = ids_ref[dc]
            flat, hub = ids[0:8], ids[8:16]
            here = ((flat >> 9) & mask) == column
            here = here & ((flat & 1) == parity)
            keys = jnp.where(here, (((flat >> 10) - z) & 7) * HALF + ((flat >> 1) & 255), -1).astype(F32)
            here = (((hub >> 5) & mask) == column) & (level < 4)
            hub_row = (((hub >> 6) - z) & 7) * 32 + ((hub & 1) ^ parity) * 16 + ((hub >> 1) & 15)
            hub_keys = jnp.where(here, hub_row, -1).astype(F32)
            found, hub_found = [], []
            for _ in range(DISTINCT):
                keys, top, times = extract(keys)
                found.append((top, pair(times)))
            for _ in range(4):
                hub_keys, top, times = extract(hub_keys)
                hub_found.append((pair(top), pair(times)))
            for tile in range(V // 128):
                lanes = slice(tile * 128, (tile + 1) * 128)
                for delta in range(NZ):
                    block = jnp.zeros((16, 16, 128), BF)
                    for top, times in found:
                        match = pair(top[:, lanes] - float(HALF * delta))[None] == rows
                        block = jnp.where(match, times[:, lanes][None], block)
                    out_ref[index, delta * HALF : (delta + 1) * HALF, lanes] = block.reshape(HALF, 128)
                block = jnp.zeros((16, 16, 128), BF)
                for top, times in hub_found:
                    block = jnp.where(top[:, lanes][None] == rows, times[:, lanes][None], block)
                out_ref[index, NZ * HALF : ROWS, lanes] = block.reshape(HALF, 128)

            @pl.when(jnp.max(keys) >= 0)
            def _():
                def more(_, keys):
                    keys, top, times = extract(keys)
                    for tile in range(V // 128):
                        lanes = slice(tile * 128, (tile + 1) * 128)
                        for delta in range(NZ):
                            span = slice(delta * HALF, (delta + 1) * HALF)
                            block = out_ref[index, span, lanes].reshape(16, 16, 128)
                            match = pair(top[:, lanes] - float(HALF * delta))[None] == rows
                            block = jnp.where(match, pair(times[:, lanes])[None], block)
                            out_ref[index, span, lanes] = block.reshape(HALF, 128)
                    return keys

                lax.fori_loop(0, 8 - DISTINCT, more, keys)

            return carry

        lax.fori_loop(0, NC, part, 0)


def far_sums_kernel(counts, t0, t1, t2, t7, t34, t65, sums_ref, turned_ref, table):
    blocks = {0: t0[...], 1: t1[...], 2: t2[...], 7: t7[...]}
    blocks[3], blocks[4] = t34[0:BLOCK], t34[BLOCK : 2 * BLOCK]
    blocks[6], blocks[5] = t65[0:BLOCK], t65[BLOCK : 2 * BLOCK]
    for delta in range(NZ):
        table[delta * HALF : (delta + 1) * HALF] = blocks[delta][0:HALF]
        start = NZ * HALF + delta * 2 * HUB_ROWS
        table[start : start + HUB_ROWS] = blocks[delta][HALF:BLOCK]
        table[start + HUB_ROWS : start + 2 * HUB_ROWS] = jnp.zeros((HUB_ROWS, COLS), BF)
    turned_ref[...] = table[...].T

    for dy in range(NY):
        sums_ref[dy] = dot(turned_ref[...], counts[NY + dy]).astype(BF)


def near_sums_kernel(counts, turned, sums_ref):
    for dy in range(NY):
        sums_ref[dy] = dot(turned[...], counts[dy])


def arrange_kernel(fg0, fg1, fg23, ws_ref, turned_ref, cot_ref, pre_ref, order_ref, back_ref, scr):
    x = lax.axis_index("x")
    for mask, (ref, start) in enumerate(((fg0, 0), (fg1, 0), (fg23, 0), (fg23, V))):
        scr[x ^ mask] = ref[start : start + V]
    rows = []
    for start in (0, HALF):
        quarters = [scr[q, start : start + HALF] for q in range(NX)]
        rows.append(
            jnp.concatenate(
                [jnp.concatenate(quarters[0:2], 1), jnp.concatenate(quarters[2:4], 1)], 0
            )
        )
    turned_ref[...] = rows[0].T
    cot_ref[...] = rows[1]
    pre_ref[...] = dot(rows[0], ws_ref[...])
    first = lax.broadcasted_iota(jnp.int32, (V, V), 0)
    second = lax.broadcasted_iota(jnp.int32, (V, V), 1)
    order_ref[...] = ((first % HALF) * 2 + first // HALF == second).astype(F32).astype(BF)
    back_ref[...] = ((second % HALF) * 2 + second // HALF == first).astype(F32).astype(BF)


def dense_kernel(
    turned_ref, cot_ref, pre_ref, order_ref, back_ref, s0, s1, s2, s3, ws_ref, wn_ref,
    out_ref, message_ref, self_ref,
    s_scr, o_scr, w_scr,
):
    x = lax.axis_index("x")
    parity, half = x // 2, x % 2
    for mask, ref in zip(MASKS, (s0, s1, s2, s3)):
        s_scr[x ^ mask] = ref[...]
    mean_t = jnp.concatenate(
        [
            s_scr[0].astype(F32) + s_scr[2].astype(F32),
            s_scr[1].astype(F32) + s_scr[3].astype(F32),
        ],
        0,
    )
    mean_t = (mean_t / 12.0).astype(BF)
    mean = dot(order_ref[...], mean_t, LAST).astype(BF)
    pre = pre_ref[...] + dot(mean, wn_ref[...])
    sig = jax.nn.sigmoid(pre)
    value = (pre * sig).astype(BF)
    grad_pre = (cot_ref[...].astype(F32) * sig * (1.0 + pre * (1.0 - sig))).astype(BF)
    for q in range(2):
        for h in range(2):
            o_scr[q * 2 + h] = value[q * HALF : (q + 1) * HALF, h * COLS : (h + 1) * COLS]
    out_ref[...] = o_scr[x]
    rows = pl.ds(pl.multiple_of(half * COLS, COLS), COLS)
    natural = dot(back_ref[...], grad_pre).astype(BF)
    message_ref[0:V] = (dot(natural, wn_ref[rows, :], LAST) / 12.0).astype(BF)
    own_self = dot(grad_pre, ws_ref[rows, :], LAST)
    self_ref[...] = jnp.where(parity == 0, own_self[0:HALF], own_self[HALF:V])
    w_scr[0] = dot(turned_ref[...], grad_pre)
    w_scr[1] = dot(mean_t, natural)
    quarter = pl.ds(pl.multiple_of(x * 64, 64), 64)
    for which in range(2):
        part = w_scr[which, quarter, :]
        for h in range(2):
            start = V + which * 128 + h * 64
            message_ref[start : start + 64, :] = part[:, h * COLS : (h + 1) * COLS].astype(BF)


def block_sum(counts, base, messages, block, total=None):
    span = slice(block * HALF, (block + 1) * HALF)
    for index, ref in enumerate(messages):
        dy = base + index // NY * NY + MASKS[index % NY]
        term = dot(counts[dy, span], ref[0:V])
        total = term if total is None else total + term
    return total


FIRST_BLOCKS = (4, 5, NZ)
REST = (0, 1, 2, 3, 6, 7)


def near_grads_kernel(counts, m0, m1, m2, m3, out_ref):
    for index, block in enumerate(FIRST_BLOCKS):
        out_ref[index] = block_sum(counts, 0, (m0, m1, m2, m3), block)


def first_grads_kernel(
    counts, m0, m1, m2, m3, o0, o1, o2, o3, near, up_ref, down_ref, hub_ref
):
    parity = lax.axis_index("x") // 2
    others = (o0, o1, o2, o3)
    blocks = [block_sum(counts, NY, others, block, near[index]) for index, block in enumerate(FIRST_BLOCKS)]
    hubs = blocks[2]
    lane = lax.broadcasted_iota(jnp.int32, (HUB_ROWS, COLS), 1)
    low = (lane < 64) == (parity == 0)
    for delta in range(NZ):
        start = delta * 2 * HUB_ROWS
        mine = hubs[start : start + HUB_ROWS]
        rest = pltpu.roll(hubs[start + HUB_ROWS : start + 2 * HUB_ROWS], 64, 1)
        hub_ref[delta] = jnp.where(low, mine, rest)
    tail = slice(V, V + WROWS)
    sums = [
        (a[tail].astype(F32) + b[tail].astype(F32)) + (c[tail].astype(F32) + d[tail].astype(F32))
        for a, b, c, d in ((m0, m1, m2, m3), others)
    ]
    weight = (sums[0] + sums[1]).astype(BF)
    for index, ref in enumerate((up_ref, down_ref)):
        ref[0:HALF] = blocks[index].astype(BF)
        ref[HALF:BLOCK] = hub_ref[FIRST_BLOCKS[index]].astype(BF)
        ref[BLOCK:] = weight


def rest_grads_kernel(counts, m0, m1, m2, m3, o0, o1, o2, o3, out_ref):
    for index, block in enumerate(REST):
        out_ref[index] = block_sum(counts, 0, (m0, m1, m2, m3, o0, o1, o2, o3), block)


def hop_kernel(up, down, rest, hubs, next_up, next_down, *, deltas):
    for delta, got, ref in zip(deltas, (up, down), (next_up, next_down)):
        ref[0:HALF] = (got[0:HALF].astype(F32) + rest[REST.index(delta)]).astype(BF)
        ref[HALF:BLOCK] = (got[HALF:BLOCK].astype(F32) + hubs[delta]).astype(BF)
        ref[BLOCK:] = got[BLOCK:]


def last_hop_kernel(up, down, rest, hubs, next_up, hub_up, hub_here):
    next_up[0:HALF] = (up[0:HALF].astype(F32) + rest[REST.index(1)]).astype(BF)
    next_up[HALF:] = up[BLOCK:]
    hub_up[...] = up[HALF:BLOCK].astype(F32) + hubs[1]
    hub_here[...] = down[HALF:BLOCK].astype(F32) + hubs[0]


def final_kernel(
    self_ref, rest, first, up1, up2, up3, up4, down1, down2, down3, hub_up, hub_here,
    feat_ref, hub_ref, gself_ref, gnbr_ref, w_scr,
):
    z = lax.axis_index("z")
    total = rest[0] + up4[0:HALF].astype(F32) + down3[0:HALF].astype(F32)
    feat_ref[...] = (self_ref[...] + total).astype(BF)
    hubs = hub_up[...] + hub_here[...]
    shape = (2 * HUB_ROWS, HUB_ROWS)
    target = lax.broadcasted_iota(jnp.int32, shape, 0)
    source = lax.broadcasted_iota(jnp.int32, shape, 1)
    spread = [
        dot((target == 2 * source + q).astype(F32), hubs[:, q * 64 : (q + 1) * 64], precision=lax.Precision.HIGHEST)
        for q in range(2)
    ]
    hub_ref[...] = spread[0] + spread[1]
    arrived = {0: first, 7: up1, 6: up2, 5: up3, 1: down1, 2: down2, 3: down3}
    for step in range(NZ):
        if step == 4:
            w_scr[(z + step) % NZ] = up4[HALF:]
        else:
            w_scr[(z + step) % NZ] = arrived[step][BLOCK:]
    weight = w_scr[0].astype(F32)
    for step in range(1, NZ):
        weight = weight + w_scr[step].astype(F32)
    gself_ref[...] = jnp.concatenate([weight[0:64], weight[64:128]], 1)
    gnbr_ref[...] = jnp.concatenate([weight[128:192], weight[192:256]], 1)


def body(features, hub_feats, nbr_owner, nbr_row, hub_ids, w_self, w_nbr, grad_out):
    ids, mine, fg = call(
        prepare_kernel,
        (pltpu.VMEM((16, V), jnp.int32), pltpu.VMEM((BLOCK, COLS), BF), pltpu.VMEM((V, COLS), BF)),
        (features, grad_out, hub_feats, nbr_owner.reshape(8, 1, V), nbr_row, hub_ids.T),
        "prepare",
        scratch=[
            pltpu.VMEM((8, 1, V), jnp.int32),
            pltpu.VMEM((8, V), jnp.int32),
            pltpu.VMEM((4, V), jnp.int32),
            pltpu.VMEM((2 * HUB_ROWS, 256), BF),
            pltpu.SemaphoreType.DMA((7,)),
        ],
        far=6,
        mib=56,
    )

    fg1 = swap(fg, "x", NX, 1)
    fg23 = swap(jnp.concatenate([fg, fg1], 0), "x", NX, 2)

    pair = jnp.stack([ids, swap(ids, "c", NC, 1)])
    t1, t7, t2 = shift(mine, "z", NZ, -1), shift(mine, "z", NZ, 1), shift(mine, "z", NZ, -2)
    pairs = three(pair, "y", NY)
    t34 = shift(jnp.concatenate([t1, t2], 0), "z", NZ, -2)
    t65 = shift(jnp.concatenate([mine, t7], 0), "z", NZ, 2)
    counts = call(
        counts_kernel,
        pltpu.VMEM((PARTS, ROWS, V), BF),
        (*pairs,),
        "counts",
        flops=1 << 34,
        mib=8,
    )

    far, turned = call(
        far_sums_kernel,
        (shaped((NY, COLS, V), BF), shaped((COLS, ROWS), BF)),
        (counts, mine, t1, t2, t7, t34, t65),
        "far_sums",
        scratch=[pltpu.VMEM((ROWS, COLS), BF)],
        flops=1 << 31,
    )
    got = swap(far, "c", NC, 1)
    near = call(
        near_sums_kernel, shaped((NY, COLS, V), F32), (counts, turned), "near_sums", flops=1 << 31
    )
    both = near + got.astype(F32)
    parts = three(both.astype(BF), "y", NY, each=True)
    total = both[0] + parts[1].astype(F32) + parts[2].astype(F32) + parts[3].astype(F32)
    sums = three(total.astype(BF), "x", NX)

    arranged = call(
        arrange_kernel,
        (
            shaped((256, V), BF),
            shaped((V, 256), BF),
            shaped((V, 256), F32),
            shaped((V, V), BF),
            shaped((V, V), BF),
        ),
        (fg, fg1, fg23, w_self),
        "arrange",
        scratch=[pltpu.VMEM((NX, V, COLS), BF)],
        flops=1 << 28,
    )
    outputs, message, self_term = call(
        dense_kernel,
        (shaped((HALF, COLS), BF), shaped((V + WROWS, COLS), BF), shaped((HALF, COLS), F32)),
        (*arranged, *sums, w_self, w_nbr),
        "dense",
        scratch=[
            pltpu.VMEM((4, COLS, V), BF),
            pltpu.VMEM((4, HALF, COLS), BF),
            pltpu.VMEM((2, 256, 256), F32),
        ],
        flops=1 << 30,
    )

    messages = three(message, "y", NY)
    others = [swap(m, "c", NC, 1) for m in messages]
    near_grads = call(
        near_grads_kernel,
        shaped((len(FIRST_BLOCKS), HALF, COLS), F32),
        (counts, *messages),
        "near_grads",
        flops=1 << 30,
    )
    hop_shapes = (shaped((BLOCK + WROWS, COLS), BF),) * 2
    up0, down0, hubs = call(
        first_grads_kernel,
        (*hop_shapes, shaped((NZ, HUB_ROWS, COLS), F32)),
        (counts, *messages, *others, near_grads),
        "first_grads",
        flops=1 << 30,
    )
    up1, down1 = shift(up0, "z", NZ, 1), shift(down0, "z", NZ, -1)
    rest = call(
        rest_grads_kernel,
        shaped((len(REST), HALF, COLS), F32),
        (counts, *messages, *others),
        "rest_grads",
        flops=1 << 31,
    )
    ups, downs = [up1], [down1]
    for deltas in ((3, 6), (2, 7)):
        up, down = call(
            functools.partial(hop_kernel, deltas=deltas),
            hop_shapes,
            (ups[-1], downs[-1], rest, hubs),
            "hop",
        )
        ups.append(shift(up, "z", NZ, 1))
        downs.append(shift(down, "z", NZ, -1))
    up, hub_up, hub_here = call(
        last_hop_kernel,
        (
            shaped((HALF + WROWS, COLS), BF),
            shaped((HUB_ROWS, COLS), F32),
            shaped((HUB_ROWS, COLS), F32),
        ),
        (ups[-1], downs[-1], rest, hubs),
        "last_hop",
    )
    ups.append(shift(up, "z", NZ, 1))
    turn = (0, 2, 1, 3)
    cross = [(z * NX + x, (z + 1) % NZ * NX + turn[x]) for z in range(NZ) for x in range(NX)]
    hub_up = lax.ppermute(hub_up, ("z", "x"), cross)
    hub_here = lax.ppermute(hub_here, "x", [(x, turn[x]) for x in range(NX)])
    grad_features, hub_rows, grad_self, grad_nbr = call(
        final_kernel,
        (
            shaped((HALF, COLS), BF),
            shaped((2 * HUB_ROWS, 64), F32),
            shaped((64, 256), F32),
            shaped((64, 256), F32),
        ),
        (self_term, rest, up0, *ups, *downs, hub_up, hub_here),
        "last_sums",
        scratch=[pltpu.VMEM((NZ, WROWS, COLS), BF)],
    )
    return outputs, grad_features, hub_rows, grad_self, grad_nbr


def solution(mesh):
    fine = Mesh(mesh.devices.reshape(NY, NZ, NC, NX), ("y", "z", "c", "x"))
    dom = ("y", "z", "c")
    in_specs = (
        P(dom, "x"),
        P(dom, None),
        P(None, dom, None),
        P(None, dom),
        P(dom, None),
        P(),
        P(),
        P(dom, "x"),
    )
    out_specs = (P(dom, "x"), P(dom, "x"), P(dom, "x"), P("x", None), P("x", None))
    return jax.shard_map(body, mesh=fine, in_specs=in_specs, out_specs=out_specs, check_vma=False)
```

```python
import functools

import jax
import jax.numpy as jnp
from jax import lax
from jax.experimental import pallas as pl
from jax.experimental.pallas import tpu as pltpu
from jax.sharding import Mesh, PartitionSpec as P

NY, NZ, NC, NX = 4, 8, 2, 4
V = 512
HALF = 256
COLS = 128
HUB_ROWS = 16
BLOCK = HALF + HUB_ROWS
ROWS = (NZ + 1) * HALF
PARTS = NC * NY
WROWS = 256
DISTINCT = 4
BF = jnp.bfloat16
F32 = jnp.float32
VM = pl.BlockSpec(memory_space=pltpu.VMEM)
PLAIN = (((1,), (0,)), ((), ()))
LAST = (((1,), (1,)), ((), ()))
FIRST = (((0,), (0,)), ((), ()))


def dot(a, b, dims=PLAIN, **kw):
    return lax.dot_general(a, b, dims, preferred_element_type=F32, **kw)


def shift(x, axis, size, step):
    return lax.ppermute(x, axis, [(i, (i + step) % size) for i in range(size)])


def swap(x, axis, size, mask):
    return lax.ppermute(x, axis, [(i, i ^ mask) for i in range(size)])


MASKS = (0, 2, 1, 3)


def three(x, axis, size, each=False):
    own = x[0] if each else x
    return [own] + [swap(x[mask] if each else x, axis, size, mask) for mask in MASKS[1:]]


def call(kernel, outs, inputs, name, scratch=(), flops=0, mib=16, far=0):
    return pl.pallas_call(
        kernel,
        out_shape=outs,
        in_specs=[VM] * (len(inputs) - far) + [pl.BlockSpec(memory_space=pl.ANY)] * far,
        out_specs=jax.tree.map(lambda _: VM, outs),
        scratch_shapes=list(scratch),
        compiler_params=pltpu.CompilerParams(vmem_limit_bytes=mib << 20),
        cost_estimate=pl.CostEstimate(flops=flops, bytes_accessed=1 << 18, transcendentals=0),
        name=name,
    )(*inputs)


def shaped(shape, dtype):
    return jax.ShapeDtypeStruct(shape, dtype)


def prepare_kernel(
    feat, cot, hub, owner, row, hub_id, ids_ref, mine_ref, both,
    owner_scr, row_scr, hub_id_scr, hub_scr, sems,
):
    parity, half = lax.axis_index("x") // 2, lax.axis_index("x") % 2
    pairs = (
        (owner, owner_scr),
        (row, row_scr),
        (hub_id, hub_id_scr),
        (hub, hub_scr),
        (feat, mine_ref.at[pl.ds(0, HALF)]),
        (feat, both.at[pl.ds(0, HALF)]),
        (cot, both.at[pl.ds(HALF, HALF)]),
    )
    copies = [pltpu.make_async_copy(a, b, sems.at[i]) for i, (a, b) in enumerate(pairs)]
    for copy in copies:
        copy.start()
    for copy in copies:
        copy.wait()
    ids_ref[0:8] = owner_scr[...].reshape(8, V) * V + row_scr[...]
    ids_ref[8:12] = hub_id_scr[...]
    ids_ref[12:16] = jnp.full((4, V), -1, jnp.int32)
    pick = lax.broadcasted_iota(jnp.int32, (HUB_ROWS, 2 * HUB_ROWS), 1) == (
        2 * lax.broadcasted_iota(jnp.int32, (HUB_ROWS, 2 * HUB_ROWS), 0) + parity
    )
    columns = hub_scr[:, pl.ds(pl.multiple_of(half * COLS, COLS), COLS)]
    mine_ref[HALF:BLOCK] = dot(pick.astype(F32).astype(BF), columns).astype(BF)


def counts_kernel(ids0, ids1, ids2, ids3, out_ref, ids_scr):
    y, z, c, x = (lax.axis_index(a) for a in ("y", "z", "c", "x"))
    parity = x // 2
    rows = lax.broadcasted_iota(jnp.int32, (16, 16, 128), 0) * 16 + lax.broadcasted_iota(
        jnp.int32, (16, 16, 128), 1
    )
    rows = rows.astype(F32).astype(BF)
    level = lax.broadcasted_iota(jnp.int32, (8, V), 0)
    column = y * (NZ * NC) + c
    mask = (NY - 1) * (NZ * NC) + (NC - 1)

    def allmax(a):
        for s in (4, 2, 1):
            a = jnp.maximum(a, pltpu.roll(a, s, 0))
        return a

    def allsum(a):
        for s in (4, 2, 1):
            a = a + pltpu.roll(a, s, 0)
        return a

    def extract(keys):
        top = allmax(keys)
        hit = keys == top
        return jnp.where(hit, -1.0, keys), top, allsum(jnp.where(hit, 1.0, 0.0))

    def pair(a):
        return jnp.concatenate([a, a], 0).astype(BF)

    for dy, ids_ref in zip(MASKS, (ids0, ids1, ids2, ids3)):
        for dc in range(NC):
            ids_scr[dc * NY + dy] = ids_ref[dc]

    def part(index, carry):
        ids = ids_scr[index]
        flat, hub = ids[0:8], ids[8:16]
        here = ((flat >> 9) & mask) == column
        here = here & ((flat & 1) == parity)
        keys = jnp.where(here, (((flat >> 10) - z) & 7) * HALF + ((flat >> 1) & 255), -1).astype(F32)
        here = (((hub >> 5) & mask) == column) & (level < 4)
        hub_row = (((hub >> 6) - z) & 7) * 32 + ((hub & 1) ^ parity) * 16 + ((hub >> 1) & 15)
        hub_keys = jnp.where(here, hub_row, -1).astype(F32)
        found, hub_found = [], []
        for _ in range(DISTINCT):
            keys, top, times = extract(keys)
            found.append((top, pair(times)))
        for _ in range(4):
            hub_keys, top, times = extract(hub_keys)
            hub_found.append((pair(top), pair(times)))
        for tile in range(V // 128):
            lanes = slice(tile * 128, (tile + 1) * 128)
            for delta in range(NZ):
                block = jnp.zeros((16, 16, 128), BF)
                for top, times in found:
                    match = pair(top[:, lanes] - float(HALF * delta))[None] == rows
                    block = jnp.where(match, times[:, lanes][None], block)
                out_ref[index, delta * HALF : (delta + 1) * HALF, lanes] = block.reshape(HALF, 128)
            block = jnp.zeros((16, 16, 128), BF)
            for top, times in hub_found:
                block = jnp.where(top[:, lanes][None] == rows, times[:, lanes][None], block)
            out_ref[index, NZ * HALF : ROWS, lanes] = block.reshape(HALF, 128)

        @pl.when(jnp.max(keys) >= 0)
        def _():
            def more(_, keys):
                keys, top, times = extract(keys)
                for tile in range(V // 128):
                    lanes = slice(tile * 128, (tile + 1) * 128)
                    for delta in range(NZ):
                        span = slice(delta * HALF, (delta + 1) * HALF)
                        block = out_ref[index, span, lanes].reshape(16, 16, 128)
                        match = pair(top[:, lanes] - float(HALF * delta))[None] == rows
                        block = jnp.where(match, pair(times[:, lanes])[None], block)
                        out_ref[index, span, lanes] = block.reshape(HALF, 128)
                return keys

            lax.fori_loop(0, 8 - DISTINCT, more, keys)

        return carry

    lax.fori_loop(0, PARTS, part, 0)


def far_sums_kernel(counts, t0, t1, t2, t7, t34, t65, sums_ref, turned_ref, table):
    blocks = {0: t0[...], 1: t1[...], 2: t2[...], 7: t7[...]}
    blocks[3], blocks[4] = t34[0:BLOCK], t34[BLOCK : 2 * BLOCK]
    blocks[6], blocks[5] = t65[0:BLOCK], t65[BLOCK : 2 * BLOCK]
    for delta in range(NZ):
        table[delta * HALF : (delta + 1) * HALF] = blocks[delta][0:HALF]
        start = NZ * HALF + delta * 2 * HUB_ROWS
        table[start : start + HUB_ROWS] = blocks[delta][HALF:BLOCK]
        table[start + HUB_ROWS : start + 2 * HUB_ROWS] = jnp.zeros((HUB_ROWS, COLS), BF)
    turned_ref[...] = table[...].T

    for dy in range(NY):
        sums_ref[dy] = dot(turned_ref[...], counts[NY + dy]).astype(BF)


def near_sums_kernel(counts, turned, sums_ref):
    for dy in range(NY):
        sums_ref[dy] = dot(turned[...], counts[dy])


def arrange_kernel(fg0, fg1, fg23, ws_ref, turned_ref, cot_ref, pre_ref, order_ref, back_ref, scr):
    x = lax.axis_index("x")
    for mask, (ref, start) in enumerate(((fg0, 0), (fg1, 0), (fg23, 0), (fg23, V))):
        scr[x ^ mask] = ref[start : start + V]
    rows = []
    for start in (0, HALF):
        quarters = [scr[q, start : start + HALF] for q in range(NX)]
        rows.append(
            jnp.concatenate(
                [jnp.concatenate(quarters[0:2], 1), jnp.concatenate(quarters[2:4], 1)], 0
            )
        )
    turned_ref[...] = rows[0].T
    cot_ref[...] = rows[1]
    pre_ref[...] = dot(rows[0], ws_ref[...])
    first = lax.broadcasted_iota(jnp.int32, (V, V), 0)
    second = lax.broadcasted_iota(jnp.int32, (V, V), 1)
    order_ref[...] = ((first % HALF) * 2 + first // HALF == second).astype(F32).astype(BF)
    back_ref[...] = ((second % HALF) * 2 + second // HALF == first).astype(F32).astype(BF)


def dense_kernel(
    turned_ref, cot_ref, pre_ref, order_ref, back_ref, s0, s1, s2, s3, ws_ref, wn_ref,
    out_ref, message_ref, self_ref,
    s_scr, o_scr, w_scr,
):
    x = lax.axis_index("x")
    parity, half = x // 2, x % 2
    for mask, ref in zip(MASKS, (s0, s1, s2, s3)):
        s_scr[x ^ mask] = ref[...]
    mean_t = jnp.concatenate(
        [
            s_scr[0].astype(F32) + s_scr[2].astype(F32),
            s_scr[1].astype(F32) + s_scr[3].astype(F32),
        ],
        0,
    )
    mean_t = (mean_t / 12.0).astype(BF)
    mean = dot(order_ref[...], mean_t, LAST).astype(BF)
    pre = pre_ref[...] + dot(mean, wn_ref[...])
    sig = jax.nn.sigmoid(pre)
    value = (pre * sig).astype(BF)
    grad_pre = (cot_ref[...].astype(F32) * sig * (1.0 + pre * (1.0 - sig))).astype(BF)
    for q in range(2):
        for h in range(2):
            o_scr[q * 2 + h] = value[q * HALF : (q + 1) * HALF, h * COLS : (h + 1) * COLS]
    out_ref[...] = o_scr[x]
    rows = pl.ds(pl.multiple_of(half * COLS, COLS), COLS)
    natural = dot(back_ref[...], grad_pre).astype(BF)
    message_ref[0:V] = (dot(natural, wn_ref[rows, :], LAST) / 12.0).astype(BF)
    own_self = dot(grad_pre, ws_ref[rows, :], LAST)
    self_ref[...] = jnp.where(parity == 0, own_self[0:HALF], own_self[HALF:V])
    w_scr[0] = dot(turned_ref[...], grad_pre)
    w_scr[1] = dot(mean_t, natural)
    quarter = pl.ds(pl.multiple_of(x * 64, 64), 64)
    for which in range(2):
        part = w_scr[which, quarter, :]
        for h in range(2):
            start = V + which * 128 + h * 64
            message_ref[start : start + 64, :] = part[:, h * COLS : (h + 1) * COLS].astype(BF)


def block_sum(counts, base, messages, block, total=None):
    span = slice(block * HALF, (block + 1) * HALF)
    for index, ref in enumerate(messages):
        dy = base + index // NY * NY + MASKS[index % NY]
        term = dot(counts[dy, span], ref[0:V])
        total = term if total is None else total + term
    return total


FIRST_BLOCKS = (4, 5, NZ)


def near_grads_kernel(counts, m0, m1, m2, m3, out_ref):
    for index, block in enumerate(FIRST_BLOCKS):
        out_ref[index] = block_sum(counts, 0, (m0, m1, m2, m3), block)


def first_grads_kernel(
    counts, m0, m1, m2, m3, o0, o1, o2, o3, near, up_ref, down_ref, hub_ref, skip_ref
):
    parity = lax.axis_index("x") // 2
    others = (o0, o1, o2, o3)
    blocks = [block_sum(counts, NY, others, block, near[index]) for index, block in enumerate(FIRST_BLOCKS)]
    hubs = blocks[2]
    lane = lax.broadcasted_iota(jnp.int32, (HUB_ROWS, COLS), 1)
    low = (lane < 64) == (parity == 0)
    for delta in range(NZ):
        start = delta * 2 * HUB_ROWS
        mine = hubs[start : start + HUB_ROWS]
        rest = pltpu.roll(hubs[start + HUB_ROWS : start + 2 * HUB_ROWS], 64, 1)
        hub_ref[delta] = jnp.where(low, mine, rest)
    tail = slice(V, V + WROWS)
    sums = [
        (a[tail].astype(F32) + b[tail].astype(F32)) + (c[tail].astype(F32) + d[tail].astype(F32))
        for a, b, c, d in ((m0, m1, m2, m3), others)
    ]
    weight = (sums[0] + sums[1]).astype(BF)
    skip_ref[...] = hub_ref[4]
    for index, (hub_delta, ref) in enumerate(((3, up_ref), (5, down_ref))):
        ref[0:HALF] = blocks[index].astype(BF)
        ref[HALF:BLOCK] = hub_ref[hub_delta].astype(BF)
        ref[BLOCK:] = weight


def rest_grads_kernel(counts, m0, m1, m2, m3, o0, o1, o2, o3, out_ref, *, blocks):
    for index, block in enumerate(blocks):
        out_ref[index] = block_sum(counts, 0, (m0, m1, m2, m3, o0, o1, o2, o3), block)


def hop_kernel(got, rest, hubs, skip, turn, next_ref, token_ref, *, index, hub_delta):
    next_ref[0:HALF] = (got[0:HALF].astype(F32) + rest[index]).astype(BF)
    hub = got[HALF:BLOCK].astype(F32) + hubs[hub_delta]
    if hub_delta == 2:
        hub = hub + skip[...]
    next_ref[HALF:BLOCK] = hub.astype(BF)
    next_ref[BLOCK:] = got[BLOCK:]
    token_ref[...] = jnp.zeros_like(token_ref)


def last_hop_kernel(up, rest, turn, next_up, token_ref):
    next_up[0:HALF] = (up[0:HALF].astype(F32) + rest[0]).astype(BF)
    next_up[HALF:] = up[BLOCK:]
    token_ref[...] = jnp.zeros_like(token_ref)


def hub_kernel(up, down, hubs, turn, hub_sum):
    hub_sum[...] = up[HALF:BLOCK].astype(F32) + down[HALF:BLOCK].astype(F32) + hubs[0]


def final_kernel(
    self_ref, rest, first, up1, up2, up3, up4, down1, down2, down3, hub_sum,
    feat_ref, hub_ref, gself_ref, gnbr_ref, w_scr,
):
    z = lax.axis_index("z")
    total = rest[1] + up4[0:HALF].astype(F32) + down3[0:HALF].astype(F32)
    feat_ref[...] = (self_ref[...] + total).astype(BF)
    hubs = hub_sum[...]
    shape = (2 * HUB_ROWS, HUB_ROWS)
    target = lax.broadcasted_iota(jnp.int32, shape, 0)
    source = lax.broadcasted_iota(jnp.int32, shape, 1)
    spread = [
        dot((target == 2 * source + q).astype(F32), hubs[:, q * 64 : (q + 1) * 64], precision=lax.Precision.HIGHEST)
        for q in range(2)
    ]
    hub_ref[...] = spread[0] + spread[1]
    arrived = {0: first, 7: up1, 6: up2, 5: up3, 1: down1, 2: down2, 3: down3}
    for step in range(NZ):
        if step == 4:
            w_scr[(z + step) % NZ] = up4[HALF:]
        else:
            w_scr[(z + step) % NZ] = arrived[step][BLOCK:]
    weight = w_scr[0].astype(F32)
    for step in range(1, NZ):
        weight = weight + w_scr[step].astype(F32)
    gself_ref[...] = jnp.concatenate([weight[0:64], weight[64:128]], 1)
    gnbr_ref[...] = jnp.concatenate([weight[128:192], weight[192:256]], 1)


def body(features, hub_feats, nbr_owner, nbr_row, hub_ids, w_self, w_nbr, grad_out):
    ids, mine, fg = call(
        prepare_kernel,
        (pltpu.VMEM((16, V), jnp.int32), pltpu.VMEM((BLOCK, COLS), BF), pltpu.VMEM((V, COLS), BF)),
        (features, grad_out, hub_feats, nbr_owner.reshape(8, 1, V), nbr_row, hub_ids.T),
        "prepare",
        scratch=[
            pltpu.VMEM((8, 1, V), jnp.int32),
            pltpu.VMEM((8, V), jnp.int32),
            pltpu.VMEM((4, V), jnp.int32),
            pltpu.VMEM((2 * HUB_ROWS, 256), BF),
            pltpu.SemaphoreType.DMA((7,)),
        ],
        far=6,
        mib=56,
    )

    fg1 = swap(fg, "x", NX, 1)
    fg23 = swap(jnp.concatenate([fg, fg1], 0), "x", NX, 2)

    pair = jnp.stack([ids, swap(ids, "c", NC, 1)])
    t1, t7, t2 = shift(mine, "z", NZ, -1), shift(mine, "z", NZ, 1), shift(mine, "z", NZ, -2)
    pairs = three(pair, "y", NY)
    t34 = shift(jnp.concatenate([t1, t2], 0), "z", NZ, -2)
    t65 = shift(jnp.concatenate([mine, t7], 0), "z", NZ, 2)
    counts = call(
        counts_kernel,
        pltpu.VMEM((PARTS, ROWS, V), BF),
        (*pairs,),
        "counts",
        flops=1 << 34,
        scratch=[pltpu.VMEM((PARTS, 16, V), jnp.int32)],
        mib=8,
    )

    far, turned = call(
        far_sums_kernel,
        (shaped((NY, COLS, V), BF), shaped((COLS, ROWS), BF)),
        (counts, mine, t1, t2, t7, t34, t65),
        "far_sums",
        scratch=[pltpu.VMEM((ROWS, COLS), BF)],
        flops=1 << 31,
    )
    got = swap(far, "c", NC, 1)
    near = call(
        near_sums_kernel, shaped((NY, COLS, V), F32), (counts, turned), "near_sums", flops=1 << 31
    )
    both = near + got.astype(F32)
    parts = three(both.astype(BF), "y", NY, each=True)
    total = both[0] + parts[1].astype(F32) + parts[2].astype(F32) + parts[3].astype(F32)
    sums = three(total.astype(BF), "x", NX)

    arranged = call(
        arrange_kernel,
        (
            shaped((256, V), BF),
            shaped((V, 256), BF),
            shaped((V, 256), F32),
            shaped((V, V), BF),
            shaped((V, V), BF),
        ),
        (fg, fg1, fg23, w_self),
        "arrange",
        scratch=[pltpu.VMEM((NX, V, COLS), BF)],
        flops=1 << 28,
    )
    outputs, message, self_term = call(
        dense_kernel,
        (shaped((HALF, COLS), BF), shaped((V + WROWS, COLS), BF), shaped((HALF, COLS), F32)),
        (*arranged, *sums, w_self, w_nbr),
        "dense",
        scratch=[
            pltpu.VMEM((4, COLS, V), BF),
            pltpu.VMEM((4, HALF, COLS), BF),
            pltpu.VMEM((2, 256, 256), F32),
        ],
        flops=1 << 30,
    )

    messages = three(message, "y", NY)
    others = [swap(m, "c", NC, 1) for m in messages]
    near_grads = call(
        near_grads_kernel,
        shaped((len(FIRST_BLOCKS), HALF, COLS), F32),
        (counts, *messages),
        "near_grads",
        flops=1 << 30,
    )
    hop_shapes = (shaped((BLOCK + WROWS, COLS), BF),) * 2
    up0, down0, hubs, skip = call(
        first_grads_kernel,
        (*hop_shapes, shaped((NZ, HUB_ROWS, COLS), F32), shaped((HUB_ROWS, COLS), F32)),
        (counts, *messages, *others, near_grads),
        "first_grads",
        flops=1 << 30,
    )
    up1, down1 = shift(up0, "z", NZ, 1), shift(down0, "z", NZ, -1)
    rests = [
        call(
            functools.partial(rest_grads_kernel, blocks=blocks),
            shaped((2, HALF, COLS), F32),
            (counts, *messages, *others),
            "rest_grads",
            flops=1 << 29,
        )
        for blocks in ((3, 6), (2, 7), (1, 0))
    ]
    skip = shift(skip, "z", NZ, 2)
    ups, downs = [up1], [down1]
    hop_shape, token_shape = shaped((BLOCK + WROWS, COLS), BF), shaped((8, 128), F32)
    token = hubs
    for hub_deltas, rest in zip(((2, 6), (1, 7)), rests):
        for index, (hub_delta, side, step) in enumerate(zip(hub_deltas, (ups, downs), (1, -1))):
            message, token = call(
                functools.partial(hop_kernel, index=index, hub_delta=hub_delta),
                (hop_shape, token_shape),
                (side[-1], rest, hubs, skip, token),
                "hop",
            )
            side.append(shift(message, "z", NZ, step))
    up, token = call(
        last_hop_kernel,
        (shaped((HALF + WROWS, COLS), BF), token_shape),
        (ups[-1], rests[2], token),
        "last_hop",
    )
    hub_sum = call(
        hub_kernel, shaped((HUB_ROWS, COLS), F32), (ups[-1], downs[-1], hubs, token), "hub_sum"
    )
    ups.append(shift(up, "z", NZ, 1))
    hub_sum = lax.ppermute(hub_sum, "x", [(0, 0), (1, 2), (2, 1), (3, 3)])
    grad_features, hub_rows, grad_self, grad_nbr = call(
        final_kernel,
        (
            shaped((HALF, COLS), BF),
            shaped((2 * HUB_ROWS, 64), F32),
            shaped((64, 256), F32),
            shaped((64, 256), F32),
        ),
        (self_term, rests[2], up0, *ups, *downs, hub_sum),
        "last_sums",
        scratch=[pltpu.VMEM((NZ, WROWS, COLS), BF)],
    )
    return outputs, grad_features, hub_rows, grad_self, grad_nbr


def solution(mesh):
    fine = Mesh(mesh.devices.reshape(NY, NZ, NC, NX), ("y", "z", "c", "x"))
    dom = ("y", "z", "c")
    in_specs = (
        P(dom, "x"),
        P(dom, None),
        P(None, dom, None),
        P(None, dom),
        P(dom, None),
        P(),
        P(),
        P(dom, "x"),
    )
    out_specs = (P(dom, "x"), P(dom, "x"), P(dom, "x"), P("x", None), P("x", None))
    return jax.shard_map(body, mesh=fine, in_specs=in_specs, out_specs=out_specs, check_vma=False)
```

```python
import functools

import jax
import jax.numpy as jnp
from jax import lax
from jax.experimental import pallas as pl
from jax.experimental.pallas import tpu as pltpu
from jax.sharding import Mesh, PartitionSpec as P

NY, NZ, NC, NX = 4, 8, 2, 4
V = 512
HALF = 256
COLS = 128
HUB_ROWS = 16
BLOCK = HALF + HUB_ROWS
ROWS = (NZ + 1) * HALF
PARTS = NC * NY
WROWS = 256
DISTINCT = 4
BF = jnp.bfloat16
F32 = jnp.float32
VM = pl.BlockSpec(memory_space=pltpu.VMEM)
PLAIN = (((1,), (0,)), ((), ()))
LAST = (((1,), (1,)), ((), ()))
FIRST = (((0,), (0,)), ((), ()))


def dot(a, b, dims=PLAIN, **kw):
    return lax.dot_general(a, b, dims, preferred_element_type=F32, **kw)


def shift(x, axis, size, step):
    return lax.ppermute(x, axis, [(i, (i + step) % size) for i in range(size)])


def swap(x, axis, size, mask):
    return lax.ppermute(x, axis, [(i, i ^ mask) for i in range(size)])


MASKS = (0, 2, 1, 3)


def three(x, axis, size, each=False):
    own = x[0] if each else x
    return [own] + [swap(x[mask] if each else x, axis, size, mask) for mask in MASKS[1:]]


def call(kernel, outs, inputs, name, scratch=(), flops=0, mib=16, far=0):
    return pl.pallas_call(
        kernel,
        out_shape=outs,
        in_specs=[VM] * (len(inputs) - far) + [pl.BlockSpec(memory_space=pl.ANY)] * far,
        out_specs=jax.tree.map(lambda _: VM, outs),
        scratch_shapes=list(scratch),
        compiler_params=pltpu.CompilerParams(vmem_limit_bytes=mib << 20),
        cost_estimate=pl.CostEstimate(flops=flops, bytes_accessed=1 << 18, transcendentals=0),
        name=name,
    )(*inputs)


def shaped(shape, dtype):
    return jax.ShapeDtypeStruct(shape, dtype)


def prepare_kernel(
    feat, cot, hub, owner, row, hub_id, ids_ref, mine_ref, both,
    owner_scr, row_scr, hub_id_scr, hub_scr, sems,
):
    parity, half = lax.axis_index("x") // 2, lax.axis_index("x") % 2
    pairs = (
        (owner, owner_scr),
        (row, row_scr),
        (hub_id, hub_id_scr),
        (hub, hub_scr),
        (feat, mine_ref.at[pl.ds(0, HALF)]),
        (feat, both.at[pl.ds(0, HALF)]),
        (cot, both.at[pl.ds(HALF, HALF)]),
    )
    copies = [pltpu.make_async_copy(a, b, sems.at[i]) for i, (a, b) in enumerate(pairs)]
    for copy in copies:
        copy.start()
    for copy in copies:
        copy.wait()
    ids_ref[0:8] = owner_scr[...].reshape(8, V) * V + row_scr[...]
    ids_ref[8:12] = hub_id_scr[...]
    ids_ref[12:16] = jnp.full((4, V), -1, jnp.int32)
    pick = lax.broadcasted_iota(jnp.int32, (HUB_ROWS, 2 * HUB_ROWS), 1) == (
        2 * lax.broadcasted_iota(jnp.int32, (HUB_ROWS, 2 * HUB_ROWS), 0) + parity
    )
    columns = hub_scr[:, pl.ds(pl.multiple_of(half * COLS, COLS), COLS)]
    mine_ref[HALF:BLOCK] = dot(pick.astype(F32).astype(BF), columns).astype(BF)


def counts_kernel(ids0, ids1, ids2, ids3, out_ref, ids_scr, key_scr):
    y, z, c, x = (lax.axis_index(a) for a in ("y", "z", "c", "x"))
    parity = x // 2
    rows = lax.broadcasted_iota(jnp.int32, (16, 16, 128), 0) * 16 + lax.broadcasted_iota(
        jnp.int32, (16, 16, 128), 1
    )
    rows = rows.astype(F32).astype(BF)
    level = lax.broadcasted_iota(jnp.int32, (8, V), 0)
    column = y * (NZ * NC) + c
    mask = (NY - 1) * (NZ * NC) + (NC - 1)

    def allmax(a):
        for s in (4, 2, 1):
            a = jnp.maximum(a, pltpu.roll(a, s, 0))
        return a

    def allsum(a):
        for s in (4, 2, 1):
            a = a + pltpu.roll(a, s, 0)
        return a

    def extract(keys):
        top = allmax(keys)
        hit = keys == top
        return jnp.where(hit, -1.0, keys), top, allsum(jnp.where(hit, 1.0, 0.0))

    def pair(a):
        return jnp.concatenate([a, a], 0).astype(BF)

    for dy, ids_ref in zip(MASKS, (ids0, ids1, ids2, ids3)):
        for dc in range(NC):
            ids_scr[dc * NY + dy] = ids_ref[dc]

    def part(index, carry):
        ids = ids_scr[index]
        flat, hub = ids[0:8], ids[8:16]
        here = ((flat >> 9) & mask) == column
        here = here & ((flat & 1) == parity)
        keys = jnp.where(here, (((flat >> 10) - z) & 7) * HALF + ((flat >> 1) & 255), -1).astype(F32)
        here = (((hub >> 5) & mask) == column) & (level < 4)
        hub_row = (((hub >> 6) - z) & 7) * 32 + ((hub & 1) ^ parity) * 16 + ((hub >> 1) & 15)
        hub_keys = jnp.where(here, hub_row, -1).astype(F32)
        found, hub_found = [], []
        for _ in range(DISTINCT):
            keys, top, times = extract(keys)
            found.append((top, pair(times)))
        for _ in range(4):
            hub_keys, top, times = extract(hub_keys)
            hub_found.append((pair(top), pair(times)))
        for tile in range(V // 128):
            lanes = slice(tile * 128, (tile + 1) * 128)
            for delta in range(NZ):
                block = jnp.zeros((16, 16, 128), BF)
                for top, times in found:
                    match = pair(top[:, lanes] - float(HALF * delta))[None] == rows
                    block = jnp.where(match, times[:, lanes][None], block)
                out_ref[index, delta * HALF : (delta + 1) * HALF, lanes] = block.reshape(HALF, 128)
            block = jnp.zeros((16, 16, 128), BF)
            for top, times in hub_found:
                block = jnp.where(top[:, lanes][None] == rows, times[:, lanes][None], block)
            out_ref[index, NZ * HALF : ROWS, lanes] = block.reshape(HALF, 128)

        def more(keys):
            keys, top, times = extract(keys)
            key_scr[0] = top
            key_scr[1] = times

            def fix(step, inner):
                delta = step % NZ
                lanes = pl.ds(pl.multiple_of(step // NZ * 128, 128), 128)
                span = pl.ds(pl.multiple_of(delta * HALF, HALF), HALF)
                wanted = key_scr[0, :, lanes] - (delta * HALF).astype(F32)
                block = out_ref[index, span, lanes].reshape(16, 16, 128)
                block = jnp.where(pair(wanted)[None] == rows, pair(key_scr[1, :, lanes])[None], block)
                out_ref[index, span, lanes] = block.reshape(HALF, 128)
                return inner

            lax.fori_loop(0, NZ * (V // 128), fix, 0)
            return keys

        lax.while_loop(lambda keys: jnp.max(keys) >= 0, more, keys)
        return carry

    lax.fori_loop(0, PARTS, part, 0)


def far_sums_kernel(counts, t0, t1, t2, t7, t34, t65, sums_ref, turned_ref, table):
    blocks = {0: t0[...], 1: t1[...], 2: t2[...], 7: t7[...]}
    blocks[3], blocks[4] = t34[0:BLOCK], t34[BLOCK : 2 * BLOCK]
    blocks[6], blocks[5] = t65[0:BLOCK], t65[BLOCK : 2 * BLOCK]
    for delta in range(NZ):
        table[delta * HALF : (delta + 1) * HALF] = blocks[delta][0:HALF]
        start = NZ * HALF + delta * 2 * HUB_ROWS
        table[start : start + HUB_ROWS] = blocks[delta][HALF:BLOCK]
        table[start + HUB_ROWS : start + 2 * HUB_ROWS] = jnp.zeros((HUB_ROWS, COLS), BF)
    turned_ref[...] = table[...].T

    for dy in range(NY):
        sums_ref[dy] = dot(turned_ref[...], counts[NY + dy]).astype(BF)


def near_sums_kernel(counts, turned, sums_ref):
    for dy in range(NY):
        sums_ref[dy] = dot(turned[...], counts[dy])


def arrange_kernel(fg0, fg1, fg23, ws_ref, turned_ref, cot_ref, pre_ref, order_ref, back_ref, scr):
    x = lax.axis_index("x")
    for mask, (ref, start) in enumerate(((fg0, 0), (fg1, 0), (fg23, 0), (fg23, V))):
        scr[x ^ mask] = ref[start : start + V]
    rows = []
    for start in (0, HALF):
        quarters = [scr[q, start : start + HALF] for q in range(NX)]
        rows.append(
            jnp.concatenate(
                [jnp.concatenate(quarters[0:2], 1), jnp.concatenate(quarters[2:4], 1)], 0
            )
        )
    turned_ref[...] = rows[0].T
    cot_ref[...] = rows[1]
    pre_ref[...] = dot(rows[0], ws_ref[...])
    first = lax.broadcasted_iota(jnp.int32, (V, V), 0)
    second = lax.broadcasted_iota(jnp.int32, (V, V), 1)
    order_ref[...] = ((first % HALF) * 2 + first // HALF == second).astype(F32).astype(BF)
    back_ref[...] = ((second % HALF) * 2 + second // HALF == first).astype(F32).astype(BF)


def dense_kernel(
    turned_ref, cot_ref, pre_ref, order_ref, back_ref, s0, s1, s2, s3, ws_ref, wn_ref,
    out_ref, message_ref, self_ref,
    s_scr, o_scr, w_scr,
):
    x = lax.axis_index("x")
    parity, half = x // 2, x % 2
    for mask, ref in zip(MASKS, (s0, s1, s2, s3)):
        s_scr[x ^ mask] = ref[...]
    mean_t = jnp.concatenate(
        [
            s_scr[0].astype(F32) + s_scr[2].astype(F32),
            s_scr[1].astype(F32) + s_scr[3].astype(F32),
        ],
        0,
    )
    mean_t = (mean_t / 12.0).astype(BF)
    mean = dot(order_ref[...], mean_t, LAST).astype(BF)
    pre = pre_ref[...] + dot(mean, wn_ref[...])
    sig = jax.nn.sigmoid(pre)
    value = (pre * sig).astype(BF)
    grad_pre = (cot_ref[...].astype(F32) * sig * (1.0 + pre * (1.0 - sig))).astype(BF)
    for q in range(2):
        for h in range(2):
            o_scr[q * 2 + h] = value[q * HALF : (q + 1) * HALF, h * COLS : (h + 1) * COLS]
    out_ref[...] = o_scr[x]
    rows = pl.ds(pl.multiple_of(half * COLS, COLS), COLS)
    natural = dot(back_ref[...], grad_pre).astype(BF)
    message_ref[0:V] = (dot(natural, wn_ref[rows, :], LAST) / 12.0).astype(BF)
    own_self = dot(grad_pre, ws_ref[rows, :], LAST)
    self_ref[...] = jnp.where(parity == 0, own_self[0:HALF], own_self[HALF:V])
    w_scr[0] = dot(turned_ref[...], grad_pre)
    w_scr[1] = dot(mean_t, natural)
    quarter = pl.ds(pl.multiple_of(x * 64, 64), 64)
    for which in range(2):
        part = w_scr[which, quarter, :]
        for h in range(2):
            start = V + which * 128 + h * 64
            message_ref[start : start + 64, :] = part[:, h * COLS : (h + 1) * COLS].astype(BF)


def block_sum(counts, base, messages, block, total=None):
    span = slice(block * HALF, (block + 1) * HALF)
    for index, ref in enumerate(messages):
        dy = base + index // NY * NY + MASKS[index % NY]
        term = dot(counts[dy, span], ref[0:V])
        total = term if total is None else total + term
    return total


FIRST_BLOCKS = (4, 5, NZ)


def near_grads_kernel(counts, m0, m1, m2, m3, out_ref):
    for index, block in enumerate(FIRST_BLOCKS):
        out_ref[index] = block_sum(counts, 0, (m0, m1, m2, m3), block)


def first_grads_kernel(
    counts, m0, m1, m2, m3, o0, o1, o2, o3, near, up_ref, down_ref, hub_ref, skip_ref
):
    parity = lax.axis_index("x") // 2
    others = (o0, o1, o2, o3)
    blocks = [block_sum(counts, NY, others, block, near[index]) for index, block in enumerate(FIRST_BLOCKS)]
    hubs = blocks[2]
    lane = lax.broadcasted_iota(jnp.int32, (HUB_ROWS, COLS), 1)
    low = (lane < 64) == (parity == 0)
    for delta in range(NZ):
        start = delta * 2 * HUB_ROWS
        mine = hubs[start : start + HUB_ROWS]
        rest = pltpu.roll(hubs[start + HUB_ROWS : start + 2 * HUB_ROWS], 64, 1)
        hub_ref[delta] = jnp.where(low, mine, rest)
    tail = slice(V, V + WROWS)
    sums = [
        (a[tail].astype(F32) + b[tail].astype(F32)) + (c[tail].astype(F32) + d[tail].astype(F32))
        for a, b, c, d in ((m0, m1, m2, m3), others)
    ]
    weight = (sums[0] + sums[1]).astype(BF)
    skip_ref[...] = hub_ref[4]
    for index, (hub_delta, ref) in enumerate(((3, up_ref), (5, down_ref))):
        ref[0:HALF] = blocks[index].astype(BF)
        ref[HALF:BLOCK] = hub_ref[hub_delta].astype(BF)
        ref[BLOCK:] = weight


def rest_grads_kernel(counts, m0, m1, m2, m3, o0, o1, o2, o3, out_ref, *, blocks):
    for index, block in enumerate(blocks):
        out_ref[index] = block_sum(counts, 0, (m0, m1, m2, m3, o0, o1, o2, o3), block)


def hop_kernel(got, rest, hubs, skip, turn, next_ref, token_ref, *, index, hub_delta):
    next_ref[0:HALF] = (got[0:HALF].astype(F32) + rest[index]).astype(BF)
    hub = got[HALF:BLOCK].astype(F32) + hubs[hub_delta]
    if hub_delta == 2:
        hub = hub + skip[...]
    next_ref[HALF:BLOCK] = hub.astype(BF)
    next_ref[BLOCK:] = got[BLOCK:]
    token_ref[...] = jnp.zeros_like(token_ref)


def last_hop_kernel(up, rest, turn, next_up, token_ref):
    next_up[0:HALF] = (up[0:HALF].astype(F32) + rest[0]).astype(BF)
    next_up[HALF:] = up[BLOCK:]
    token_ref[...] = jnp.zeros_like(token_ref)


def hub_kernel(up, down, hubs, turn, hub_sum):
    hub_sum[...] = up[HALF:BLOCK].astype(F32) + down[HALF:BLOCK].astype(F32) + hubs[0]


def final_kernel(
    self_ref, rest, first, up1, up2, up3, up4, down1, down2, down3, hub_sum,
    feat_ref, hub_ref, gself_ref, gnbr_ref, w_scr,
):
    z = lax.axis_index("z")
    total = rest[1] + up4[0:HALF].astype(F32) + down3[0:HALF].astype(F32)
    feat_ref[...] = (self_ref[...] + total).astype(BF)
    hubs = hub_sum[...]
    shape = (2 * HUB_ROWS, HUB_ROWS)
    target = lax.broadcasted_iota(jnp.int32, shape, 0)
    source = lax.broadcasted_iota(jnp.int32, shape, 1)
    spread = [
        dot((target == 2 * source + q).astype(F32), hubs[:, q * 64 : (q + 1) * 64], precision=lax.Precision.HIGHEST)
        for q in range(2)
    ]
    hub_ref[...] = spread[0] + spread[1]
    arrived = {0: first, 7: up1, 6: up2, 5: up3, 1: down1, 2: down2, 3: down3}
    for step in range(NZ):
        if step == 4:
            w_scr[(z + step) % NZ] = up4[HALF:]
        else:
            w_scr[(z + step) % NZ] = arrived[step][BLOCK:]
    weight = w_scr[0].astype(F32)
    for step in range(1, NZ):
        weight = weight + w_scr[step].astype(F32)
    gself_ref[...] = jnp.concatenate([weight[0:64], weight[64:128]], 1)
    gnbr_ref[...] = jnp.concatenate([weight[128:192], weight[192:256]], 1)


def body(features, hub_feats, nbr_owner, nbr_row, hub_ids, w_self, w_nbr, grad_out):
    ids, mine, fg = call(
        prepare_kernel,
        (pltpu.VMEM((16, V), jnp.int32), pltpu.VMEM((BLOCK, COLS), BF), pltpu.VMEM((V, COLS), BF)),
        (features, grad_out, hub_feats, nbr_owner.reshape(8, 1, V), nbr_row, hub_ids.T),
        "prepare",
        scratch=[
            pltpu.VMEM((8, 1, V), jnp.int32),
            pltpu.VMEM((8, V), jnp.int32),
            pltpu.VMEM((4, V), jnp.int32),
            pltpu.VMEM((2 * HUB_ROWS, 256), BF),
            pltpu.SemaphoreType.DMA((7,)),
        ],
        far=6,
        mib=56,
    )

    fg1 = swap(fg, "x", NX, 1)
    fg23 = swap(jnp.concatenate([fg, fg1], 0), "x", NX, 2)

    pair = jnp.stack([ids, swap(ids, "c", NC, 1)])
    t1, t7, t2 = shift(mine, "z", NZ, -1), shift(mine, "z", NZ, 1), shift(mine, "z", NZ, -2)
    pairs = three(pair, "y", NY)
    t34 = shift(jnp.concatenate([t1, t2], 0), "z", NZ, -2)
    t65 = shift(jnp.concatenate([mine, t7], 0), "z", NZ, 2)
    counts = call(
        counts_kernel,
        pltpu.VMEM((PARTS, ROWS, V), BF),
        (*pairs,),
        "counts",
        flops=1 << 34,
        scratch=[pltpu.VMEM((PARTS, 16, V), jnp.int32), pltpu.VMEM((2, 8, V), F32)],
        mib=8,
    )

    far, turned = call(
        far_sums_kernel,
        (shaped((NY, COLS, V), BF), shaped((COLS, ROWS), BF)),
        (counts, mine, t1, t2, t7, t34, t65),
        "far_sums",
        scratch=[pltpu.VMEM((ROWS, COLS), BF)],
        flops=1 << 31,
    )
    got = swap(far, "c", NC, 1)
    near = call(
        near_sums_kernel, shaped((NY, COLS, V), F32), (counts, turned), "near_sums", flops=1 << 31
    )
    both = near + got.astype(F32)
    parts = three(both.astype(BF), "y", NY, each=True)
    total = both[0] + parts[1].astype(F32) + parts[2].astype(F32) + parts[3].astype(F32)
    sums = three(total.astype(BF), "x", NX)

    arranged = call(
        arrange_kernel,
        (
            shaped((256, V), BF),
            shaped((V, 256), BF),
            shaped((V, 256), F32),
            shaped((V, V), BF),
            shaped((V, V), BF),
        ),
        (fg, fg1, fg23, w_self),
        "arrange",
        scratch=[pltpu.VMEM((NX, V, COLS), BF)],
        flops=1 << 28,
    )
    outputs, message, self_term = call(
        dense_kernel,
        (shaped((HALF, COLS), BF), shaped((V + WROWS, COLS), BF), shaped((HALF, COLS), F32)),
        (*arranged, *sums, w_self, w_nbr),
        "dense",
        scratch=[
            pltpu.VMEM((4, COLS, V), BF),
            pltpu.VMEM((4, HALF, COLS), BF),
            pltpu.VMEM((2, 256, 256), F32),
        ],
        flops=1 << 30,
    )

    messages = three(message, "y", NY)
    others = [swap(m, "c", NC, 1) for m in messages]
    near_grads = call(
        near_grads_kernel,
        shaped((len(FIRST_BLOCKS), HALF, COLS), F32),
        (counts, *messages),
        "near_grads",
        flops=1 << 30,
    )
    hop_shapes = (shaped((BLOCK + WROWS, COLS), BF),) * 2
    up0, down0, hubs, skip = call(
        first_grads_kernel,
        (*hop_shapes, shaped((NZ, HUB_ROWS, COLS), F32), shaped((HUB_ROWS, COLS), F32)),
        (counts, *messages, *others, near_grads),
        "first_grads",
        flops=1 << 30,
    )
    up1, down1 = shift(up0, "z", NZ, 1), shift(down0, "z", NZ, -1)
    rests = [
        call(
            functools.partial(rest_grads_kernel, blocks=blocks),
            shaped((2, HALF, COLS), F32),
            (counts, *messages, *others),
            "rest_grads",
            flops=1 << 29,
        )
        for blocks in ((3, 6), (2, 7), (1, 0))
    ]
    skip = shift(skip, "z", NZ, 2)
    ups, downs = [up1], [down1]
    hop_shape, token_shape = shaped((BLOCK + WROWS, COLS), BF), shaped((8, 128), F32)
    token = hubs
    for hub_deltas, rest in zip(((2, 6), (1, 7)), rests):
        for index, (hub_delta, side, step) in enumerate(zip(hub_deltas, (ups, downs), (1, -1))):
            message, token = call(
                functools.partial(hop_kernel, index=index, hub_delta=hub_delta),
                (hop_shape, token_shape),
                (side[-1], rest, hubs, skip, token),
                "hop",
            )
            side.append(shift(message, "z", NZ, step))
    up, token = call(
        last_hop_kernel,
        (shaped((HALF + WROWS, COLS), BF), token_shape),
        (ups[-1], rests[2], token),
        "last_hop",
    )
    hub_sum = call(
        hub_kernel, shaped((HUB_ROWS, COLS), F32), (ups[-1], downs[-1], hubs, token), "hub_sum"
    )
    ups.append(shift(up, "z", NZ, 1))
    hub_sum = lax.ppermute(hub_sum, "x", [(0, 0), (1, 2), (2, 1), (3, 3)])
    grad_features, hub_rows, grad_self, grad_nbr = call(
        final_kernel,
        (
            shaped((HALF, COLS), BF),
            shaped((2 * HUB_ROWS, 64), F32),
            shaped((64, 256), F32),
            shaped((64, 256), F32),
        ),
        (self_term, rests[2], up0, *ups, *downs, hub_sum),
        "last_sums",
        scratch=[pltpu.VMEM((NZ, WROWS, COLS), BF)],
    )
    return outputs, grad_features, hub_rows, grad_self, grad_nbr


def solution(mesh):
    fine = Mesh(mesh.devices.reshape(NY, NZ, NC, NX), ("y", "z", "c", "x"))
    dom = ("y", "z", "c")
    in_specs = (
        P(dom, "x"),
        P(dom, None),
        P(None, dom, None),
        P(None, dom),
        P(dom, None),
        P(),
        P(),
        P(dom, "x"),
    )
    out_specs = (P(dom, "x"), P(dom, "x"), P(dom, "x"), P("x", None), P("x", None))
    return jax.shard_map(body, mesh=fine, in_specs=in_specs, out_specs=out_specs, check_vma=False)
```

```python
import functools

import jax
import jax.numpy as jnp
from jax import lax
from jax.experimental import pallas as pl
from jax.experimental.pallas import tpu as pltpu
from jax.sharding import Mesh, PartitionSpec as P

NY, NZ, NC, NX = 4, 8, 2, 4
V = 512
HALF = 256
COLS = 128
HUB_ROWS = 16
BLOCK = HALF + HUB_ROWS
ROWS = (NZ + 1) * HALF
PARTS = NC * NY
WROWS = 256
DISTINCT = 4
BF = jnp.bfloat16
F32 = jnp.float32
VM = pl.BlockSpec(memory_space=pltpu.VMEM)
PLAIN = (((1,), (0,)), ((), ()))
LAST = (((1,), (1,)), ((), ()))
FIRST = (((0,), (0,)), ((), ()))


def dot(a, b, dims=PLAIN, **kw):
    return lax.dot_general(a, b, dims, preferred_element_type=F32, **kw)


def shift(x, axis, size, step):
    return lax.ppermute(x, axis, [(i, (i + step) % size) for i in range(size)])


def swap(x, axis, size, mask):
    return lax.ppermute(x, axis, [(i, i ^ mask) for i in range(size)])


MASKS = (0, 2, 1, 3)


def three(x, axis, size, each=False):
    own = x[0] if each else x
    return [own] + [swap(x[mask] if each else x, axis, size, mask) for mask in MASKS[1:]]


def call(kernel, outs, inputs, name, scratch=(), flops=0, mib=16, far=0):
    return pl.pallas_call(
        kernel,
        out_shape=outs,
        in_specs=[VM] * (len(inputs) - far) + [pl.BlockSpec(memory_space=pl.ANY)] * far,
        out_specs=jax.tree.map(lambda _: VM, outs),
        scratch_shapes=list(scratch),
        compiler_params=pltpu.CompilerParams(vmem_limit_bytes=mib << 20),
        cost_estimate=pl.CostEstimate(flops=flops, bytes_accessed=1 << 18, transcendentals=0),
        name=name,
    )(*inputs)


def shaped(shape, dtype):
    return jax.ShapeDtypeStruct(shape, dtype)


def prepare_kernel(
    feat, cot, hub, owner, row, hub_id, ids_ref, mine_ref, both,
    owner_scr, row_scr, hub_id_scr, hub_scr, sems,
):
    parity, half = lax.axis_index("x") // 2, lax.axis_index("x") % 2
    pairs = (
        (owner, owner_scr),
        (row, row_scr),
        (hub_id, hub_id_scr),
        (hub, hub_scr),
        (feat, mine_ref.at[pl.ds(0, HALF)]),
        (feat, both.at[pl.ds(0, HALF)]),
        (cot, both.at[pl.ds(HALF, HALF)]),
    )
    copies = [pltpu.make_async_copy(a, b, sems.at[i]) for i, (a, b) in enumerate(pairs)]
    for copy in copies:
        copy.start()
    for copy in copies:
        copy.wait()
    ids_ref[0:8] = owner_scr[...].reshape(8, V) * V + row_scr[...]
    ids_ref[8:12] = hub_id_scr[...]
    ids_ref[12:16] = jnp.full((4, V), -1, jnp.int32)
    pick = lax.broadcasted_iota(jnp.int32, (HUB_ROWS, 2 * HUB_ROWS), 1) == (
        2 * lax.broadcasted_iota(jnp.int32, (HUB_ROWS, 2 * HUB_ROWS), 0) + parity
    )
    columns = hub_scr[:, pl.ds(pl.multiple_of(half * COLS, COLS), COLS)]
    mine_ref[HALF:BLOCK] = dot(pick.astype(F32).astype(BF), columns).astype(BF)


def counts_kernel(ids0, ids1, ids2, ids3, out_ref, ids_scr):
    y, z, c, x = (lax.axis_index(a) for a in ("y", "z", "c", "x"))
    parity = x // 2
    rows = lax.broadcasted_iota(jnp.int32, (16, 16, 128), 0) * 16 + lax.broadcasted_iota(
        jnp.int32, (16, 16, 128), 1
    )
    rows = rows.astype(F32).astype(BF)
    level = lax.broadcasted_iota(jnp.int32, (8, V), 0)
    column = y * (NZ * NC) + c
    mask = (NY - 1) * (NZ * NC) + (NC - 1)

    def allmax(a):
        for s in (4, 2, 1):
            a = jnp.maximum(a, pltpu.roll(a, s, 0))
        return a

    def allsum(a):
        for s in (4, 2, 1):
            a = a + pltpu.roll(a, s, 0)
        return a

    def extract(keys):
        top = allmax(keys)
        hit = keys == top
        return jnp.where(hit, -1.0, keys), top, allsum(jnp.where(hit, 1.0, 0.0))

    def pair(a):
        return jnp.concatenate([a, a], 0).astype(BF)

    for dy, ids_ref in zip(MASKS, (ids0, ids1, ids2, ids3)):
        for dc in range(NC):
            ids_scr[dc * NY + dy] = ids_ref[dc]

    def part(index, carry):
        ids = ids_scr[index]
        flat, hub = ids[0:8], ids[8:16]
        here = ((flat >> 9) & mask) == column
        here = here & ((flat & 1) == parity)
        keys = jnp.where(here, (((flat >> 10) - z) & 7) * HALF + ((flat >> 1) & 255), -1).astype(F32)
        here = (((hub >> 5) & mask) == column) & (level < 4)
        hub_row = (((hub >> 6) - z) & 7) * 32 + ((hub & 1) ^ parity) * 16 + ((hub >> 1) & 15)
        hub_keys = jnp.where(here, hub_row, -1).astype(F32)
        found, hub_found = [], []
        for _ in range(DISTINCT):
            keys, top, times = extract(keys)
            found.append((top, pair(times)))
        for _ in range(4):
            hub_keys, top, times = extract(hub_keys)
            hub_found.append((pair(top), pair(times)))
        for tile in range(V // 128):
            lanes = slice(tile * 128, (tile + 1) * 128)
            for delta in range(NZ):
                block = jnp.zeros((16, 16, 128), BF)
                for top, times in found:
                    match = pair(top[:, lanes] - float(HALF * delta))[None] == rows
                    block = jnp.where(match, times[:, lanes][None], block)
                out_ref[index, delta * HALF : (delta + 1) * HALF, lanes] = block.reshape(HALF, 128)
            block = jnp.zeros((16, 16, 128), BF)
            for top, times in hub_found:
                block = jnp.where(top[:, lanes][None] == rows, times[:, lanes][None], block)
            out_ref[index, NZ * HALF : ROWS, lanes] = block.reshape(HALF, 128)

        def more(keys):
            keys, top, times = extract(keys)
            for tile in range(V // 128):
                lanes = slice(tile * 128, (tile + 1) * 128)
                for delta in range(NZ):
                    span = slice(delta * HALF, (delta + 1) * HALF)
                    block = out_ref[index, span, lanes].reshape(16, 16, 128)
                    match = pair(top[:, lanes] - float(HALF * delta))[None] == rows
                    block = jnp.where(match, pair(times[:, lanes])[None], block)
                    out_ref[index, span, lanes] = block.reshape(HALF, 128)
            return keys

        lax.while_loop(lambda keys: jnp.max(keys) >= 0, more, keys)
        return carry

    lax.fori_loop(0, PARTS, part, 0)


def far_sums_kernel(counts, t0, t1, t2, t7, t34, t65, sums_ref, turned_ref, table):
    blocks = {0: t0[...], 1: t1[...], 2: t2[...], 7: t7[...]}
    blocks[3], blocks[4] = t34[0:BLOCK], t34[BLOCK : 2 * BLOCK]
    blocks[6], blocks[5] = t65[0:BLOCK], t65[BLOCK : 2 * BLOCK]
    for delta in range(NZ):
        table[delta * HALF : (delta + 1) * HALF] = blocks[delta][0:HALF]
        start = NZ * HALF + delta * 2 * HUB_ROWS
        table[start : start + HUB_ROWS] = blocks[delta][HALF:BLOCK]
        table[start + HUB_ROWS : start + 2 * HUB_ROWS] = jnp.zeros((HUB_ROWS, COLS), BF)
    turned_ref[...] = table[...].T

    for dy in range(NY):
        sums_ref[dy] = dot(turned_ref[...], counts[NY + dy]).astype(BF)


def near_sums_kernel(counts, turned, sums_ref):
    for dy in range(NY):
        sums_ref[dy] = dot(turned[...], counts[dy])


def arrange_kernel(fg0, fg1, fg23, ws_ref, turned_ref, cot_ref, pre_ref, order_ref, back_ref, scr):
    x = lax.axis_index("x")
    for mask, (ref, start) in enumerate(((fg0, 0), (fg1, 0), (fg23, 0), (fg23, V))):
        scr[x ^ mask] = ref[start : start + V]
    rows = []
    for start in (0, HALF):
        quarters = [scr[q, start : start + HALF] for q in range(NX)]
        rows.append(
            jnp.concatenate(
                [jnp.concatenate(quarters[0:2], 1), jnp.concatenate(quarters[2:4], 1)], 0
            )
        )
    turned_ref[...] = rows[0].T
    cot_ref[...] = rows[1]
    pre_ref[...] = dot(rows[0], ws_ref[...])
    first = lax.broadcasted_iota(jnp.int32, (V, V), 0)
    second = lax.broadcasted_iota(jnp.int32, (V, V), 1)
    order_ref[...] = ((first % HALF) * 2 + first // HALF == second).astype(F32).astype(BF)
    back_ref[...] = ((second % HALF) * 2 + second // HALF == first).astype(F32).astype(BF)


def dense_kernel(
    turned_ref, cot_ref, pre_ref, order_ref, back_ref, s0, s1, s2, s3, ws_ref, wn_ref,
    out_ref, message_ref, self_ref,
    s_scr, o_scr, w_scr,
):
    x = lax.axis_index("x")
    parity, half = x // 2, x % 2
    for mask, ref in zip(MASKS, (s0, s1, s2, s3)):
        s_scr[x ^ mask] = ref[...]
    mean_t = jnp.concatenate(
        [
            s_scr[0].astype(F32) + s_scr[2].astype(F32),
            s_scr[1].astype(F32) + s_scr[3].astype(F32),
        ],
        0,
    )
    mean_t = (mean_t / 12.0).astype(BF)
    mean = dot(order_ref[...], mean_t, LAST).astype(BF)
    pre = pre_ref[...] + dot(mean, wn_ref[...])
    sig = jax.nn.sigmoid(pre)
    value = (pre * sig).astype(BF)
    grad_pre = (cot_ref[...].astype(F32) * sig * (1.0 + pre * (1.0 - sig))).astype(BF)
    for q in range(2):
        for h in range(2):
            o_scr[q * 2 + h] = value[q * HALF : (q + 1) * HALF, h * COLS : (h + 1) * COLS]
    out_ref[...] = o_scr[x]
    rows = pl.ds(pl.multiple_of(half * COLS, COLS), COLS)
    natural = dot(back_ref[...], grad_pre).astype(BF)
    message_ref[0:V] = (dot(natural, wn_ref[rows, :], LAST) / 12.0).astype(BF)
    own_self = dot(grad_pre, ws_ref[rows, :], LAST)
    self_ref[...] = jnp.where(parity == 0, own_self[0:HALF], own_self[HALF:V])
    w_scr[0] = dot(turned_ref[...], grad_pre)
    w_scr[1] = dot(mean_t, natural)
    quarter = pl.ds(pl.multiple_of(x * 64, 64), 64)
    for which in range(2):
        part = w_scr[which, quarter, :]
        for h in range(2):
            start = V + which * 128 + h * 64
            message_ref[start : start + 64, :] = part[:, h * COLS : (h + 1) * COLS].astype(BF)


def block_sum(counts, base, messages, block, total=None):
    span = slice(block * HALF, (block + 1) * HALF)
    for index, ref in enumerate(messages):
        dy = base + index // NY * NY + MASKS[index % NY]
        term = dot(counts[dy, span], ref[0:V])
        total = term if total is None else total + term
    return total


FIRST_BLOCKS = (4, 5, NZ)


def near_grads_kernel(counts, m0, m1, m2, m3, out_ref):
    for index, block in enumerate(FIRST_BLOCKS):
        out_ref[index] = block_sum(counts, 0, (m0, m1, m2, m3), block)


def first_grads_kernel(
    counts, m0, m1, m2, m3, o0, o1, o2, o3, near, up_ref, down_ref, hub_ref, skip_ref
):
    parity = lax.axis_index("x") // 2
    others = (o0, o1, o2, o3)
    blocks = [block_sum(counts, NY, others, block, near[index]) for index, block in enumerate(FIRST_BLOCKS)]
    hubs = blocks[2]
    lane = lax.broadcasted_iota(jnp.int32, (HUB_ROWS, COLS), 1)
    low = (lane < 64) == (parity == 0)
    for delta in range(NZ):
        start = delta * 2 * HUB_ROWS
        mine = hubs[start : start + HUB_ROWS]
        rest = pltpu.roll(hubs[start + HUB_ROWS : start + 2 * HUB_ROWS], 64, 1)
        hub_ref[delta] = jnp.where(low, mine, rest)
    tail = slice(V, V + WROWS)
    sums = [
        (a[tail].astype(F32) + b[tail].astype(F32)) + (c[tail].astype(F32) + d[tail].astype(F32))
        for a, b, c, d in ((m0, m1, m2, m3), others)
    ]
    weight = (sums[0] + sums[1]).astype(BF)
    skip_ref[...] = hub_ref[4]
    for index, (hub_delta, ref) in enumerate(((3, up_ref), (5, down_ref))):
        ref[0:HALF] = blocks[index].astype(BF)
        ref[HALF:BLOCK] = hub_ref[hub_delta].astype(BF)
        ref[BLOCK:] = weight


def rest_grads_kernel(counts, m0, m1, m2, m3, o0, o1, o2, o3, out_ref, *, blocks):
    for index, block in enumerate(blocks):
        out_ref[index] = block_sum(counts, 0, (m0, m1, m2, m3, o0, o1, o2, o3), block)


def hop_kernel(got, rest, hubs, skip, turn, next_ref, token_ref, *, index, hub_delta):
    next_ref[0:HALF] = (got[0:HALF].astype(F32) + rest[index]).astype(BF)
    hub = got[HALF:BLOCK].astype(F32) + hubs[hub_delta]
    if hub_delta == 2:
        hub = hub + skip[...]
    next_ref[HALF:BLOCK] = hub.astype(BF)
    next_ref[BLOCK:] = got[BLOCK:]
    token_ref[...] = jnp.zeros_like(token_ref)


def last_hop_kernel(up, rest, turn, next_up, token_ref):
    next_up[0:HALF] = (up[0:HALF].astype(F32) + rest[0]).astype(BF)
    next_up[HALF:] = up[BLOCK:]
    token_ref[...] = jnp.zeros_like(token_ref)


def hub_kernel(up, down, hubs, turn, hub_sum):
    hub_sum[...] = up[HALF:BLOCK].astype(F32) + down[HALF:BLOCK].astype(F32) + hubs[0]


def final_kernel(
    self_ref, rest, first, up1, up2, up3, up4, down1, down2, down3, hub_sum,
    feat_ref, hub_ref, gself_ref, gnbr_ref, w_scr,
):
    z = lax.axis_index("z")
    total = rest[1] + up4[0:HALF].astype(F32) + down3[0:HALF].astype(F32)
    feat_ref[...] = (self_ref[...] + total).astype(BF)
    hubs = hub_sum[...]
    shape = (2 * HUB_ROWS, HUB_ROWS)
    target = lax.broadcasted_iota(jnp.int32, shape, 0)
    source = lax.broadcasted_iota(jnp.int32, shape, 1)
    spread = [
        dot((target == 2 * source + q).astype(F32), hubs[:, q * 64 : (q + 1) * 64], precision=lax.Precision.HIGHEST)
        for q in range(2)
    ]
    hub_ref[...] = spread[0] + spread[1]
    arrived = {0: first, 7: up1, 6: up2, 5: up3, 1: down1, 2: down2, 3: down3}
    for step in range(NZ):
        if step == 4:
            w_scr[(z + step) % NZ] = up4[HALF:]
        else:
            w_scr[(z + step) % NZ] = arrived[step][BLOCK:]
    weight = w_scr[0].astype(F32)
    for step in range(1, NZ):
        weight = weight + w_scr[step].astype(F32)
    gself_ref[...] = jnp.concatenate([weight[0:64], weight[64:128]], 1)
    gnbr_ref[...] = jnp.concatenate([weight[128:192], weight[192:256]], 1)


def body(features, hub_feats, nbr_owner, nbr_row, hub_ids, w_self, w_nbr, grad_out):
    ids, mine, fg = call(
        prepare_kernel,
        (pltpu.VMEM((16, V), jnp.int32), pltpu.VMEM((BLOCK, COLS), BF), pltpu.VMEM((V, COLS), BF)),
        (features, grad_out, hub_feats, nbr_owner.reshape(8, 1, V), nbr_row, hub_ids.T),
        "prepare",
        scratch=[
            pltpu.VMEM((8, 1, V), jnp.int32),
            pltpu.VMEM((8, V), jnp.int32),
            pltpu.VMEM((4, V), jnp.int32),
            pltpu.VMEM((2 * HUB_ROWS, 256), BF),
            pltpu.SemaphoreType.DMA((7,)),
        ],
        far=6,
        mib=56,
    )

    fg1 = swap(fg, "x", NX, 1)
    fg23 = swap(jnp.concatenate([fg, fg1], 0), "x", NX, 2)

    pair = jnp.stack([ids, swap(ids, "c", NC, 1)])
    t1, t7, t2 = shift(mine, "z", NZ, -1), shift(mine, "z", NZ, 1), shift(mine, "z", NZ, -2)
    pairs = three(pair, "y", NY)
    t34 = shift(jnp.concatenate([t1, t2], 0), "z", NZ, -2)
    t65 = shift(jnp.concatenate([mine, t7], 0), "z", NZ, 2)
    counts = call(
        counts_kernel,
        pltpu.VMEM((PARTS, ROWS, V), BF),
        (*pairs,),
        "counts",
        flops=1 << 34,
        scratch=[pltpu.VMEM((PARTS, 16, V), jnp.int32)],
        mib=8,
    )

    far, turned = call(
        far_sums_kernel,
        (shaped((NY, COLS, V), BF), shaped((COLS, ROWS), BF)),
        (counts, mine, t1, t2, t7, t34, t65),
        "far_sums",
        scratch=[pltpu.VMEM((ROWS, COLS), BF)],
        flops=1 << 31,
    )
    got = swap(far, "c", NC, 1)
    near = call(
        near_sums_kernel, shaped((NY, COLS, V), F32), (counts, turned), "near_sums", flops=1 << 31
    )
    both = near + got.astype(F32)
    parts = three(both.astype(BF), "y", NY, each=True)
    total = both[0] + parts[1].astype(F32) + parts[2].astype(F32) + parts[3].astype(F32)
    sums = three(total.astype(BF), "x", NX)

    arranged = call(
        arrange_kernel,
        (
            shaped((256, V), BF),
            shaped((V, 256), BF),
            shaped((V, 256), F32),
            shaped((V, V), BF),
            shaped((V, V), BF),
        ),
        (fg, fg1, fg23, w_self),
        "arrange",
        scratch=[pltpu.VMEM((NX, V, COLS), BF)],
        flops=1 << 28,
    )
    outputs, message, self_term = call(
        dense_kernel,
        (shaped((HALF, COLS), BF), shaped((V + WROWS, COLS), BF), shaped((HALF, COLS), F32)),
        (*arranged, *sums, w_self, w_nbr),
        "dense",
        scratch=[
            pltpu.VMEM((4, COLS, V), BF),
            pltpu.VMEM((4, HALF, COLS), BF),
            pltpu.VMEM((2, 256, 256), F32),
        ],
        flops=1 << 30,
    )

    messages = three(message, "y", NY)
    others = [swap(m, "c", NC, 1) for m in messages]
    near_grads = call(
        near_grads_kernel,
        shaped((len(FIRST_BLOCKS), HALF, COLS), F32),
        (counts, *messages),
        "near_grads",
        flops=1 << 30,
    )
    hop_shapes = (shaped((BLOCK + WROWS, COLS), BF),) * 2
    up0, down0, hubs, skip = call(
        first_grads_kernel,
        (*hop_shapes, shaped((NZ, HUB_ROWS, COLS), F32), shaped((HUB_ROWS, COLS), F32)),
        (counts, *messages, *others, near_grads),
        "first_grads",
        flops=1 << 30,
    )
    up1, down1 = shift(up0, "z", NZ, 1), shift(down0, "z", NZ, -1)
    rests = [
        call(
            functools.partial(rest_grads_kernel, blocks=blocks),
            shaped((2, HALF, COLS), F32),
            (counts, *messages, *others),
            "rest_grads",
            flops=1 << 29,
        )
        for blocks in ((3, 6), (2, 7), (1, 0))
    ]
    skip = shift(skip, "z", NZ, 2)
    ups, downs = [up1], [down1]
    hop_shape, token_shape = shaped((BLOCK + WROWS, COLS), BF), shaped((8, 128), F32)
    token = hubs
    for hub_deltas, rest in zip(((2, 6), (1, 7)), rests):
        for index, (hub_delta, side, step) in enumerate(zip(hub_deltas, (ups, downs), (1, -1))):
            message, token = call(
                functools.partial(hop_kernel, index=index, hub_delta=hub_delta),
                (hop_shape, token_shape),
                (side[-1], rest, hubs, skip, token),
                "hop",
            )
            side.append(shift(message, "z", NZ, step))
    up, token = call(
        last_hop_kernel,
        (shaped((HALF + WROWS, COLS), BF), token_shape),
        (ups[-1], rests[2], token),
        "last_hop",
    )
    hub_sum = call(
        hub_kernel, shaped((HUB_ROWS, COLS), F32), (ups[-1], downs[-1], hubs, token), "hub_sum"
    )
    ups.append(shift(up, "z", NZ, 1))
    hub_sum = lax.ppermute(hub_sum, "x", [(0, 0), (1, 2), (2, 1), (3, 3)])
    grad_features, hub_rows, grad_self, grad_nbr = call(
        final_kernel,
        (
            shaped((HALF, COLS), BF),
            shaped((2 * HUB_ROWS, 64), F32),
            shaped((64, 256), F32),
            shaped((64, 256), F32),
        ),
        (self_term, rests[2], up0, *ups, *downs, hub_sum),
        "last_sums",
        scratch=[pltpu.VMEM((NZ, WROWS, COLS), BF)],
    )
    return outputs, grad_features, hub_rows, grad_self, grad_nbr


def solution(mesh):
    fine = Mesh(mesh.devices.reshape(NY, NZ, NC, NX), ("y", "z", "c", "x"))
    dom = ("y", "z", "c")
    in_specs = (
        P(dom, "x"),
        P(dom, None),
        P(None, dom, None),
        P(None, dom),
        P(dom, None),
        P(),
        P(),
        P(dom, "x"),
    )
    out_specs = (P(dom, "x"), P(dom, "x"), P(dom, "x"), P("x", None), P("x", None))
    return jax.shard_map(body, mesh=fine, in_specs=in_specs, out_specs=out_specs, check_vma=False)
```
